32 devices in a mesh: dp: 8 (over z, x), head: 4 (over y, core).
Axes of the slice: x: 2, y: 2, z: 4, core: 2. Of those that a mesh axis runs over, the one named last changes fastest.
Arguments:
- layer_in: float32 [24576, 1024], P('dp', 'head'), may hold values from -6 to 6
- bucket: int32 [8], P('dp'), may hold values from 0 to 1, as said below
- w_query: bfloat16 [1024, 1024], P(None, 'head'), may hold values from -0.1875 to 0.1875
- w_key: bfloat16 [1024, 1024], P(None, 'head'), may hold values from -0.1875 to 0.1875
- w_value: bfloat16 [1024, 1024], P(None, 'head'), may hold values from -0.1875 to 0.1875
- w_proj: bfloat16 [1024, 1024], P('head'), may hold values from -0.75 to 0.75
- attn_gain: float32 [1024], replicated, may hold values from 0.5 to 1.5
- attn_shift: float32 [1024], replicated, may hold values from -3 to 3
- ffn_gain: float32 [1024], replicated, may hold values from 0.5 to 1.5
- ffn_shift: float32 [1024], replicated, may hold values from -3 to 3
- w_expand: bfloat16 [1024, 4096], P(None, ('dp', 'head')), may hold values from -0.1875 to 0.1875
- bias_expand: bfloat16 [1, 4096], P(None, ('dp', 'head')), may hold values from -3 to 3
- w_reduce: bfloat16 [1024, 4096], P(None, ('dp', 'head')), may hold values from -0.09375 to 0.09375
- bias_reduce: float32 [1024], P('head'), may hold values from -3 to 3
- grad_out: float32 [24576, 1024], P('dp', 'head'), may hold values from -6 to 6
Outputs:
- layer_out: float32 [24576, 1024], P('dp', 'head')
- grad_in: float32 [24576, 1024], P('dp', 'head')
- grad_query: float32 [1024, 1024], P(None, 'head')
- grad_key: float32 [1024, 1024], P(None, 'head')
- grad_value: float32 [1024, 1024], P(None, 'head')
- grad_proj: float32 [1024, 1024], P('head')
- grad_attn_gain: float32 [1024], replicated
- grad_attn_shift: float32 [1024], replicated
- grad_ffn_gain: float32 [1024], replicated
- grad_ffn_shift: float32 [1024], replicated
- grad_expand: float32 [1024, 4096], P(None, ('dp', 'head'))
- grad_bias_expand: float32 [1, 4096], P(None, ('dp', 'head'))
- grad_reduce: float32 [1024, 4096], P(None, ('dp', 'head'))
- grad_bias_reduce: float32 [1024], P('head')
The draws below stay inside these ranges and needn't reach their ends.
Inputs may be any that keep to these rules, and one draw needn't show every extreme that they name: Group g's 3072 rows hold one sequence of 3072 tokens where bucket[g] is 1 and 6 sequences of 512 tokens where it is 0; both values occur in every draw.
All inputs are finite; a program needn't handle non-finite values.
Results may differ from the reference program's by a relative error of at most 0.017.
Values may be sent and summed in bfloat16 or wider, within the bound.
A program may use at most 256 MiB of HBM per device.

```python
import jax
import jax.numpy as jnp
from jax import lax

D = 1024
HEADS = 8
HEAD_DIM = 128
FF = 4096
SHORT = 512
ROWS = 3072
TOKENS = 24576
N_DP = 8


def draw_bucket(key, part):
    key = jax.random.fold_in(key, 7)
    first, second, third = jax.random.split(key, 3)
    kinds = (jax.random.randint(first, (N_DP,), 0, 10) < 3).astype(jnp.int32)
    chosen = jax.random.randint(second, (), 0, N_DP)
    other = (chosen + 1 + jax.random.randint(third, (), 0, N_DP - 1)) % N_DP
    kinds = kinds.at[chosen].set(1)
    kinds = kinds.at[other].set(0)
    return kinds


def levels(own_key, shape, cuts, least, high):
    level = 1.0
    for position, shards_of in cuts:
        steps = jax.random.uniform(jax.random.fold_in(jax.random.fold_in(own_key, 6), position), (shards_of,), jnp.float32, least / len(cuts), high / len(cuts))
        level = level * jnp.repeat(jnp.exp(steps), shape[position] // shards_of).reshape((-1,) + (1,) * (len(shape) - 1 - position))
    return level


def centred(rng, extent, scale, bound, cuts=(), kind=jnp.bfloat16):
    array = scale * jax.random.normal(rng, extent, jnp.float32)
    if cuts:
        array = array * levels(rng, extent, cuts, -0.22, 0.18)
    return jnp.clip(array, -bound, bound).astype(kind)


def setup_inputs(seed: int = 0) -> dict:
    splits = jax.random.split(jax.random.key(seed), 16)
    return {
        "layer_in": centred(splits[0], (TOKENS, D), 1.0, 6.0, ((0, 8), (1, 4)), jnp.float32),
        "bucket": draw_bucket(jax.random.fold_in(splits[15], 71), 0),
        "w_query": centred(splits[2], (D, D), D ** -0.5, 0.1875, ((1, 4),)),
        "w_key": centred(splits[3], (D, D), D ** -0.5, 0.1875, ((1, 4),)),
        "w_value": centred(splits[4], (D, D), D ** -0.5, 0.1875, ((1, 4),)),
        "w_proj": centred(splits[5], (D, D), (D // 16) ** -0.5, 0.75, ((0, 4),)),
        "attn_gain": jnp.clip(1.0 + 0.1 * jax.random.normal(splits[6], (D,), jnp.float32), 0.5, 1.5),
        "attn_shift": centred(splits[7], (D,), 0.5, 3.0, (), jnp.float32),
        "ffn_gain": jnp.clip(1.0 + 0.1 * jax.random.normal(splits[8], (D,), jnp.float32), 0.5, 1.5),
        "ffn_shift": centred(splits[9], (D,), 0.5, 3.0, (), jnp.float32),
        "w_expand": centred(splits[10], (D, FF), D ** -0.5, 0.1875, ((1, 32),)),
        "bias_expand": centred(splits[11], (1, FF), 0.5, 3.0, ((1, 32),)),
        "w_reduce": centred(splits[12], (D, FF), FF ** -0.5, 0.09375, ((1, 32),)),
        "bias_reduce": centred(splits[13], (D,), 0.5, 3.0, ((0, 4),), jnp.float32),
        "grad_out": centred(splits[14], (TOKENS, D), 1.0, 6.0, ((0, 8), (1, 4)), jnp.float32),
    }


@jax.custom_vjp
def low(v):
    return lax.optimization_barrier(v.astype(jnp.bfloat16)).astype(jnp.float32)

@jax.custom_vjp
def low_back(v):
    return v

def low_keep(v):
    return (low(v), None)

def low_pass(kept, grad):
    return (grad,)

def back_keep(v):
    return (v, None)

def back_low(kept, grad):
    return (low(grad),)
low.defvjp(low_keep, low_pass)
low_back.defvjp(back_keep, back_low)
precise = lax.Precision.HIGHEST
eps = 1e-05
masked_value = -1e+30

def matmul(left, right):
    return jnp.dot(left, right, precision=precise)

def layer_norm(values, gain, shift):
    center = values - lax.optimization_barrier(jnp.mean(values, axis=-1, keepdims=True))
    spread = lax.optimization_barrier(jnp.mean(center * center, axis=-1, keepdims=True))
    return center * lax.rsqrt(spread + eps) * gain + shift

def block_attend(query_block, key_rows, value_rows, query_place, key_place, slopes):
    logits = low_back(jnp.einsum('qhe,khe->hqk', query_block, key_rows, precision=precise) * HEAD_DIM ** (-0.5))
    distance = (query_place[:, None] - key_place[None, :]).astype(jnp.float32)
    scores = logits - slopes[:, None, None] * distance[None]
    allowed = (key_place[None, :] <= query_place[:, None])[None]
    scores = jnp.where(allowed, scores, masked_value)
    largest = lax.optimization_barrier(jnp.max(scores, axis=-1, keepdims=True))
    powers = jnp.exp(scores - largest)
    weights = powers / lax.optimization_barrier(jnp.sum(powers, axis=-1, keepdims=True))
    return jnp.einsum('hqk,khe->qhe', low(weights), value_rows, precision=precise)

def attend(queries, keys, values, slopes, is_long):
    rows = queries.shape[0]
    blocks = rows // SHORT
    local_place = jnp.arange(SHORT, dtype=jnp.int32)
    order = jnp.arange(blocks, dtype=jnp.int32)

    def short_path(queries, keys, values):

        def single_block(block_index):
            start = (block_index * SHORT).astype(jnp.int32)
            query_block = lax.dynamic_slice_in_dim(queries, start, SHORT, 0)
            key_block = lax.dynamic_slice_in_dim(keys, start, SHORT, 0)
            value_block = lax.dynamic_slice_in_dim(values, start, SHORT, 0)
            return block_attend(query_block, key_block, value_block, local_place, local_place, slopes)
        return lax.map(jax.checkpoint(single_block), order).reshape(queries.shape)

    def long_path(queries, keys, values):
        key_place = jnp.arange(rows, dtype=jnp.int32)

        def single_block(block_index):
            start = (block_index * SHORT).astype(jnp.int32)
            query_block = lax.dynamic_slice_in_dim(queries, start, SHORT, 0)
            return block_attend(query_block, keys, values, start + local_place, key_place, slopes)
        return lax.map(jax.checkpoint(single_block), order).reshape(queries.shape)
    return lax.cond(is_long, long_path, short_path, queries, keys, values)

def group_layer(rows_in, kind, w_query, w_key, w_value, w_proj, attn_gain, attn_shift, ffn_gain, ffn_shift, w_expand, bias_expand, w_reduce, bias_reduce):
    rows = rows_in.shape[0]
    slopes = jnp.exp2(-8.0 * (jnp.arange(HEADS, dtype=jnp.float32) + 1.0) / HEADS)
    normed_attn = low(layer_norm(rows_in, attn_gain, attn_shift))
    queries = low_back(low(matmul(normed_attn, w_query))).reshape(rows, HEADS, HEAD_DIM)
    keys = low_back(low(matmul(normed_attn, w_key))).reshape(rows, HEADS, HEAD_DIM)
    values = low_back(low(matmul(normed_attn, w_value))).reshape(rows, HEADS, HEAD_DIM)
    attended = low_back(low(attend(queries, keys, values, slopes, kind == 1).reshape(rows, D)))
    hidden = rows_in + low_back(matmul(attended, w_proj))
    normed_ffn = low(layer_norm(hidden, ffn_gain, ffn_shift))
    preact = low_back(matmul(normed_ffn, w_expand) + bias_expand)
    activated = low(jax.nn.gelu(preact))
    ffn_result = low_back(lax.dot_general(activated, w_reduce, (((1,), (1,)), ((), ())), precision=precise))
    return hidden + ffn_result + bias_reduce

def reference(layer_in, bucket, w_query, w_key, w_value, w_proj, attn_gain, attn_shift, ffn_gain, ffn_shift, w_expand, bias_expand, w_reduce, bias_reduce, grad_out):

    def forward(layer_in, w_query, w_key, w_value, w_proj, attn_gain, attn_shift, ffn_gain, ffn_shift, w_expand, bias_expand, w_reduce, bias_reduce):
        groups = layer_in.reshape(N_DP, ROWS, D)

        def per_group(member):
            return group_layer(member[0], member[1], w_query, w_key, w_value, w_proj, attn_gain, attn_shift, ffn_gain, ffn_shift, w_expand, bias_expand, w_reduce, bias_reduce)
        return lax.map(jax.checkpoint(per_group), (groups, bucket)).reshape(TOKENS, D)
    floats = (layer_in, w_query.astype(jnp.float32), w_key.astype(jnp.float32), w_value.astype(jnp.float32), w_proj.astype(jnp.float32), attn_gain, attn_shift, ffn_gain, ffn_shift, w_expand.astype(jnp.float32), bias_expand.astype(jnp.float32), w_reduce.astype(jnp.float32), bias_reduce)
    result, pullback = jax.vjp(forward, *floats)
    gradients = pullback(grad_out)
    return (result, gradients[0], gradients[1], gradients[2], gradients[3], gradients[4], gradients[5], gradients[6], gradients[7], gradients[8], gradients[9], gradients[10], gradients[11], gradients[12])
```

```python
import functools

import jax
import jax.numpy as jnp
from jax import lax
from jax.experimental import pallas as pl
from jax.experimental.pallas import tpu as pltpu
from jax.sharding import PartitionSpec as P

HEADS = 8
HEAD_DIM = 128
SHORT = 512
eps = 1e-05
masked_value = -1e30
LOG2E = 1.4426950408889634
LN2 = 0.6931471805599453
SCALE = HEAD_DIM ** (-0.5)
MIB = 1024 * 1024
f32 = jnp.float32
bf16 = jnp.bfloat16

NN = (((1,), (0,)), ((), ()))
NT = (((1,), (1,)), ((), ()))
TN = (((0,), (0,)), ((), ()))


def dot(left, right, dims=NN):
    return lax.dot_general(left, right, dims, preferred_element_type=f32)


def full_spec(shape):
    return pl.BlockSpec(shape, lambda *_: (0,) * len(shape))


def project_kernel(x0, x1, x2, x3, gain, shift, weight, normed, qkv):
    parts = [ref[...].astype(f32) for ref in (x0, x1, x2, x3)]
    width = parts[0].shape[1]
    features = 4 * width
    mean = sum(jnp.sum(p, axis=1, keepdims=True) for p in parts) * (1.0 / features)
    parts = [p - mean for p in parts]
    spread = sum(jnp.sum(p * p, axis=1, keepdims=True) for p in parts) * (1.0 / features)
    scale = lax.rsqrt(spread + eps)
    for k, p in enumerate(parts):
        cols = slice(k * width, (k + 1) * width)
        normed[:, cols] = (p * scale * gain[:, cols] + shift[:, cols]).astype(bf16)
    qkv[...] = dot(normed[...], weight[...]).astype(bf16)


def project(pieces, gain, shift, weight):
    rows, width = pieces[0].shape
    block = SHORT
    out = weight.shape[1]
    return pl.pallas_call(
        project_kernel,
        grid=(rows // block,),
        in_specs=[pl.BlockSpec((block, width), lambda i: (i, 0))] * 4
        + [full_spec(gain.shape), full_spec(shift.shape), full_spec(weight.shape)],
        out_specs=[
            pl.BlockSpec((block, 4 * width), lambda i: (i, 0)),
            pl.BlockSpec((block, out), lambda i: (i, 0)),
        ],
        out_shape=[
            jax.ShapeDtypeStruct((rows, 4 * width), bf16),
            jax.ShapeDtypeStruct((rows, out), bf16),
        ],
        compiler_params=pltpu.CompilerParams(vmem_limit_bytes=40 * MIB),
        cost_estimate=pl.CostEstimate(
            flops=2 * rows * 4 * width * out, bytes_accessed=rows * 4 * width * 4, transcendentals=0
        ),
    )(*pieces, gain, shift, weight)


def positions(block):
    return lax.broadcasted_iota(jnp.int32, (block, block), 0)


def attend_kernel(heads, kind, slopes, qkv, out, logsum, total):
    block = SHORT
    i = pl.program_id(0)
    low = jnp.where(kind[0] == 1, 0, i)
    start = pl.multiple_of(i * block, block)
    key_place = lax.broadcasted_iota(jnp.int32, (block, block), 0)
    query_place = lax.broadcasted_iota(jnp.int32, (block, block), 1)
    width = heads * HEAD_DIM

    def scores(h, j):
        at = pl.multiple_of(j * block, block)
        q = qkv[pl.ds(start, block), h * HEAD_DIM : (h + 1) * HEAD_DIM]
        k = qkv[pl.ds(at, block), width + h * HEAD_DIM : width + (h + 1) * HEAD_DIM]
        v = qkv[pl.ds(at, block), 2 * width + h * HEAD_DIM : 2 * width + (h + 1) * HEAD_DIM]
        place = (key_place + (j - i) * block).astype(f32) * (slopes[h] * LOG2E)
        return dot(k, q, NT) * (SCALE * LOG2E) + place, v

    carry = []
    for h in range(heads):
        s, v = scores(h, i)
        s = jnp.where(key_place <= query_place, s, masked_value)
        m = jnp.max(s, axis=0, keepdims=True)
        p = jnp.exp2(s - m)
        carry += [m, jnp.sum(p, axis=0, keepdims=True)]
        total[h] = dot(v, p.astype(bf16), TN)

    def step(j, carry):
        new = []
        for h in range(heads):
            m, l = carry[2 * h], carry[2 * h + 1]
            s, v = scores(h, j)
            m_new = jnp.maximum(m, jnp.max(s, axis=0, keepdims=True))
            p = jnp.exp2(s - m_new)
            fade = jnp.exp2(m - m_new)
            new += [m_new, l * fade + jnp.sum(p, axis=0, keepdims=True)]
            total[h] = total[h] * fade + dot(v, p.astype(bf16), TN)
        return tuple(new)

    carry = lax.fori_loop(low, i, step, tuple(carry))
    for h in range(heads):
        m, l = carry[2 * h], carry[2 * h + 1]
        out[:, h * HEAD_DIM : (h + 1) * HEAD_DIM] = (total[h] * (1.0 / l)).T.astype(bf16)
        logsum[0, h : h + 1, :] = m + jnp.log(l) * LOG2E


def attend(qkv, slopes, kind):
    rows = qkv.shape[0]
    width = qkv.shape[1] // 3
    heads = width // HEAD_DIM
    block = SHORT
    n = rows // block
    return pl.pallas_call(
        functools.partial(attend_kernel, heads),
        grid=(n,),
        in_specs=[
            pl.BlockSpec(memory_space=pltpu.SMEM),
            pl.BlockSpec(memory_space=pltpu.SMEM),
            full_spec(qkv.shape),
        ],
        out_specs=[
            pl.BlockSpec((block, width), lambda i: (i, 0)),
            pl.BlockSpec((1, heads, block), lambda i: (i, 0, 0)),
        ],
        out_shape=[
            jax.ShapeDtypeStruct((rows, width), bf16),
            jax.ShapeDtypeStruct((n, heads, block), f32),
        ],
        scratch_shapes=[pltpu.VMEM((heads, HEAD_DIM, block), f32)],
        compiler_params=pltpu.CompilerParams(vmem_limit_bytes=48 * MIB),
        cost_estimate=pl.CostEstimate(
            flops=8 * rows * rows * width, bytes_accessed=rows * width * 8, transcendentals=0
        ),
    )(kind, slopes, qkv)


def attend_back_kernel(heads, kind, slopes, qkv, grad, attended, logsum, grad_qkv, total_q, delta):
    block = SHORT
    j = pl.program_id(0)
    n = pl.num_programs(0)
    high = jnp.where(kind[0] == 1, n, j + 1)
    at = pl.multiple_of(j * block, block)
    key_place = lax.broadcasted_iota(jnp.int32, (block, block), 0)
    query_place = lax.broadcasted_iota(jnp.int32, (block, block), 1)
    width = heads * HEAD_DIM

    @pl.when(j == 0)
    def _():
        total_q[...] = jnp.zeros_like(total_q)

        def fill(i, _):
            here = pl.ds(pl.multiple_of(i * block, block), block)
            for h in range(heads):
                cols = slice(h * HEAD_DIM, (h + 1) * HEAD_DIM)
                both = grad[here, cols].astype(f32) * attended[here, cols].astype(f32)
                delta[i, h : h + 1, :] = jnp.sum(both.T, axis=0, keepdims=True)
            return 0

        lax.fori_loop(0, n, fill, 0)

    def pair(h, i, masked):
        start = pl.multiple_of(i * block, block)
        cols = slice(h * HEAD_DIM, (h + 1) * HEAD_DIM)
        q = qkv[pl.ds(start, block), h * HEAD_DIM : (h + 1) * HEAD_DIM]
        k = qkv[pl.ds(at, block), width + h * HEAD_DIM : width + (h + 1) * HEAD_DIM]
        v = qkv[pl.ds(at, block), 2 * width + h * HEAD_DIM : 2 * width + (h + 1) * HEAD_DIM]
        g = grad[pl.ds(start, block), cols]
        place = (key_place + (j - i) * block).astype(f32) * (slopes[h] * LOG2E)
        s = dot(k, q, NT) * (SCALE * LOG2E) + place
        if masked:
            s = jnp.where(key_place <= query_place, s, masked_value)
        p = jnp.exp2(s - logsum[i, h : h + 1, :])
        ds = (p * (dot(v, g, NT) - delta[i, h : h + 1, :])).astype(bf16)
        dv = dot(p.astype(bf16), g)
        dk = dot(ds, q)
        total_q[pl.ds(start, block), cols] += dot(ds, k, TN)
        return dk, dv

    first = [pair(h, j, True) for h in range(heads)]
    carry = tuple(x for both in first for x in both)

    def step(i, carry):
        new = []
        for h in range(heads):
            dk, dv = pair(h, i, False)
            new += [carry[2 * h] + dk, carry[2 * h + 1] + dv]
        return tuple(new)

    carry = lax.fori_loop(j + 1, high, step, carry)
    for h in range(heads):
        cols = slice(h * HEAD_DIM, (h + 1) * HEAD_DIM)
        grad_qkv[:, cols] = (total_q[pl.ds(at, block), cols] * SCALE).astype(bf16)
        grad_qkv[:, width + h * HEAD_DIM : width + (h + 1) * HEAD_DIM] = (
            carry[2 * h] * SCALE
        ).astype(bf16)
        grad_qkv[:, 2 * width + h * HEAD_DIM : 2 * width + (h + 1) * HEAD_DIM] = carry[
            2 * h + 1
        ].astype(bf16)


def attend_back(qkv, grad, attended, logsum, slopes, kind):
    rows = qkv.shape[0]
    width = qkv.shape[1] // 3
    heads = width // HEAD_DIM
    block = SHORT
    n = rows // block
    return pl.pallas_call(
        functools.partial(attend_back_kernel, heads),
        grid=(n,),
        in_specs=[
            pl.BlockSpec(memory_space=pltpu.SMEM),
            pl.BlockSpec(memory_space=pltpu.SMEM),
            full_spec(qkv.shape),
            full_spec(grad.shape),
            full_spec(attended.shape),
            full_spec(logsum.shape),
        ],
        out_specs=pl.BlockSpec((block, 3 * width), lambda j: (j, 0)),
        out_shape=jax.ShapeDtypeStruct((rows, 3 * width), bf16),
        scratch_shapes=[pltpu.VMEM((rows, width), f32), pltpu.VMEM((n, heads, block), f32)],
        compiler_params=pltpu.CompilerParams(vmem_limit_bytes=56 * MIB),
        cost_estimate=pl.CostEstimate(
            flops=20 * rows * rows * width, bytes_accessed=rows * width * 20, transcendentals=0
        ),
    )(kind, slopes, qkv, grad, attended, logsum)


def middle_kernel(
    x0, x1, x2, x3, a0, a1, a2, a3, g0, g1, g2, g3,
    w_proj, gain, shift, w_expand, bias, w_reduce,
    normed, activated, grad_pre, grad_hid, heads_keep, heads_send, attn_out, sums, grad_bias,
):
    step = pl.program_id(0)
    width = x0.shape[1]
    features = 4 * width
    attn = dot(a0[...], w_proj[0:width, :])
    for k, ref in enumerate((a1, a2, a3), 1):
        attn += dot(ref[...], w_proj[k * width : (k + 1) * width, :])
    attn_out[...] = attn[:, 0:width].astype(attn_out.dtype)
    hidden = attn + jnp.concatenate([ref[...] for ref in (x0, x1, x2, x3)], axis=1).astype(f32)
    centre = hidden - jnp.sum(hidden, axis=1, keepdims=True) * (1.0 / features)
    spread = jnp.sum(centre * centre, axis=1, keepdims=True) * (1.0 / features)
    scale = lax.rsqrt(spread + eps)
    centred = centre * scale
    low = (centred * gain[...] + shift[...]).astype(bf16)
    normed[...] = low
    z = dot(low, w_expand[...]) + bias[...]
    c = 0.7978845608028654
    z2 = z * z
    t = jnp.tanh(z * (c + (c * 0.044715) * z2))
    half = 0.5 + 0.5 * t
    activated[...] = (z * half).astype(bf16)
    slope = half + (0.5 * z) * (1.0 - t * t) * (c + (3.0 * c * 0.044715) * z2)
    grads = jnp.concatenate([ref[...] for ref in (g0, g1, g2, g3)], axis=1)
    gp = slope * dot(grads, w_reduce[...])
    gp_low = gp.astype(bf16)
    grad_pre[...] = gp_low
    gn = dot(gp_low, w_expand[...], NT)
    scaled = gn * gain[...]
    mean_scaled = jnp.sum(scaled, axis=1, keepdims=True) * (1.0 / features)
    mean_both = jnp.sum(scaled * centred, axis=1, keepdims=True) * (1.0 / features)
    back = (scaled - mean_scaled - centred * mean_both) * scale
    back_low = (back + 0.25 * grads.astype(f32)).astype(bf16)
    grad_hid[...] = back_low
    gh = dot(back_low, w_proj[...], NT).astype(bf16)
    heads_keep[:, 0:width] = gh[:, 0:width]
    heads_keep[:, width:] = gh[:, 2 * width : 3 * width]
    heads_send[:, 0:width] = gh[:, width : 2 * width]
    heads_send[:, width:] = gh[:, 3 * width :]

    @pl.when(step == 0)
    def _():
        sums[...] = jnp.zeros_like(sums)
        grad_bias[...] = jnp.zeros_like(grad_bias)

    sums[0:1, :] += jnp.sum(gn * centred, axis=0, keepdims=True)
    sums[1:2, :] += jnp.sum(gn, axis=0, keepdims=True)
    grad_bias[...] += jnp.sum(gp_low.astype(f32), axis=0, keepdims=True)


def middle(x, a, g, w_proj, gain, shift, w_expand, bias, w_reduce):
    rows, width = x[0].shape
    hidden_units = w_expand.shape[1]
    features = 4 * width
    block = SHORT

    def rows_of(columns):
        return pl.BlockSpec((block, columns), lambda i: (i, 0))

    def out(columns, kind=bf16):
        return jax.ShapeDtypeStruct((rows, columns), kind)

    return pl.pallas_call(
        middle_kernel,
        grid=(rows // block,),
        in_specs=[rows_of(width)] * 12
        + [full_spec(v.shape) for v in (w_proj, gain, shift, w_expand, bias, w_reduce)],
        out_specs=[
            rows_of(features),
            rows_of(hidden_units),
            rows_of(hidden_units),
            rows_of(features),
            rows_of(2 * width),
            rows_of(2 * width),
            rows_of(width),
            full_spec((2, features)),
            full_spec((1, hidden_units)),
        ],
        out_shape=[
            out(features),
            out(hidden_units),
            out(hidden_units),
            out(features),
            out(2 * width),
            out(2 * width),
            out(width, f32),
            jax.ShapeDtypeStruct((2, features), f32),
            jax.ShapeDtypeStruct((1, hidden_units), f32),
        ],
        compiler_params=pltpu.CompilerParams(vmem_limit_bytes=60 * MIB),
        cost_estimate=pl.CostEstimate(
            flops=10 * rows * features * hidden_units,
            bytes_accessed=rows * features * 16,
            transcendentals=0,
        ),
    )(*x, *a, *g, w_proj, gain, shift, w_expand, bias, w_reduce)


def finish_kernel(x0, x1, x2, x3, grad_qkv, weight, gain, grad_hid, keep, send, sums):
    step = pl.program_id(0)
    width = x0.shape[1]
    features = 4 * width
    gf = dot(grad_qkv[...], weight[...], NT)
    x = jnp.concatenate([ref[...] for ref in (x0, x1, x2, x3)], axis=1).astype(f32)
    centre = x - jnp.sum(x, axis=1, keepdims=True) * (1.0 / features)
    spread = jnp.sum(centre * centre, axis=1, keepdims=True) * (1.0 / features)
    scale = lax.rsqrt(spread + eps)
    centred = centre * scale
    scaled = gf * gain[...]
    mean_scaled = jnp.sum(scaled, axis=1, keepdims=True) * (1.0 / features)
    mean_both = jnp.sum(scaled * centred, axis=1, keepdims=True) * (1.0 / features)
    back = (scaled - mean_scaled - centred * mean_both) * scale
    total = (back + grad_hid[...].astype(f32)).astype(bf16)
    keep[:, 0:width] = total[:, 0:width]
    keep[:, width:] = total[:, 2 * width : 3 * width]
    send[:, 0:width] = total[:, width : 2 * width]
    send[:, width:] = total[:, 3 * width :]

    @pl.when(step == 0)
    def _():
        sums[...] = jnp.zeros_like(sums)

    sums[0:1, :] += jnp.sum(gf * centred, axis=0, keepdims=True)
    sums[1:2, :] += jnp.sum(gf, axis=0, keepdims=True)


def finish(x, grad_qkv, weight, gain, grad_hid):
    rows, width = x[0].shape
    features = 4 * width
    block = SHORT

    def rows_of(columns):
        return pl.BlockSpec((block, columns), lambda i: (i, 0))

    return pl.pallas_call(
        finish_kernel,
        grid=(rows // block,),
        in_specs=[rows_of(width)] * 4
        + [rows_of(grad_qkv.shape[1]), full_spec(weight.shape), full_spec(gain.shape), rows_of(features)],
        out_specs=[rows_of(2 * width), rows_of(2 * width), full_spec((2, features))],
        out_shape=[
            jax.ShapeDtypeStruct((rows, 2 * width), bf16),
            jax.ShapeDtypeStruct((rows, 2 * width), bf16),
            jax.ShapeDtypeStruct((2, features), f32),
        ],
        compiler_params=pltpu.CompilerParams(vmem_limit_bytes=48 * MIB),
        cost_estimate=pl.CostEstimate(
            flops=2 * rows * features * grad_qkv.shape[1],
            bytes_accessed=rows * features * 8,
            transcendentals=0,
        ),
    )(*x, grad_qkv, weight, gain, grad_hid)


def flip(value, axis, size, mask):
    return lax.ppermute(value, axis, [(k, k ^ mask) for k in range(size)])


def gather_head(piece):
    other_core = flip(piece, "head", 4, 1)
    other_chip = flip(piece, "head", 4, 2)
    return [piece, other_core, other_chip, flip(other_chip, "head", 4, 1)]


def scatter_head(keep, send):
    width = keep.shape[1] // 2
    got = flip(send, "head", 4, 1)
    far = keep[:, width:].astype(f32) + got[:, width:].astype(f32)
    near = keep[:, :width].astype(f32) + got[:, :width].astype(f32)
    return near + flip(far.astype(bf16), "head", 4, 2).astype(f32)


def reorder(value, rank, axis=0, size=4):
    width = value.shape[axis] // size
    return jnp.concatenate(
        [lax.dynamic_slice_in_dim(value, (rank ^ k) * width, width, axis) for k in range(size)], axis
    )


def masks_of(size):
    return [1 << k for k in range(size.bit_length() - 1)]


def gather_dp(value, size):
    blocks = {0: value}
    for mask in reversed(masks_of(size)):
        order = sorted(blocks)
        got = flip(jnp.stack([blocks[k] for k in order]), "dp", size, mask)
        for k, at in enumerate(order):
            blocks[at ^ mask] = got[k]
    return [blocks[k] for k in range(size)]


def scatter_dp(blocks, size):
    held = {k: blocks[k] for k in range(size)}
    for mask in masks_of(size):
        mine = [k for k in sorted(held) if not k & mask]
        got = flip(jnp.stack([held[k ^ mask] for k in mine]).astype(bf16), "dp", size, mask)
        held = {k: held[k] + got[p].astype(f32) for p, k in enumerate(mine)}
    return held[0]


def sum_small(value, dp_size):
    for mask in (1, 2):
        value = value + flip(value, "head", 4, mask)
    return sum_dp(value, dp_size)


def sum_dp(value, dp_size):
    for mask in masks_of(dp_size):
        value = value + flip(value, "dp", dp_size, mask)
    return value


def all_sum_dp(value, dp_size):
    parts = value.reshape(dp_size, value.shape[0] // dp_size, value.shape[1])
    me = lax.axis_index("dp")
    own = scatter_dp(reorder(parts, me, 0, dp_size), dp_size)
    blocks = gather_dp(own.astype(bf16), dp_size)
    return reorder(jnp.concatenate(blocks, 0), me, 0, dp_size).astype(f32)


def shards(
    dp_size,
    layer_in,
    bucket,
    w_query,
    w_key,
    w_value,
    w_proj,
    attn_gain,
    attn_shift,
    ffn_gain,
    ffn_shift,
    w_expand,
    bias_expand,
    w_reduce,
    bias_reduce,
    grad_out,
):
    rank = lax.axis_index("head")
    rows, width = layer_in.shape
    features = 4 * width
    heads_here = w_query.shape[1] // HEAD_DIM
    head_index = rank * heads_here + jnp.arange(heads_here)
    slopes = jnp.exp2(-8.0 * (head_index.astype(f32) + 1.0) / HEADS)

    gain_1 = reorder(attn_gain, rank)[None]
    shift_1 = reorder(attn_shift, rank)[None]
    gain_2 = reorder(ffn_gain, rank)[None]
    shift_2 = reorder(ffn_shift, rank)[None]
    w_qkv = reorder(jnp.concatenate([w_query, w_key, w_value], 1), rank)

    x = gather_head(layer_in.astype(bf16))
    proj = reorder(jnp.concatenate(gather_head(w_proj), 0), rank, 1)
    expand = jnp.concatenate(gather_dp(reorder(w_expand, rank), dp_size), 1)
    reduce = jnp.concatenate(gather_dp(reorder(w_reduce, rank), dp_size), 1)
    bias = jnp.concatenate(gather_dp(bias_expand, dp_size), 1).astype(f32)

    normed_attn, qkv = project(x, gain_1, shift_1, w_qkv)
    g = gather_head(grad_out.astype(bf16))
    attended, logsum = attend(qkv, slopes, bucket)
    a = gather_head(attended)

    normed_ffn, activated, grad_pre, grad_hid, heads_keep, heads_send, attn_out, sums_2, grad_bias = middle(
        x, a, g, proj, gain_2, shift_2, expand, bias, reduce
    )
    grad_heads = scatter_head(heads_keep, heads_send).astype(bf16)

    ffn_partial = dot(activated, reduce, NT).astype(bf16)
    ffn_out = scatter_head(
        jnp.concatenate([ffn_partial[:, :width], ffn_partial[:, 2 * width : 3 * width]], 1),
        jnp.concatenate([ffn_partial[:, width : 2 * width], ffn_partial[:, 3 * width :]], 1),
    )
    layer_out = layer_in + attn_out + ffn_out + bias_reduce

    grad_all = jnp.concatenate(g, 1)
    grad_wide = dot(normed_ffn, grad_pre, TN)
    grad_narrow = dot(grad_all, activated, TN)
    local = w_expand.shape[1]

    def columns_home(value):
        blocks = [value[:, k * local : (k + 1) * local] for k in range(dp_size)]
        return scatter_dp(blocks, dp_size)

    grad_expand = reorder(columns_home(grad_wide), rank)
    grad_reduce = reorder(columns_home(grad_narrow), rank)
    grad_bias_expand = columns_home(grad_bias)

    proj_part = reorder(dot(jnp.concatenate(a, 1), grad_hid, TN), rank, 1).astype(bf16)
    proj_sum = scatter_head(
        jnp.concatenate([proj_part[:width].T, proj_part[2 * width : 3 * width].T], 1),
        jnp.concatenate([proj_part[width : 2 * width].T, proj_part[3 * width :].T], 1),
    ).T
    grad_proj = all_sum_dp(proj_sum, dp_size)

    grad_qkv = attend_back(qkv, grad_heads, attended, logsum, slopes, bucket)
    weight_grad = reorder(dot(normed_attn, grad_qkv, TN), rank)
    weight_grad = all_sum_dp(weight_grad, dp_size)
    grad_query, grad_key, grad_value = (
        weight_grad[:, k * heads_here * HEAD_DIM : (k + 1) * heads_here * HEAD_DIM] for k in range(3)
    )
    keep, send, sums_1 = finish(x, grad_qkv, w_qkv, gain_1, grad_hid)
    grad_in = scatter_head(keep, send)

    small = sum_small(
        reorder(jnp.concatenate([sums_2, sums_1], 0), rank, 1), dp_size
    )
    grad_bias_reduce = sum_dp(jnp.sum(grad_out, axis=0), dp_size)
    return (
        layer_out,
        grad_in,
        grad_query,
        grad_key,
        grad_value,
        grad_proj,
        small[2],
        small[3],
        small[0],
        small[1],
        grad_expand,
        grad_bias_expand,
        grad_reduce,
        grad_bias_reduce,
    )


def solution(mesh):
    placed = (
        P("dp", "head"),
        P("dp"),
        P(None, "head"),
        P(None, "head"),
        P(None, "head"),
        P("head", None),
        P(),
        P(),
        P(),
        P(),
        P(None, ("dp", "head")),
        P(None, ("dp", "head")),
        P(None, ("dp", "head")),
        P("head"),
        P("dp", "head"),
    )
    return jax.shard_map(
        functools.partial(shards, mesh.shape["dp"]),
        mesh=mesh,
        in_specs=placed,
        out_specs=(
            P("dp", "head"),
            P("dp", "head"),
            P(None, "head"),
            P(None, "head"),
            P(None, "head"),
            P("head", None),
            P(),
            P(),
            P(),
            P(),
            P(None, ("dp", "head")),
            P(None, ("dp", "head")),
            P(None, ("dp", "head")),
            P("head"),
        ),
        check_vma=False,
    )
```

```python
import functools

import jax
import jax.numpy as jnp
from jax import lax
from jax.experimental import pallas as pl
from jax.experimental.pallas import tpu as pltpu
from jax.sharding import PartitionSpec as P

HEADS = 8
HEAD_DIM = 128
SHORT = 512
eps = 1e-05
masked_value = -1e30
LOG2E = 1.4426950408889634
LN2 = 0.6931471805599453
SCALE = HEAD_DIM ** (-0.5)
MIB = 1024 * 1024
f32 = jnp.float32
bf16 = jnp.bfloat16

NN = (((1,), (0,)), ((), ()))
NT = (((1,), (1,)), ((), ()))
TN = (((0,), (0,)), ((), ()))


def dot(left, right, dims=NN):
    return lax.dot_general(left, right, dims, preferred_element_type=f32)


def full_spec(shape):
    return pl.BlockSpec(shape, lambda *_: (0,) * len(shape))


MESH = pl.DeviceIdType.MESH


def partner(index, mask):
    return index + mask - 2 * mask * ((index // mask) % 2)


def masks_of(size):
    return [1 << k for k in range(size.bit_length() - 1)]


def send_to(src, dst, send, recv, **where):
    return pltpu.make_async_remote_copy(
        src_ref=src, dst_ref=dst, send_sem=send, recv_sem=recv, device_id=where, device_id_type=MESH
    )


def greet(dp_masks):
    me, group = lax.axis_index("head"), lax.axis_index("dp")
    barrier = pltpu.get_barrier_semaphore()
    for mask in (1, 2):
        pl.semaphore_signal(
            barrier, inc=1, device_id={"head": partner(me, mask)}, device_id_type=MESH
        )
    for mask in dp_masks:
        pl.semaphore_signal(
            barrier, inc=1, device_id={"dp": partner(group, mask)}, device_id_type=MESH
        )
    pl.semaphore_wait(barrier, 2 + len(dp_masks))


def at_rows(r, block=SHORT):
    return pl.ds(pl.multiple_of(r * block, block), block)


def at_cols(k, width):
    return pl.ds(pl.multiple_of(k * width, width), width)


class HeadGather:
    def __init__(self, own, full, width, sems):
        self.own, self.full, self.width = own, full, width
        self.me = lax.axis_index("head")
        self.core, self.chip = partner(self.me, 1), partner(self.me, 2)
        self.far = partner(self.core, 2)
        self.sems = sems

    def slot(self, r, who):
        return self.full.at[at_rows(r), at_cols(who, self.width)]

    def copy(self, r, src, owner, kind, **where):
        return send_to(
            src, self.slot(r, owner), self.sems.at[2 * kind, r], self.sems.at[2 * kind + 1, r], **where
        )

    def own_src(self, r):
        return self.own(r) if self.own is not None else self.slot(r, self.me)

    def start(self, r):
        self.copy(r, self.own_src(r), self.me, 0, head=self.chip).start()
        self.copy(r, self.own_src(r), self.me, 1, head=self.core).start()

    def forward(self, r):
        self.copy(r, self.slot(r, self.chip), self.chip, 0, head=self.chip).wait_recv()
        self.copy(r, self.slot(r, self.chip), self.chip, 2, head=self.core).start()

    def arrive(self, r):
        self.copy(r, self.slot(r, self.core), self.core, 1, head=self.core).wait_recv()
        self.copy(r, self.slot(r, self.far), self.far, 2, head=self.core).wait_recv()

    def sent(self, r):
        self.copy(r, self.own_src(r), self.me, 0, head=self.chip).wait_send()
        self.copy(r, self.own_src(r), self.me, 1, head=self.core).wait_send()
        self.copy(r, self.slot(r, self.chip), self.chip, 2, head=self.core).wait_send()


class DpGather:
    def __init__(self, own, full, width, masks, send, recv):
        self.own, self.full, self.width = own, full, width
        self.masks = list(reversed(masks))
        self.group = lax.axis_index("dp")
        self.send, self.recv = send, recv
        held, self.plan, at = [0], [], 0
        for mask in self.masks:
            self.plan.append((mask, [(k, at + p) for p, k in enumerate(held)]))
            at += len(held)
            held = held + [k ^ mask for k in held]

    def block(self, k):
        who = self.group
        for mask in masks_of(1 << len(self.masks)):
            if k & mask:
                who = partner(who, mask)
        return self.full.at[:, at_cols(who, self.width)]

    def copies(self, step, there):
        mask, items = self.plan[step]
        out = []
        for k, sem in items:
            if there:
                src, at = (self.own if k == 0 else self.block(k)), self.block(k)
            else:
                src = at = self.block(k ^ mask)
            out.append(
                send_to(src, at, self.send.at[sem], self.recv.at[sem], dp=partner(self.group, mask))
            )
        return out

    def start(self, step):
        for copy in self.copies(step, True):
            copy.start()

    def arrive(self, step):
        for copy in self.copies(step, False):
            copy.wait_recv()

    def sent(self):
        for step in range(len(self.plan)):
            for copy in self.copies(step, True):
                copy.wait_send()


def head_slopes(me, heads, n_head=4):
    slopes = []
    for h in range(heads):
        value = jnp.float32(0.0)
        for k in range(n_head):
            value = jnp.where(me == k, jnp.float32(2.0 ** (-8.0 * (k * heads + h + 1) / HEADS)), value)
        slopes.append(value)
    return slopes


def first_kernel(
    masks, gather,
    kind, layer_in, wq, wk, wv, gain, shift, bias_expand, w_proj, w_expand, w_reduce,
    x_out, a_out, normed_out, qkv_out, proj_out, expand_out, reduce_out, bias_out, logsum,
    x_buf, normed_buf, qkv_buf, a_buf, bias_buf, total, x_sems, a_sems, p_sems, local_sems, copy_sems,
    e_send, e_recv, r_send, r_recv, b_send, b_recv,
):
    rows, width = layer_in.shape
    features = 4 * width
    block = SHORT
    n = rows // block
    heads = width // HEAD_DIM
    me, group = lax.axis_index("head"), lax.axis_index("dp")
    core, chip = partner(me, 1), partner(me, 2)
    greet(masks if gather else [])

    x_gather = HeadGather(None, x_buf, width, x_sems)
    a_gather = HeadGather(lambda r: a_buf.at[at_rows(r), :], a_out, width, a_sems)

    def p_copy(src, owner, k, **where):
        return send_to(src, proj_out.at[at_cols(owner, width), :], p_sems.at[2 * k], p_sems.at[2 * k + 1], **where)

    if gather:
        expand = DpGather(w_expand, expand_out, w_expand.shape[1], masks, e_send, e_recv)
        reduce = DpGather(w_reduce, reduce_out, w_reduce.shape[1], masks, r_send, r_recv)
        bias_buf[...] = jnp.broadcast_to(bias_expand[...], bias_buf.shape)
        bias = DpGather(bias_buf, bias_out, w_expand.shape[1], masks, b_send, b_recv)
        expand.start(0)
        bias.start(0)
        reduce.start(0)

    def own_chunk(r):
        x_buf[at_rows(r), at_cols(me, width)] = layer_in[at_rows(r), :].astype(bf16)
        x_gather.start(r)

    own_chunk(0)
    own_chunk(1)
    keeps = [pltpu.make_async_copy(w_proj, proj_out.at[at_cols(me, width), :], local_sems.at[0])]
    if gather:
        own_cols = at_cols(group, w_expand.shape[1])
        keeps.append(pltpu.make_async_copy(w_expand, expand_out.at[:, own_cols], local_sems.at[1]))
        keeps.append(pltpu.make_async_copy(w_reduce, reduce_out.at[:, own_cols], local_sems.at[2]))
        keeps.append(pltpu.make_async_copy(bias_buf, bias_out.at[:, own_cols], local_sems.at[3]))
    for keep in keeps:
        keep.start()

    slopes = [s * LOG2E for s in head_slopes(me, heads)]
    apart = (1 - kind[0]).astype(f32) * masked_value
    key_place = lax.broadcasted_iota(jnp.int32, (block, block), 0)
    query_place = lax.broadcasted_iota(jnp.int32, (block, block), 1)

    def normed_copy(r):
        return pltpu.make_async_copy(normed_buf.at[r % 2], normed_out.at[at_rows(r), :], copy_sems.at[0, r])

    def x_copy(r):
        return pltpu.make_async_copy(x_buf.at[at_rows(r), :], x_out.at[at_rows(r), :], copy_sems.at[1, r])

    def qkv_copy(r):
        return pltpu.make_async_copy(qkv_buf.at[at_rows(r), :], qkv_out.at[at_rows(r), :], copy_sems.at[2, r])

    def a_copy(r):
        return pltpu.make_async_copy(
            a_buf.at[at_rows(r), :], a_out.at[at_rows(r), at_cols(me, width)], copy_sems.at[3, r]
        )

    def chunk(i):
        x_gather.arrive(i)
        x_copy(i).start()
        x = x_buf[at_rows(i), :].astype(f32)
        centre = x - jnp.sum(x, axis=1, keepdims=True) * (1.0 / features)
        spread = jnp.sum(centre * centre, axis=1, keepdims=True) * (1.0 / features)
        low = (centre * lax.rsqrt(spread + eps) * gain[...] + shift[...]).astype(bf16)

        @pl.when(i >= 2)
        def _():
            normed_copy(i - 2).wait()

        normed_buf[i % 2] = low
        normed_copy(i).start()
        for k, w in enumerate((wq, wk, wv)):
            qkv_buf[at_rows(i), k * width : (k + 1) * width] = dot(low, w[...]).astype(bf16)
        qkv_copy(i).start()

        def scores(h, j):
            q = qkv_buf[at_rows(i), h * HEAD_DIM : (h + 1) * HEAD_DIM]
            k = qkv_buf[at_rows(j), width + h * HEAD_DIM : width + (h + 1) * HEAD_DIM]
            v = qkv_buf[at_rows(j), 2 * width + h * HEAD_DIM : 2 * width + (h + 1) * HEAD_DIM]
            place = (key_place + (j - i) * block).astype(f32) * slopes[h]
            return dot(k, q, NT) * (SCALE * LOG2E) + place, v

        carry = []
        for h in range(heads):
            s, v = scores(h, i)
            s = jnp.where(key_place <= query_place, s, masked_value)
            m = jnp.max(s, axis=0, keepdims=True)
            p = jnp.exp2(s - m)
            carry += [m, jnp.sum(p, axis=0, keepdims=True)]
            total[h] = dot(v, p.astype(bf16), TN)

        def step(j, carry):
            new = []
            for h in range(heads):
                m, l = carry[2 * h], carry[2 * h + 1]
                s, v = scores(h, j)
                s = s + apart
                m_new = jnp.maximum(m, jnp.max(s, axis=0, keepdims=True))
                p = jnp.exp2(s - m_new)
                fade = jnp.exp2(m - m_new)
                new += [m_new, l * fade + jnp.sum(p, axis=0, keepdims=True)]
                total[h] = total[h] * fade + dot(v, p.astype(bf16), TN)
            return tuple(new)

        carry = lax.fori_loop(0, i, step, tuple(carry))
        for h in range(heads):
            m, l = carry[2 * h], carry[2 * h + 1]
            a_buf[at_rows(i), h * HEAD_DIM : (h + 1) * HEAD_DIM] = (total[h] * (1.0 / l)).T.astype(bf16)
            logsum[i, h : h + 1, :] = m + jnp.log(l) * LOG2E
        a_gather.start(i)
        a_copy(i).start()

    steps = len(masks)

    def body(r, _):
        @pl.when(r < n)
        def _():
            x_gather.forward(r)

            @pl.when(r + 2 < n)
            def _():
                own_chunk(r + 2)

            @pl.when(r + 2 == n)
            def _():
                p_copy(w_proj, me, 0, head=chip).start()
                p_copy(w_proj, me, 1, head=core).start()

        if gather:
            for s in range(1, steps):
                @pl.when(r == min(2 * s, n - 1))
                def _(s=s):
                    expand.arrive(s - 1)
                    bias.arrive(s - 1)
                    expand.start(s)
                    bias.start(s)

                @pl.when(r == min(2 * s + 1, n))
                def _(s=s):
                    reduce.arrive(s - 1)
                    reduce.start(s)

        @pl.when(r >= 1)
        def _():
            chunk(r - 1)

        return 0

    lax.fori_loop(0, n + 1, body, 0)

    p_copy(w_proj, chip, 0, head=chip).wait_recv()
    p_forward = p_copy(proj_out.at[at_cols(chip, width), :], chip, 2, head=core)
    p_forward.start()

    def pass_on(r, _):
        a_gather.forward(r)
        return 0

    lax.fori_loop(0, n, pass_on, 0)

    def settle(r, _):
        a_gather.arrive(r)
        a_gather.sent(r)
        x_gather.sent(r)
        x_copy(r).wait()
        qkv_copy(r).wait()
        a_copy(r).wait()

        @pl.when(r >= n - 2)
        def _():
            normed_copy(r).wait()

        return 0

    lax.fori_loop(0, n, settle, 0)
    p_copy(w_proj, core, 1, head=core).wait_recv()
    p_copy(w_proj, partner(core, 2), 2, head=core).wait_recv()
    p_copy(w_proj, me, 0, head=chip).wait_send()
    p_copy(w_proj, me, 1, head=core).wait_send()
    p_forward.wait_send()
    for keep in keeps:
        keep.wait()
    if gather:
        expand.arrive(steps - 1)
        reduce.arrive(steps - 1)
        bias.arrive(steps - 1)
        expand.sent()
        reduce.sent()
        bias.sent()


def first(kind, layer_in, wq, wk, wv, gain, shift, bias_expand, w_proj, w_expand, w_reduce, dp_size):
    rows, width = layer_in.shape
    features = 4 * width
    block = SHORT
    n = rows // block
    heads = width // HEAD_DIM
    masks = masks_of(dp_size)
    local = w_expand.shape[1]
    gather = local % 128 == 0
    units = local * dp_size if gather else 128
    any_spec = pl.BlockSpec(memory_space=pl.ANY)
    vmem = pl.BlockSpec(memory_space=pltpu.VMEM)
    blocks = max(dp_size - 1, 1)
    outs = pl.pallas_call(
        functools.partial(first_kernel, masks, gather),
        in_specs=[pl.BlockSpec(memory_space=pltpu.SMEM)] + [vmem] * 7 + [any_spec] * 3,
        out_specs=[any_spec] * 8 + [vmem],
        out_shape=[
            jax.ShapeDtypeStruct((rows, features), bf16),
            jax.ShapeDtypeStruct((rows, features), bf16),
            jax.ShapeDtypeStruct((rows, features), bf16),
            jax.ShapeDtypeStruct((rows, 3 * width), bf16),
            jax.ShapeDtypeStruct((features, features), bf16),
            jax.ShapeDtypeStruct((features, units), bf16),
            jax.ShapeDtypeStruct((features, units), bf16),
            jax.ShapeDtypeStruct((16, units), bf16),
            jax.ShapeDtypeStruct((n, heads, block), f32),
        ],
        scratch_shapes=[
            pltpu.VMEM((rows, features), bf16),
            pltpu.VMEM((2, block, features), bf16),
            pltpu.VMEM((rows, 3 * width), bf16),
            pltpu.VMEM((rows, width), bf16),
            pltpu.VMEM((16, local), bf16),
            pltpu.VMEM((heads, HEAD_DIM, block), f32),
            pltpu.SemaphoreType.DMA((6, n)),
            pltpu.SemaphoreType.DMA((6, n)),
            pltpu.SemaphoreType.DMA((6,)),
            pltpu.SemaphoreType.DMA((4,)),
            pltpu.SemaphoreType.DMA((4, n)),
            pltpu.SemaphoreType.DMA((blocks,)),
            pltpu.SemaphoreType.DMA((blocks,)),
            pltpu.SemaphoreType.DMA((blocks,)),
            pltpu.SemaphoreType.DMA((blocks,)),
            pltpu.SemaphoreType.DMA((blocks,)),
            pltpu.SemaphoreType.DMA((blocks,)),
        ],
        compiler_params=pltpu.CompilerParams(
            vmem_limit_bytes=56 * MIB, collective_id=0, has_side_effects=True
        ),
    )(kind, layer_in, wq, wk, wv, gain, shift, bias_expand, w_proj, w_expand, w_reduce)
    x, a, normed, qkv, proj, expand, reduce, bias, logsum = outs
    bias = bias[:1]
    if not gather:
        bias = lax.all_gather(bias_expand, "dp", axis=1, tiled=True)
        expand = lax.all_gather(w_expand, "dp", axis=1, tiled=True)
        reduce = lax.all_gather(w_reduce, "dp", axis=1, tiled=True)
    return x, a, normed, qkv, proj, expand, reduce, bias.astype(f32), logsum


class HeadScatter:
    def __init__(self, width, src, from_core, far, near, from_chip, sems):
        self.width, self.src, self.from_core, self.far = width, src, from_core, far
        self.near, self.from_chip, self.sems = near, from_chip, sems
        self.me = lax.axis_index("head")
        self.core, self.chip = partner(self.me, 1), partner(self.me, 2)

    def to_core(self, r, k):
        who = self.core if k == 0 else partner(self.core, 2)
        return send_to(
            self.src(r).at[:, at_cols(who, self.width)],
            self.from_core.at[at_rows(r), k * self.width : (k + 1) * self.width],
            self.sems.at[2 * k, r],
            self.sems.at[2 * k + 1, r],
            head=self.core,
        )

    def to_chip(self, r):
        return send_to(
            self.far.at[r % 2],
            self.from_chip.at[at_rows(r), :],
            self.sems.at[4, r],
            self.sems.at[5, r],
            head=self.chip,
        )

    def start(self, r):
        self.to_core(r, 1).start()
        self.to_core(r, 0).start()

    def middle(self, r):
        src = self.src(r)
        self.to_core(r, 1).wait()
        self.far[r % 2] = (
            src[:, at_cols(self.chip, self.width)].astype(f32)
            + self.from_core[at_rows(r), self.width :].astype(f32)
        ).astype(bf16)
        self.to_chip(r).start()
        self.to_core(r, 0).wait()
        self.near[r % 2] = (
            src[:, at_cols(self.me, self.width)].astype(f32)
            + self.from_core[at_rows(r), : self.width].astype(f32)
        )

    def finish(self, r):
        self.to_chip(r).wait()
        return self.near[r % 2] + self.from_chip[at_rows(r), :].astype(f32)


GELU_C = 0.7978845608028654


def second_kernel(
    x_in, a_in, grad_out, layer_in, w_proj, w_expand, w_reduce, gain, shift, bias,
    grad_heads, grad_hid_out, ffn_out, hid_own, wide_out, narrow_out, proj_out, sums, grad_bias, grad_bias_reduce,
    g_buf, x_buf, a_buf, hid_buf, own_buf, ffn_buf, gh_buf, from_core, far_buf, near_buf, from_chip, wide, narrow, proj,
    g_sems, s_sems, copy_sems, final_sems,
):
    rows, width = layer_in.shape
    features = 4 * width
    block = SHORT
    n = rows // block
    me = lax.axis_index("head")
    greet([])

    g_gather = HeadGather(None, g_buf, width, g_sems)
    scatter = HeadScatter(width, lambda r: gh_buf.at[r % 2], from_core, far_buf, near_buf, from_chip, s_sems)

    def own_chunk(r):
        chunk = grad_out[at_rows(r), :]
        g_buf[at_rows(r), at_cols(me, width)] = chunk.astype(bf16)
        g_gather.start(r)
        return chunk

    def load_x(r):
        return pltpu.make_async_copy(x_in.at[at_rows(r), :], x_buf.at[r % 2], copy_sems.at[0, r])

    def load_a(r):
        return pltpu.make_async_copy(a_in.at[at_rows(r), :], a_buf.at[r % 2], copy_sems.at[1, r])

    def store_hid(r):
        return pltpu.make_async_copy(hid_buf.at[r % 2], grad_hid_out.at[at_rows(r), :], copy_sems.at[2, r])

    def store_ffn(r):
        return pltpu.make_async_copy(ffn_buf.at[r % 2], ffn_out.at[at_rows(r), :], copy_sems.at[3, r])

    def store_own(r):
        return pltpu.make_async_copy(own_buf.at[r % 2], hid_own.at[at_rows(r), :], copy_sems.at[4, r])

    def final(k, slot, buf, out):
        half = features // 2
        return pltpu.make_async_copy(
            buf.at[slot], out.at[slot * half : (slot + 1) * half, :], final_sems.at[k, slot]
        )

    own_chunk(0)
    own_chunk(1)
    load_x(0).start()
    load_a(0).start()
    wide[...] = jnp.zeros_like(wide)
    narrow[...] = jnp.zeros_like(narrow)
    proj[...] = jnp.zeros_like(proj)
    sums[...] = jnp.zeros_like(sums)
    grad_bias[...] = jnp.zeros_like(grad_bias)
    grad_bias_reduce[...] = jnp.sum(grad_out[...], axis=0, keepdims=True)

    def body(r, _):
        g_gather.forward(r)

        @pl.when(r + 2 < n)
        def _():
            own_chunk(r + 2)

        load_x(r).wait()
        load_a(r).wait()

        @pl.when(r + 1 < n)
        def _():
            load_x(r + 1).start()
            load_a(r + 1).start()

        @pl.when(r >= 2)
        def _():
            store_hid(r - 2).wait()
            store_ffn(r - 2).wait()
            store_own(r - 2).wait()

        slot = r % 2
        a = a_buf[slot]
        attn = dot(a, w_proj[...])
        hidden = attn + x_buf[slot].astype(f32)
        own_buf[slot] = dot(a, w_proj[:, at_cols(me, width)]) + layer_in[at_rows(r), :]
        store_own(r).start()
        centre = hidden - jnp.sum(hidden, axis=1, keepdims=True) * (1.0 / features)
        spread = jnp.sum(centre * centre, axis=1, keepdims=True) * (1.0 / features)
        scale = lax.rsqrt(spread + eps)
        centred = centre * scale
        low = (centred * gain[...] + shift[...]).astype(bf16)
        z = dot(low, w_expand[...]) + bias[...]
        z2 = z * z
        t = jnp.tanh(z * (GELU_C + (GELU_C * 0.044715) * z2))
        half = 0.5 + 0.5 * t
        activated = (z * half).astype(bf16)
        slope = half + (0.5 * z) * (1.0 - t * t) * (GELU_C + (3.0 * GELU_C * 0.044715) * z2)
        g_gather.arrive(r)
        g = g_buf[at_rows(r), :]
        gp = slope * dot(g, w_reduce[...])
        gp_low = gp.astype(bf16)
        gn = dot(gp_low, w_expand[...], NT)
        scaled = gn * gain[...]
        mean_scaled = jnp.sum(scaled, axis=1, keepdims=True) * (1.0 / features)
        mean_both = jnp.sum(scaled * centred, axis=1, keepdims=True) * (1.0 / features)
        back = (scaled - mean_scaled - centred * mean_both) * scale
        back_low = (back + 0.25 * g.astype(f32)).astype(bf16)
        hid_buf[slot] = back_low
        store_hid(r).start()
        gh_buf[slot] = dot(back_low, w_proj[...], NT).astype(bf16)
        scatter.start(r)
        sums[0:1, :] += jnp.sum(gn * centred, axis=0, keepdims=True)
        sums[1:2, :] += jnp.sum(gn, axis=0, keepdims=True)
        grad_bias[...] += jnp.sum(gp_low.astype(f32), axis=0, keepdims=True)
        ffn_buf[slot] = dot(activated, w_reduce[...], NT).astype(bf16)
        store_ffn(r).start()
        wide[...] += dot(low, gp_low, TN)
        narrow[...] += dot(g, activated, TN)
        scatter.middle(r)
        proj[...] += dot(a, back_low, TN)

        @pl.when(r >= 1)
        def _():
            grad_heads[at_rows(r - 1), :] = scatter.finish(r - 1).astype(bf16)

        return 0

    lax.fori_loop(0, n, body, 0)
    for k, (full, buf, out) in enumerate(
        ((wide, ffn_buf, wide_out), (narrow, x_buf, narrow_out), (proj, hid_buf, proj_out))
    ):
        for p in range(2):
            if buf is ffn_buf:
                store_ffn(n - 2 + p).wait()
            if buf is hid_buf:
                store_hid(n - 2 + p).wait()
            half = features // 2
            slot = (n - 2 + p) % 2
            buf[slot] = full[slot * half : (slot + 1) * half, :].astype(bf16)
            final(k, slot, buf, out).start()
    grad_heads[at_rows(n - 1), :] = scatter.finish(n - 1).astype(bf16)
    for k, (buf, out) in enumerate(((ffn_buf, wide_out), (x_buf, narrow_out), (hid_buf, proj_out))):
        for slot in range(2):
            final(k, slot, buf, out).wait()

    def settle(r, _):
        g_gather.sent(r)

        @pl.when(r >= n - 2)
        def _():
            store_own(r).wait()

        return 0

    lax.fori_loop(0, n, settle, 0)


def second(x, a, grad_out, layer_in, w_proj, w_expand, w_reduce, gain, shift, bias):
    rows, width = layer_in.shape
    features = 4 * width
    units = w_expand.shape[1]
    block = SHORT
    n = rows // block
    any_spec = pl.BlockSpec(memory_space=pl.ANY)
    vmem = pl.BlockSpec(memory_space=pltpu.VMEM)
    return pl.pallas_call(
        second_kernel,
        in_specs=[any_spec] * 2 + [vmem] * 8,
        out_specs=[vmem] + [any_spec] * 6 + [vmem] * 3,
        out_shape=[
            jax.ShapeDtypeStruct((rows, width), bf16),
            jax.ShapeDtypeStruct((rows, features), bf16),
            jax.ShapeDtypeStruct((rows, features), bf16),
            jax.ShapeDtypeStruct((rows, width), f32),
            jax.ShapeDtypeStruct((features, units), bf16),
            jax.ShapeDtypeStruct((features, units), bf16),
            jax.ShapeDtypeStruct((features, features), bf16),
            jax.ShapeDtypeStruct((2, features), f32),
            jax.ShapeDtypeStruct((1, units), f32),
            jax.ShapeDtypeStruct((1, width), f32),
        ],
        scratch_shapes=[
            pltpu.VMEM((rows, features), bf16),
            pltpu.VMEM((2, block, features), bf16),
            pltpu.VMEM((2, block, features), bf16),
            pltpu.VMEM((2, block, features), bf16),
            pltpu.VMEM((2, block, width), f32),
            pltpu.VMEM((2, block, features), bf16),
            pltpu.VMEM((2, block, features), bf16),
            pltpu.VMEM((rows, 2 * width), bf16),
            pltpu.VMEM((2, block, width), bf16),
            pltpu.VMEM((2, block, width), f32),
            pltpu.VMEM((rows, width), bf16),
            pltpu.VMEM((features, units), f32),
            pltpu.VMEM((features, units), f32),
            pltpu.VMEM((features, features), f32),
            pltpu.SemaphoreType.DMA((6, n)),
            pltpu.SemaphoreType.DMA((6, n)),
            pltpu.SemaphoreType.DMA((5, n)),
            pltpu.SemaphoreType.DMA((3, 2)),
        ],
        compiler_params=pltpu.CompilerParams(
            vmem_limit_bytes=62 * MIB, collective_id=1, has_side_effects=True
        ),
    )(x, a, grad_out, layer_in, w_proj, w_expand, w_reduce, gain, shift, bias)


def attend_back_kernel(heads, kind, slopes, qkv, grad, attended, logsum, grad_qkv, total_q, delta):
    block = SHORT
    j = pl.program_id(0)
    n = pl.num_programs(0)
    high = jnp.where(kind[0] == 1, n, j + 1)
    at = pl.multiple_of(j * block, block)
    key_place = lax.broadcasted_iota(jnp.int32, (block, block), 0)
    query_place = lax.broadcasted_iota(jnp.int32, (block, block), 1)
    width = heads * HEAD_DIM

    @pl.when(j == 0)
    def _():
        total_q[...] = jnp.zeros_like(total_q)

        def fill(i, _):
            here = pl.ds(pl.multiple_of(i * block, block), block)
            for h in range(heads):
                cols = slice(h * HEAD_DIM, (h + 1) * HEAD_DIM)
                both = grad[here, cols].astype(f32) * attended[here, cols].astype(f32)
                delta[i, h : h + 1, :] = jnp.sum(both.T, axis=0, keepdims=True)
            return 0

        lax.fori_loop(0, n, fill, 0)

    def pair(h, i, masked):
        start = pl.multiple_of(i * block, block)
        cols = slice(h * HEAD_DIM, (h + 1) * HEAD_DIM)
        q = qkv[pl.ds(start, block), h * HEAD_DIM : (h + 1) * HEAD_DIM]
        k = qkv[pl.ds(at, block), width + h * HEAD_DIM : width + (h + 1) * HEAD_DIM]
        v = qkv[pl.ds(at, block), 2 * width + h * HEAD_DIM : 2 * width + (h + 1) * HEAD_DIM]
        g = grad[pl.ds(start, block), cols]
        place = (key_place + (j - i) * block).astype(f32) * (slopes[h] * LOG2E)
        s = dot(k, q, NT) * (SCALE * LOG2E) + place
        if masked:
            s = jnp.where(key_place <= query_place, s, masked_value)
        p = jnp.exp2(s - logsum[i, h : h + 1, :])
        ds = (p * (dot(v, g, NT) - delta[i, h : h + 1, :])).astype(bf16)
        dv = dot(p.astype(bf16), g)
        dk = dot(ds, q)
        total_q[pl.ds(start, block), cols] += dot(ds, k, TN)
        return dk, dv

    first = [pair(h, j, True) for h in range(heads)]
    carry = tuple(x for both in first for x in both)

    def step(i, carry):
        new = []
        for h in range(heads):
            dk, dv = pair(h, i, False)
            new += [carry[2 * h] + dk, carry[2 * h + 1] + dv]
        return tuple(new)

    carry = lax.fori_loop(j + 1, high, step, carry)
    for h in range(heads):
        cols = slice(h * HEAD_DIM, (h + 1) * HEAD_DIM)
        grad_qkv[:, cols] = (total_q[pl.ds(at, block), cols] * SCALE).astype(bf16)
        grad_qkv[:, width + h * HEAD_DIM : width + (h + 1) * HEAD_DIM] = (
            carry[2 * h] * SCALE
        ).astype(bf16)
        grad_qkv[:, 2 * width + h * HEAD_DIM : 2 * width + (h + 1) * HEAD_DIM] = carry[
            2 * h + 1
        ].astype(bf16)


def attend_back(qkv, grad, attended, logsum, slopes, kind):
    rows = qkv.shape[0]
    width = qkv.shape[1] // 3
    heads = width // HEAD_DIM
    block = SHORT
    n = rows // block
    return pl.pallas_call(
        functools.partial(attend_back_kernel, heads),
        grid=(n,),
        in_specs=[
            pl.BlockSpec(memory_space=pltpu.SMEM),
            pl.BlockSpec(memory_space=pltpu.SMEM),
            full_spec(qkv.shape),
            full_spec(grad.shape),
            full_spec(attended.shape),
            full_spec(logsum.shape),
        ],
        out_specs=pl.BlockSpec((block, 3 * width), lambda j: (j, 0)),
        out_shape=jax.ShapeDtypeStruct((rows, 3 * width), bf16),
        scratch_shapes=[pltpu.VMEM((rows, width), f32), pltpu.VMEM((n, heads, block), f32)],
        compiler_params=pltpu.CompilerParams(vmem_limit_bytes=56 * MIB),
        cost_estimate=pl.CostEstimate(
            flops=20 * rows * rows * width, bytes_accessed=rows * width * 20, transcendentals=0
        ),
    )(kind, slopes, qkv, grad, attended, logsum)


def finish_kernel(x_in, grad_qkv, weight, gain, grad_hid, last, sums):
    step = pl.program_id(0)
    features = x_in.shape[1]
    gf = dot(grad_qkv[...], weight[...], NT)
    x = x_in[...].astype(f32)
    centre = x - jnp.sum(x, axis=1, keepdims=True) * (1.0 / features)
    spread = jnp.sum(centre * centre, axis=1, keepdims=True) * (1.0 / features)
    scale = lax.rsqrt(spread + eps)
    centred = centre * scale
    scaled = gf * gain[...]
    mean_scaled = jnp.sum(scaled, axis=1, keepdims=True) * (1.0 / features)
    mean_both = jnp.sum(scaled * centred, axis=1, keepdims=True) * (1.0 / features)
    back = (scaled - mean_scaled - centred * mean_both) * scale
    last[...] = (back + grad_hid[...].astype(f32)).astype(bf16)

    @pl.when(step == 0)
    def _():
        sums[...] = jnp.zeros_like(sums)

    sums[0:1, :] += jnp.sum(gf * centred, axis=0, keepdims=True)
    sums[1:2, :] += jnp.sum(gf, axis=0, keepdims=True)


def finish(x, grad_qkv, weight, gain, grad_hid):
    rows, features = x.shape
    block = SHORT

    def rows_of(columns):
        return pl.BlockSpec((block, columns), lambda i: (i, 0))

    return pl.pallas_call(
        finish_kernel,
        grid=(rows // block,),
        in_specs=[rows_of(features), rows_of(grad_qkv.shape[1]), full_spec(weight.shape), full_spec(gain.shape), rows_of(features)],
        out_specs=[rows_of(features), full_spec((2, features))],
        out_shape=[jax.ShapeDtypeStruct((rows, features), bf16), jax.ShapeDtypeStruct((2, features), f32)],
        compiler_params=pltpu.CompilerParams(vmem_limit_bytes=48 * MIB),
        cost_estimate=pl.CostEstimate(
            flops=2 * rows * features * grad_qkv.shape[1], bytes_accessed=rows * features * 8, transcendentals=0
        ),
    )(x, grad_qkv, weight, gain, grad_hid)


def flip(value, axis, size, mask):
    return lax.ppermute(value, axis, [(k, k ^ mask) for k in range(size)])


def reorder(value, rank, axis=0, size=4):
    width = value.shape[axis] // size
    return jnp.concatenate(
        [lax.dynamic_slice_in_dim(value, (rank ^ k) * width, width, axis) for k in range(size)], axis
    )


def scatter_dp(blocks, size):
    held = {k: blocks[k].astype(f32) for k in range(size)}
    for mask in masks_of(size):
        mine = [k for k in sorted(held) if not k & mask]
        got = flip(jnp.stack([held[k ^ mask] for k in mine]).astype(bf16), "dp", size, mask)
        held = {k: held[k] + got[p].astype(f32) for p, k in enumerate(mine)}
    return held[0]


def gather_dp(value, size):
    blocks = {0: value}
    for mask in reversed(masks_of(size)):
        order = sorted(blocks)
        got = flip(jnp.stack([blocks[k] for k in order]), "dp", size, mask)
        for k, at in enumerate(order):
            blocks[at ^ mask] = got[k]
    return [blocks[k] for k in range(size)]


def scatter_head(value, rank):
    width = value.shape[1] // 4

    def cols(k):
        return lax.dynamic_slice_in_dim(value, (rank ^ k) * width, width, 1)

    got = flip(jnp.concatenate([cols(1), cols(3)], 1), "head", 4, 1).astype(f32)
    far = cols(2).astype(f32) + got[:, width:]
    near = cols(0).astype(f32) + got[:, :width]
    return near + flip(far.astype(bf16), "head", 4, 2).astype(f32)


def sum_dp(value, dp_size):
    for mask in masks_of(dp_size):
        value = value + flip(value, "dp", dp_size, mask)
    return value


def sum_small(value, dp_size):
    for mask in (1, 2):
        value = value + flip(value, "head", 4, mask)
    return sum_dp(value, dp_size)


def all_sum_dp(value, dp_size):
    me = lax.axis_index("dp")
    parts = reorder(value, me, 0, dp_size)
    r = value.shape[0] // dp_size
    own = scatter_dp([parts[k * r : (k + 1) * r] for k in range(dp_size)], dp_size)
    return reorder(jnp.concatenate(gather_dp(own.astype(bf16), dp_size), 0), me, 0, dp_size).astype(f32)


def shards(
    dp_size,
    layer_in,
    bucket,
    w_query,
    w_key,
    w_value,
    w_proj,
    attn_gain,
    attn_shift,
    ffn_gain,
    ffn_shift,
    w_expand,
    bias_expand,
    w_reduce,
    bias_reduce,
    grad_out,
):
    rank = lax.axis_index("head")
    group = lax.axis_index("dp")
    rows, width = layer_in.shape
    features = 4 * width
    heads_here = w_query.shape[1] // HEAD_DIM
    head_index = rank * heads_here + jnp.arange(heads_here)
    slopes = jnp.exp2(-8.0 * (head_index.astype(f32) + 1.0) / HEADS)
    gain_1, shift_1 = attn_gain[None], attn_shift[None]
    x, a, normed_attn, qkv, proj, expand, reduce, bias, logsum = first(
        bucket, layer_in, w_query, w_key, w_value, gain_1, shift_1, bias_expand, w_proj, w_expand, w_reduce, dp_size
    )
    (
        grad_heads, grad_hid, ffn_partial, hid_own, grad_wide, grad_narrow, proj_part, sums_2, grad_bias, grad_bias_reduce,
    ) = second(
        x, a, grad_out, layer_in, proj, expand, reduce, ffn_gain[None], ffn_shift[None], bias
    )
    layer_out = hid_own + bias_reduce + scatter_head(ffn_partial, rank)
    local = w_expand.shape[1]

    def columns_home(value):
        value = reorder(value, group, 1, dp_size)
        return scatter_dp([value[:, k * local : (k + 1) * local] for k in range(dp_size)], dp_size)

    grad_expand = columns_home(grad_wide)
    grad_reduce = columns_home(grad_narrow)
    grad_bias_expand = columns_home(grad_bias)
    grad_proj = all_sum_dp(scatter_head(proj_part.T, rank).T, dp_size)

    attended = lax.dynamic_slice_in_dim(a, rank * width, width, 1)
    grad_qkv = attend_back(qkv, grad_heads, attended, logsum, slopes, bucket)
    weight_grad = all_sum_dp(dot(normed_attn, grad_qkv, TN), dp_size)
    grad_query, grad_key, grad_value = (weight_grad[:, k * width : (k + 1) * width] for k in range(3))
    w_qkv = jnp.concatenate([w_query, w_key, w_value], 1)
    last, sums_1 = finish(x, grad_qkv, w_qkv, gain_1, grad_hid)
    grad_in = scatter_head(last, rank)
    small = sum_small(jnp.concatenate([sums_2, sums_1], 0), dp_size)
    grad_bias_reduce = sum_dp(grad_bias_reduce[0], dp_size)
    return (
        layer_out,
        grad_in,
        grad_query,
        grad_key,
        grad_value,
        grad_proj,
        small[2],
        small[3],
        small[0],
        small[1],
        grad_expand,
        grad_bias_expand,
        grad_reduce,
        grad_bias_reduce,
    )


def solution(mesh):
    placed = (
        P("dp", "head"),
        P("dp"),
        P(None, "head"),
        P(None, "head"),
        P(None, "head"),
        P("head", None),
        P(),
        P(),
        P(),
        P(),
        P(None, ("dp", "head")),
        P(None, ("dp", "head")),
        P(None, ("dp", "head")),
        P("head"),
        P("dp", "head"),
    )
    return jax.shard_map(
        functools.partial(shards, mesh.shape["dp"]),
        mesh=mesh,
        in_specs=placed,
        out_specs=(
            P("dp", "head"),
            P("dp", "head"),
            P(None, "head"),
            P(None, "head"),
            P(None, "head"),
            P("head", None),
            P(),
            P(),
            P(),
            P(),
            P(None, ("dp", "head")),
            P(None, ("dp", "head")),
            P(None, ("dp", "head")),
            P("head"),
        ),
        check_vma=False,
    )
```

```python
import functools

import jax
import jax.numpy as jnp
from jax import lax
from jax.experimental import pallas as pl
from jax.experimental.pallas import tpu as pltpu
from jax.sharding import PartitionSpec as P

HEADS = 8
HEAD_DIM = 128
SHORT = 512
eps = 1e-05
masked_value = -1e30
LOG2E = 1.4426950408889634
LN2 = 0.6931471805599453
SCALE = HEAD_DIM ** (-0.5)
MIB = 1024 * 1024
f32 = jnp.float32
bf16 = jnp.bfloat16

NN = (((1,), (0,)), ((), ()))
NT = (((1,), (1,)), ((), ()))
TN = (((0,), (0,)), ((), ()))


def dot(left, right, dims=NN):
    return lax.dot_general(left, right, dims, preferred_element_type=f32)


def full_spec(shape):
    return pl.BlockSpec(shape, lambda *_: (0,) * len(shape))


MESH = pl.DeviceIdType.MESH


def partner(index, mask):
    return index + mask - 2 * mask * ((index // mask) % 2)


def masks_of(size):
    return [1 << k for k in range(size.bit_length() - 1)]


def send_to(src, dst, send, recv, **where):
    return pltpu.make_async_remote_copy(
        src_ref=src, dst_ref=dst, send_sem=send, recv_sem=recv, device_id=where, device_id_type=MESH
    )


def greet(dp_masks):
    me, group = lax.axis_index("head"), lax.axis_index("dp")
    barrier = pltpu.get_barrier_semaphore()
    for mask in (1, 2):
        pl.semaphore_signal(
            barrier, inc=1, device_id={"head": partner(me, mask)}, device_id_type=MESH
        )
    for mask in dp_masks:
        pl.semaphore_signal(
            barrier, inc=1, device_id={"dp": partner(group, mask)}, device_id_type=MESH
        )
    pl.semaphore_wait(barrier, 2 + len(dp_masks))


def at_rows(r, block=SHORT):
    return pl.ds(pl.multiple_of(r * block, block), block)


def at_cols(k, width):
    return pl.ds(pl.multiple_of(k * width, width), width)


class HeadGather:
    def __init__(self, own, full, width, sems):
        self.own, self.full, self.width = own, full, width
        self.me = lax.axis_index("head")
        self.core, self.chip = partner(self.me, 1), partner(self.me, 2)
        self.far = partner(self.core, 2)
        self.sems = sems

    def slot(self, r, who):
        return self.full.at[at_rows(r), at_cols(who, self.width)]

    def copy(self, r, src, owner, kind, **where):
        return send_to(
            src, self.slot(r, owner), self.sems.at[2 * kind, r], self.sems.at[2 * kind + 1, r], **where
        )

    def own_src(self, r):
        return self.own(r) if self.own is not None else self.slot(r, self.me)

    def start(self, r):
        self.copy(r, self.own_src(r), self.me, 0, head=self.chip).start()
        self.copy(r, self.own_src(r), self.me, 1, head=self.core).start()

    def forward(self, r):
        self.copy(r, self.slot(r, self.chip), self.chip, 0, head=self.chip).wait_recv()
        self.copy(r, self.slot(r, self.chip), self.chip, 2, head=self.core).start()

    def arrive(self, r):
        self.copy(r, self.slot(r, self.core), self.core, 1, head=self.core).wait_recv()
        self.copy(r, self.slot(r, self.far), self.far, 2, head=self.core).wait_recv()

    def sent(self, r):
        self.copy(r, self.own_src(r), self.me, 0, head=self.chip).wait_send()
        self.copy(r, self.own_src(r), self.me, 1, head=self.core).wait_send()
        self.copy(r, self.slot(r, self.chip), self.chip, 2, head=self.core).wait_send()


class DpGather:
    def __init__(self, own, full, width, masks, send, recv):
        self.own, self.full, self.width = own, full, width
        self.masks = list(reversed(masks))
        self.group = lax.axis_index("dp")
        self.send, self.recv = send, recv
        held, self.plan, at = [0], [], 0
        for mask in self.masks:
            self.plan.append((mask, [(k, at + p) for p, k in enumerate(held)]))
            at += len(held)
            held = held + [k ^ mask for k in held]

    def block(self, k):
        who = self.group
        for mask in masks_of(1 << len(self.masks)):
            if k & mask:
                who = partner(who, mask)
        return self.full.at[:, at_cols(who, self.width)]

    def copies(self, step, there):
        mask, items = self.plan[step]
        out = []
        for k, sem in items:
            if there:
                src, at = (self.own if k == 0 else self.block(k)), self.block(k)
            else:
                src = at = self.block(k ^ mask)
            out.append(
                send_to(src, at, self.send.at[sem], self.recv.at[sem], dp=partner(self.group, mask))
            )
        return out

    def start(self, step):
        for copy in self.copies(step, True):
            copy.start()

    def arrive(self, step):
        for copy in self.copies(step, False):
            copy.wait_recv()

    def sent(self):
        for step in range(len(self.plan)):
            for copy in self.copies(step, True):
                copy.wait_send()


def head_slopes(me, heads, n_head=4):
    slopes = []
    for h in range(heads):
        value = jnp.float32(0.0)
        for k in range(n_head):
            value = jnp.where(me == k, jnp.float32(2.0 ** (-8.0 * (k * heads + h + 1) / HEADS)), value)
        slopes.append(value)
    return slopes


def first_kernel(
    masks, gather,
    kind, layer_in, wq, wk, wv, gain, shift, bias_expand, w_proj, w_expand, w_reduce,
    x_out, a_out, normed_out, qkv_out, proj_out, expand_out, reduce_out, bias_out, logsum,
    x_buf, normed_buf, qkv_buf, a_buf, bias_buf, total, x_sems, a_sems, p_sems, local_sems, copy_sems,
    e_send, e_recv, r_send, r_recv, b_send, b_recv,
):
    rows, width = layer_in.shape
    features = 4 * width
    block = SHORT
    n = rows // block
    heads = width // HEAD_DIM
    me, group = lax.axis_index("head"), lax.axis_index("dp")
    core, chip = partner(me, 1), partner(me, 2)
    greet(masks if gather else [])

    x_gather = HeadGather(None, x_buf, width, x_sems)
    a_gather = HeadGather(lambda r: a_buf.at[at_rows(r), :], a_out, width, a_sems)

    def p_copy(src, owner, k, **where):
        return send_to(src, proj_out.at[at_cols(owner, width), :], p_sems.at[2 * k], p_sems.at[2 * k + 1], **where)

    if gather:
        expand = DpGather(w_expand, expand_out, w_expand.shape[1], masks, e_send, e_recv)
        reduce = DpGather(w_reduce, reduce_out, w_reduce.shape[1], masks, r_send, r_recv)
        bias_buf[...] = jnp.broadcast_to(bias_expand[...], bias_buf.shape)
        bias = DpGather(bias_buf, bias_out, w_expand.shape[1], masks, b_send, b_recv)
        expand.start(0)
        bias.start(0)
        reduce.start(0)

    def own_chunk(r):
        x_buf[at_rows(r), at_cols(me, width)] = layer_in[at_rows(r), :].astype(bf16)
        x_gather.start(r)

    own_chunk(0)
    own_chunk(1)
    keeps = [pltpu.make_async_copy(w_proj, proj_out.at[at_cols(me, width), :], local_sems.at[0])]
    if gather:
        own_cols = at_cols(group, w_expand.shape[1])
        keeps.append(pltpu.make_async_copy(w_expand, expand_out.at[:, own_cols], local_sems.at[1]))
        keeps.append(pltpu.make_async_copy(w_reduce, reduce_out.at[:, own_cols], local_sems.at[2]))
        keeps.append(pltpu.make_async_copy(bias_buf, bias_out.at[:, own_cols], local_sems.at[3]))
    for keep in keeps:
        keep.start()

    slopes = [s * LOG2E for s in head_slopes(me, heads)]
    apart = (1 - kind[0]).astype(f32) * masked_value
    key_place = lax.broadcasted_iota(jnp.int32, (block, block), 0)
    query_place = lax.broadcasted_iota(jnp.int32, (block, block), 1)

    def normed_copy(r):
        return pltpu.make_async_copy(normed_buf.at[r % 2], normed_out.at[at_rows(r), :], copy_sems.at[0, r])

    def x_copy(r):
        return pltpu.make_async_copy(x_buf.at[at_rows(r), :], x_out.at[at_rows(r), :], copy_sems.at[1, r])

    def qkv_copy(r):
        return pltpu.make_async_copy(qkv_buf.at[at_rows(r), :], qkv_out.at[at_rows(r), :], copy_sems.at[2, r])

    def a_copy(r):
        return pltpu.make_async_copy(
            a_buf.at[at_rows(r), :], a_out.at[at_rows(r), at_cols(me, width)], copy_sems.at[3, r]
        )

    def chunk(i):
        x_gather.arrive(i)
        x_copy(i).start()
        x = x_buf[at_rows(i), :].astype(f32)
        centre = x - jnp.sum(x, axis=1, keepdims=True) * (1.0 / features)
        spread = jnp.sum(centre * centre, axis=1, keepdims=True) * (1.0 / features)
        low = (centre * lax.rsqrt(spread + eps) * gain[...] + shift[...]).astype(bf16)

        @pl.when(i >= 2)
        def _():
            normed_copy(i - 2).wait()

        normed_buf[i % 2] = low
        normed_copy(i).start()
        for k, w in enumerate((wq, wk, wv)):
            qkv_buf[at_rows(i), k * width : (k + 1) * width] = dot(low, w[...]).astype(bf16)
        qkv_copy(i).start()

        def scores(h, j):
            q = qkv_buf[at_rows(i), h * HEAD_DIM : (h + 1) * HEAD_DIM]
            k = qkv_buf[at_rows(j), width + h * HEAD_DIM : width + (h + 1) * HEAD_DIM]
            v = qkv_buf[at_rows(j), 2 * width + h * HEAD_DIM : 2 * width + (h + 1) * HEAD_DIM]
            place = (key_place + (j - i) * block).astype(f32) * slopes[h]
            return dot(k, q, NT) * (SCALE * LOG2E) + place, v

        carry = []
        for h in range(heads):
            s, v = scores(h, i)
            s = jnp.where(key_place <= query_place, s, masked_value)
            m = jnp.max(s, axis=0, keepdims=True)
            p = jnp.exp2(s - m)
            carry += [m, jnp.sum(p, axis=0, keepdims=True)]
            total[h] = dot(v, p.astype(bf16), TN)

        def step(j, carry):
            new = []
            for h in range(heads):
                m, l = carry[2 * h], carry[2 * h + 1]
                s, v = scores(h, j)
                s = s + apart
                m_new = jnp.maximum(m, jnp.max(s, axis=0, keepdims=True))
                p = jnp.exp2(s - m_new)
                fade = jnp.exp2(m - m_new)
                new += [m_new, l * fade + jnp.sum(p, axis=0, keepdims=True)]
                total[h] = total[h] * fade + dot(v, p.astype(bf16), TN)
            return tuple(new)

        carry = lax.fori_loop(0, i, step, tuple(carry))
        for h in range(heads):
            m, l = carry[2 * h], carry[2 * h + 1]
            a_buf[at_rows(i), h * HEAD_DIM : (h + 1) * HEAD_DIM] = (total[h] * (1.0 / l)).T.astype(bf16)
            logsum[i, h : h + 1, :] = m + jnp.log(l) * LOG2E
        a_gather.start(i)
        a_copy(i).start()

    steps = len(masks)

    def body(r, _):
        @pl.when(r < n)
        def _():
            x_gather.forward(r)

            @pl.when(r + 2 < n)
            def _():
                own_chunk(r + 2)

            @pl.when(r + 2 == n)
            def _():
                p_copy(w_proj, me, 0, head=chip).start()
                p_copy(w_proj, me, 1, head=core).start()

        if gather:
            for s in range(1, steps):
                @pl.when(r == min(2 * s, n - 1))
                def _(s=s):
                    expand.arrive(s - 1)
                    bias.arrive(s - 1)
                    expand.start(s)
                    bias.start(s)

                @pl.when(r == min(2 * s + 1, n))
                def _(s=s):
                    reduce.arrive(s - 1)
                    reduce.start(s)

        @pl.when(r >= 1)
        def _():
            chunk(r - 1)

        return 0

    lax.fori_loop(0, n + 1, body, 0)

    p_copy(w_proj, chip, 0, head=chip).wait_recv()
    p_forward = p_copy(proj_out.at[at_cols(chip, width), :], chip, 2, head=core)
    p_forward.start()

    def pass_on(r, _):
        a_gather.forward(r)
        return 0

    lax.fori_loop(0, n, pass_on, 0)

    def settle(r, _):
        a_gather.arrive(r)
        a_gather.sent(r)
        x_gather.sent(r)
        x_copy(r).wait()
        qkv_copy(r).wait()
        a_copy(r).wait()

        @pl.when(r >= n - 2)
        def _():
            normed_copy(r).wait()

        return 0

    lax.fori_loop(0, n, settle, 0)
    p_copy(w_proj, core, 1, head=core).wait_recv()
    p_copy(w_proj, partner(core, 2), 2, head=core).wait_recv()
    p_copy(w_proj, me, 0, head=chip).wait_send()
    p_copy(w_proj, me, 1, head=core).wait_send()
    p_forward.wait_send()
    for keep in keeps:
        keep.wait()
    if gather:
        expand.arrive(steps - 1)
        reduce.arrive(steps - 1)
        bias.arrive(steps - 1)
        expand.sent()
        reduce.sent()
        bias.sent()


def first(kind, layer_in, wq, wk, wv, gain, shift, bias_expand, w_proj, w_expand, w_reduce, dp_size):
    rows, width = layer_in.shape
    features = 4 * width
    block = SHORT
    n = rows // block
    heads = width // HEAD_DIM
    masks = masks_of(dp_size)
    local = w_expand.shape[1]
    gather = local % 128 == 0
    units = local * dp_size if gather else 128
    any_spec = pl.BlockSpec(memory_space=pl.ANY)
    vmem = pl.BlockSpec(memory_space=pltpu.VMEM)
    blocks = max(dp_size - 1, 1)
    outs = pl.pallas_call(
        functools.partial(first_kernel, masks, gather),
        in_specs=[pl.BlockSpec(memory_space=pltpu.SMEM)] + [vmem] * 7 + [any_spec] * 3,
        out_specs=[any_spec] * 8 + [vmem],
        out_shape=[
            jax.ShapeDtypeStruct((rows, features), bf16),
            jax.ShapeDtypeStruct((rows, features), bf16),
            jax.ShapeDtypeStruct((rows, features), bf16),
            jax.ShapeDtypeStruct((rows, 3 * width), bf16),
            jax.ShapeDtypeStruct((features, features), bf16),
            jax.ShapeDtypeStruct((features, units), bf16),
            jax.ShapeDtypeStruct((features, units), bf16),
            jax.ShapeDtypeStruct((16, units), bf16),
            jax.ShapeDtypeStruct((n, heads, block), f32),
        ],
        scratch_shapes=[
            pltpu.VMEM((rows, features), bf16),
            pltpu.VMEM((2, block, features), bf16),
            pltpu.VMEM((rows, 3 * width), bf16),
            pltpu.VMEM((rows, width), bf16),
            pltpu.VMEM((16, local), bf16),
            pltpu.VMEM((heads, HEAD_DIM, block), f32),
            pltpu.SemaphoreType.DMA((6, n)),
            pltpu.SemaphoreType.DMA((6, n)),
            pltpu.SemaphoreType.DMA((6,)),
            pltpu.SemaphoreType.DMA((4,)),
            pltpu.SemaphoreType.DMA((4, n)),
            pltpu.SemaphoreType.DMA((blocks,)),
            pltpu.SemaphoreType.DMA((blocks,)),
            pltpu.SemaphoreType.DMA((blocks,)),
            pltpu.SemaphoreType.DMA((blocks,)),
            pltpu.SemaphoreType.DMA((blocks,)),
            pltpu.SemaphoreType.DMA((blocks,)),
        ],
        compiler_params=pltpu.CompilerParams(
            vmem_limit_bytes=56 * MIB, collective_id=0, has_side_effects=True
        ),
    )(kind, layer_in, wq, wk, wv, gain, shift, bias_expand, w_proj, w_expand, w_reduce)
    x, a, normed, qkv, proj, expand, reduce, bias, logsum = outs
    bias = bias[:1]
    if not gather:
        bias = lax.all_gather(bias_expand, "dp", axis=1, tiled=True)
        expand = lax.all_gather(w_expand, "dp", axis=1, tiled=True)
        reduce = lax.all_gather(w_reduce, "dp", axis=1, tiled=True)
    return x, a, normed, qkv, proj, expand, reduce, bias.astype(f32), logsum


class HeadScatter:
    def __init__(self, width, src, from_core, far, near, from_chip, sems):
        self.width, self.src, self.from_core, self.far = width, src, from_core, far
        self.near, self.from_chip, self.sems = near, from_chip, sems
        self.me = lax.axis_index("head")
        self.core, self.chip = partner(self.me, 1), partner(self.me, 2)

    def to_core(self, r, k):
        who = self.core if k == 0 else partner(self.core, 2)
        return send_to(
            self.src(r).at[:, at_cols(who, self.width)],
            self.from_core.at[at_rows(r), k * self.width : (k + 1) * self.width],
            self.sems.at[2 * k, r],
            self.sems.at[2 * k + 1, r],
            head=self.core,
        )

    def to_chip(self, r):
        return send_to(
            self.far.at[r % 2],
            self.from_chip.at[at_rows(r), :],
            self.sems.at[4, r],
            self.sems.at[5, r],
            head=self.chip,
        )

    def start(self, r):
        self.to_core(r, 1).start()
        self.to_core(r, 0).start()

    def middle(self, r):
        src = self.src(r)
        self.to_core(r, 1).wait()
        self.far[r % 2] = (
            src[:, at_cols(self.chip, self.width)].astype(f32)
            + self.from_core[at_rows(r), self.width :].astype(f32)
        ).astype(bf16)
        self.to_chip(r).start()
        self.to_core(r, 0).wait()
        self.near[r % 2] = (
            src[:, at_cols(self.me, self.width)].astype(f32)
            + self.from_core[at_rows(r), : self.width].astype(f32)
        )

    def finish(self, r):
        self.to_chip(r).wait()
        return self.near[r % 2] + self.from_chip[at_rows(r), :].astype(f32)


GELU_C = 0.7978845608028654


def second_kernel(
    x_in, a_in, grad_out, layer_in, w_proj, w_expand, w_reduce, gain, shift, bias,
    grad_heads, grad_hid_out, ffn_out, hid_own, wide_out, narrow_out, proj_out, sums, grad_bias, grad_bias_reduce,
    g_buf, x_buf, a_buf, hid_buf, own_buf, ffn_buf, gh_buf, from_core, far_buf, near_buf, from_chip, wide, narrow, proj,
    g_sems, s_sems, copy_sems, final_sems,
):
    rows, width = layer_in.shape
    features = 4 * width
    block = SHORT
    n = rows // block
    me = lax.axis_index("head")
    greet([])

    g_gather = HeadGather(None, g_buf, width, g_sems)
    scatter = HeadScatter(width, lambda r: gh_buf.at[r % 2], from_core, far_buf, near_buf, from_chip, s_sems)

    def own_chunk(r):
        chunk = grad_out[at_rows(r), :]
        g_buf[at_rows(r), at_cols(me, width)] = chunk.astype(bf16)
        g_gather.start(r)
        return chunk

    def load_x(r):
        return pltpu.make_async_copy(x_in.at[at_rows(r), :], x_buf.at[r % 2], copy_sems.at[0, r])

    def load_a(r):
        return pltpu.make_async_copy(a_in.at[at_rows(r), :], a_buf.at[r % 2], copy_sems.at[1, r])

    def store_hid(r):
        return pltpu.make_async_copy(hid_buf.at[r % 2], grad_hid_out.at[at_rows(r), :], copy_sems.at[2, r])

    def store_ffn(r):
        return pltpu.make_async_copy(ffn_buf.at[r % 2], ffn_out.at[at_rows(r), :], copy_sems.at[3, r])

    def store_own(r):
        return pltpu.make_async_copy(own_buf.at[r % 2], hid_own.at[at_rows(r), :], copy_sems.at[4, r])

    def final(k, slot, buf, out):
        half = features // 2
        return pltpu.make_async_copy(
            buf.at[slot], out.at[slot * half : (slot + 1) * half, :], final_sems.at[k, slot]
        )

    own_chunk(0)
    own_chunk(1)
    load_x(0).start()
    load_a(0).start()
    wide[...] = jnp.zeros_like(wide)
    narrow[...] = jnp.zeros_like(narrow)
    proj[...] = jnp.zeros_like(proj)
    sums[...] = jnp.zeros_like(sums)
    grad_bias[...] = jnp.zeros_like(grad_bias)
    grad_bias_reduce[...] = jnp.sum(grad_out[...], axis=0, keepdims=True)

    def body(r, _):
        g_gather.forward(r)

        @pl.when(r + 2 < n)
        def _():
            own_chunk(r + 2)

        load_x(r).wait()
        load_a(r).wait()

        @pl.when(r + 1 < n)
        def _():
            load_x(r + 1).start()
            load_a(r + 1).start()

        @pl.when(r >= 2)
        def _():
            store_hid(r - 2).wait()
            store_ffn(r - 2).wait()
            store_own(r - 2).wait()

        slot = r % 2
        a = a_buf[slot]
        attn = dot(a, w_proj[...])
        hidden = attn + x_buf[slot].astype(f32)
        own_buf[slot] = dot(a, w_proj[:, at_cols(me, width)]) + layer_in[at_rows(r), :]
        store_own(r).start()
        centre = hidden - jnp.sum(hidden, axis=1, keepdims=True) * (1.0 / features)
        spread = jnp.sum(centre * centre, axis=1, keepdims=True) * (1.0 / features)
        scale = lax.rsqrt(spread + eps)
        centred = centre * scale
        low = (centred * gain[...] + shift[...]).astype(bf16)
        z = dot(low, w_expand[...]) + bias[...]
        z2 = z * z
        t = jnp.tanh(z * (GELU_C + (GELU_C * 0.044715) * z2))
        half = 0.5 + 0.5 * t
        activated = (z * half).astype(bf16)
        slope = half + (0.5 * z) * (1.0 - t * t) * (GELU_C + (3.0 * GELU_C * 0.044715) * z2)
        g_gather.arrive(r)
        g = g_buf[at_rows(r), :]
        gp = slope * dot(g, w_reduce[...])
        gp_low = gp.astype(bf16)
        gn = dot(gp_low, w_expand[...], NT)
        scaled = gn * gain[...]
        mean_scaled = jnp.sum(scaled, axis=1, keepdims=True) * (1.0 / features)
        mean_both = jnp.sum(scaled * centred, axis=1, keepdims=True) * (1.0 / features)
        back = (scaled - mean_scaled - centred * mean_both) * scale
        back_low = (back + 0.25 * g.astype(f32)).astype(bf16)
        hid_buf[slot] = back_low
        store_hid(r).start()
        gh_buf[slot] = dot(back_low, w_proj[...], NT).astype(bf16)
        scatter.start(r)
        sums[0:1, :] += jnp.sum(gn * centred, axis=0, keepdims=True)
        sums[1:2, :] += jnp.sum(gn, axis=0, keepdims=True)
        grad_bias[...] += jnp.sum(gp_low.astype(f32), axis=0, keepdims=True)
        ffn_buf[slot] = dot(activated, w_reduce[...], NT).astype(bf16)
        store_ffn(r).start()
        wide[...] += dot(low, gp_low, TN)
        narrow[...] += dot(g, activated, TN)
        scatter.middle(r)
        proj[...] += dot(back_low, a, TN)

        @pl.when(r >= 1)
        def _():
            grad_heads[at_rows(r - 1), :] = scatter.finish(r - 1).astype(bf16)

        return 0

    lax.fori_loop(0, n, body, 0)
    for k, (full, buf, out) in enumerate(
        ((wide, ffn_buf, wide_out), (narrow, x_buf, narrow_out), (proj, hid_buf, proj_out))
    ):
        for p in range(2):
            if buf is ffn_buf:
                store_ffn(n - 2 + p).wait()
            if buf is hid_buf:
                store_hid(n - 2 + p).wait()
            half = features // 2
            slot = (n - 2 + p) % 2
            buf[slot] = full[slot * half : (slot + 1) * half, :].astype(bf16)
            final(k, slot, buf, out).start()
    grad_heads[at_rows(n - 1), :] = scatter.finish(n - 1).astype(bf16)
    for k, (buf, out) in enumerate(((ffn_buf, wide_out), (x_buf, narrow_out), (hid_buf, proj_out))):
        for slot in range(2):
            final(k, slot, buf, out).wait()

    def settle(r, _):
        g_gather.sent(r)

        @pl.when(r >= n - 2)
        def _():
            store_own(r).wait()

        return 0

    lax.fori_loop(0, n, settle, 0)


def second(x, a, grad_out, layer_in, w_proj, w_expand, w_reduce, gain, shift, bias):
    rows, width = layer_in.shape
    features = 4 * width
    units = w_expand.shape[1]
    block = SHORT
    n = rows // block
    any_spec = pl.BlockSpec(memory_space=pl.ANY)
    vmem = pl.BlockSpec(memory_space=pltpu.VMEM)
    return pl.pallas_call(
        second_kernel,
        in_specs=[any_spec] * 2 + [vmem] * 8,
        out_specs=[vmem] + [any_spec] * 6 + [vmem] * 3,
        out_shape=[
            jax.ShapeDtypeStruct((rows, width), bf16),
            jax.ShapeDtypeStruct((rows, features), bf16),
            jax.ShapeDtypeStruct((rows, features), bf16),
            jax.ShapeDtypeStruct((rows, width), f32),
            jax.ShapeDtypeStruct((features, units), bf16),
            jax.ShapeDtypeStruct((features, units), bf16),
            jax.ShapeDtypeStruct((features, features), bf16),
            jax.ShapeDtypeStruct((2, features), f32),
            jax.ShapeDtypeStruct((1, units), f32),
            jax.ShapeDtypeStruct((1, width), f32),
        ],
        scratch_shapes=[
            pltpu.VMEM((rows, features), bf16),
            pltpu.VMEM((2, block, features), bf16),
            pltpu.VMEM((2, block, features), bf16),
            pltpu.VMEM((2, block, features), bf16),
            pltpu.VMEM((2, block, width), f32),
            pltpu.VMEM((2, block, features), bf16),
            pltpu.VMEM((2, block, features), bf16),
            pltpu.VMEM((rows, 2 * width), bf16),
            pltpu.VMEM((2, block, width), bf16),
            pltpu.VMEM((2, block, width), f32),
            pltpu.VMEM((rows, width), bf16),
            pltpu.VMEM((features, units), f32),
            pltpu.VMEM((features, units), f32),
            pltpu.VMEM((features, features), f32),
            pltpu.SemaphoreType.DMA((6, n)),
            pltpu.SemaphoreType.DMA((6, n)),
            pltpu.SemaphoreType.DMA((5, n)),
            pltpu.SemaphoreType.DMA((3, 2)),
        ],
        compiler_params=pltpu.CompilerParams(
            vmem_limit_bytes=62 * MIB, collective_id=1, has_side_effects=True
        ),
    )(x, a, grad_out, layer_in, w_proj, w_expand, w_reduce, gain, shift, bias)


class DpScatter:
    def __init__(self, part, recv_buf, masks, send, recv):
        self.part, self.recv_buf, self.masks = part, recv_buf, masks
        self.group = lax.axis_index("dp")
        self.send, self.recv = send, recv
        size = 1 << len(masks)
        left, at = list(range(size)), 0
        self.plan = []
        for mask in masks:
            mine = [k for k in left if not k & mask]
            self.plan.append((mask, [(k, at + p) for p, k in enumerate(mine)]))
            at += len(mine)
            left = mine

    def where(self, k):
        who = self.group
        for mask in self.masks:
            if k & mask:
                who = partner(who, mask)
        return self.part(who)

    def copy(self, mask, k, slot):
        return send_to(
            self.where(k ^ mask), self.recv_buf.at[slot], self.send.at[slot], self.recv.at[slot],
            dp=partner(self.group, mask),
        )

    def start(self, step):
        mask, items = self.plan[step]
        for k, slot in items:
            self.copy(mask, k, slot).start()

    def arrive(self, step):
        mask, items = self.plan[step]
        for k, slot in items:
            self.copy(mask, k, slot).wait_recv()
            ref = self.where(k)
            ref[...] = (ref[...].astype(f32) + self.recv_buf[slot].astype(f32)).astype(bf16)

    def sent(self):
        for mask, items in self.plan:
            for k, slot in items:
                self.copy(mask, k, slot).wait_send()


class DpSpread:
    def __init__(self, own, slot_of, masks, send, recv):
        self.own, self.slot_of = own, slot_of
        self.masks = list(reversed(masks))
        self.group = lax.axis_index("dp")
        self.send, self.recv = send, recv
        held, self.plan, at = [0], [], 0
        for mask in self.masks:
            self.plan.append((mask, [(k, at + p) for p, k in enumerate(held)]))
            at += len(held)
            held = held + [k ^ mask for k in held]

    def block(self, k):
        who = self.group
        for mask in self.masks:
            if k & mask:
                who = partner(who, mask)
        return self.slot_of(who)

    def copies(self, step, there):
        mask, items = self.plan[step]
        out = []
        for k, sem in items:
            if there:
                src, at = (self.own if k == 0 else self.block(k)), self.block(k)
            else:
                src = at = self.block(k ^ mask)
            out.append(
                send_to(src, at, self.send.at[sem], self.recv.at[sem], dp=partner(self.group, mask))
            )
        return out

    def start(self, step):
        for copy in self.copies(step, True):
            copy.start()

    def arrive(self, step):
        for copy in self.copies(step, False):
            copy.wait_recv()

    def sent(self):
        for step in range(len(self.plan)):
            for copy in self.copies(step, True):
                copy.wait_send()


class DpSum:
    def __init__(self, buf, recv_buf, out, masks, sems, keep_sem):
        size = 1 << len(masks)
        rows = buf.shape[0] // size
        self.steps = len(masks)
        self.scatter = DpScatter(lambda k: buf.at[at_rows(k, rows), :], recv_buf, masks, sems.at[0], sems.at[1])
        me = lax.axis_index("dp")
        own = buf.at[at_rows(me, rows), :]
        self.keep = pltpu.make_async_copy(own, out.at[at_rows(me, rows), :], keep_sem)
        self.spread = DpSpread(own, lambda k: out.at[at_rows(k, rows), :], masks, sems.at[2], sems.at[3])

    def start(self):
        self.scatter.start(0)

    def advance(self, step):
        if step < self.steps:
            self.scatter.arrive(step)
            if step + 1 < self.steps:
                self.scatter.start(step + 1)
            else:
                self.keep.start()
                self.spread.start(0)
        else:
            self.spread.arrive(step - self.steps)
            if step + 1 < 2 * self.steps:
                self.spread.start(step - self.steps + 1)

    def settle(self):
        self.scatter.sent()
        self.spread.sent()
        self.keep.wait()


class HeadSum:
    def __init__(self, width, src, mine, from_core, far, from_chip, sems):
        self.width, self.src, self.mine = width, src, mine
        self.from_core, self.far, self.from_chip, self.sems = from_core, far, from_chip, sems
        self.me = lax.axis_index("head")
        self.core, self.chip = partner(self.me, 1), partner(self.me, 2)

    def to_core(self, r, k):
        who = self.core if k == 0 else partner(self.core, 2)
        return send_to(
            self.src(r).at[:, at_cols(who, self.width)],
            self.from_core.at[at_rows(r), k * self.width : (k + 1) * self.width],
            self.sems.at[2 * k, r],
            self.sems.at[2 * k + 1, r],
            head=self.core,
        )

    def to_chip(self, r):
        return send_to(
            self.far(r), self.from_chip.at[at_rows(r), :], self.sems.at[4, r], self.sems.at[5, r], head=self.chip
        )

    def start(self, r):
        self.to_core(r, 1).start()
        self.to_core(r, 0).start()

    def middle(self, r):
        self.to_core(r, 1).wait()
        self.far(r)[...] = (
            self.mine(r, self.chip, 1) + self.from_core[at_rows(r), self.width :].astype(f32)
        ).astype(bf16)
        self.to_chip(r).start()
        self.to_core(r, 0).wait()
        return self.mine(r, self.me, 0) + self.from_core[at_rows(r), : self.width].astype(f32)

    def finish(self, r):
        self.to_chip(r).wait()
        return self.from_chip[at_rows(r), :].astype(f32)


def third_kernel(
    masks, scatter_inside,
    kind, qkv, grad_heads, logsum, wq, wk, wv, gain, sums_2, grad_bias, grad_bias_reduce, wide, narrow,
    a_in, x_in, normed_in, grad_hid, ffn, proj,
    ffn_sum, total_sum, sum_a, sum_b, wide_sum, narrow_sum, small,
    dqkv, dk_acc, dv_acc, dq_acc, delta, wgrad, slots, pay_a, pay_b, recv_a, recv_b, recv_w, recv_n,
    s_core, s_far, s_chip, s_near, s_mine, s_out, f_src, f_core, f_far, f_chip, small_recv,
    wg_sems, s_sems, mine_sems, out_sems, f_sems, a_sems, b_sems, w_sems, n_sems, slot_sems, keep_sems, small_sems, total_sems,
):
    rows = qkv.shape[0]
    width = grad_heads.shape[1]
    features = x_in.shape[1]
    block = SHORT
    n = rows // block
    heads = width // HEAD_DIM
    me = lax.axis_index("head")
    group = lax.axis_index("dp")
    steps = len(masks)
    greet(masks)

    if scatter_inside:
        local = wide_sum.shape[1]
        wide_rs = DpScatter(lambda k: wide.at[:, at_cols(k, local)], recv_w, masks, w_sems.at[0], w_sems.at[1])
        narrow_rs = DpScatter(lambda k: narrow.at[:, at_cols(k, local)], recv_n, masks, n_sems.at[0], n_sems.at[1])
        wide_rs.start(0)
        narrow_rs.start(0)

    n_proj = features // block
    n_side = n_proj + n

    def side_src(c):
        return proj.at[at_rows(c), :] if c < n_proj else ffn.at[at_rows(c - n_proj), :]

    def side_load(c, k):
        who = me if k == 0 else partner(me, 2)
        return pltpu.make_async_copy(
            side_src(c).at[:, at_cols(who, width)], s_mine.at[c % 2, k], mine_sems.at[k, c]
        )

    def side_mine(c, who, k):
        side_load(c, k).wait()
        return s_mine[c % 2, k].astype(f32)

    side = HeadSum(width, side_src, side_mine, s_core, lambda c: s_far.at[c % 3], s_chip, s_sems)

    def side_copy(c):
        return pltpu.make_async_copy(s_out.at[c % 2], ffn_sum.at[at_rows(c - n_proj), :], out_sems.at[c])

    def side_start(c):
        side_load(c, 1).start()
        side_load(c, 0).start()
        side.start(c)

    def side_finish(c):
        value = (s_near[c % 3] + side.finish(c)).astype(bf16)
        if c < n_proj:
            pay_a[c * block : (c + 1) * block, 3 * HEAD_DIM :] = value
        else:
            if c - 2 >= n_proj:
                side_copy(c - 2).wait()
            s_out[c % 2] = value
            side_copy(c).start()

    def side_step(c):
        if c < n_side:
            s_near[c % 3] = side.middle(c)
            if c + 2 < n_side:
                side_start(c + 2)
        if 0 <= c - 2 < n_side:
            side_finish(c - 2)

    side_start(0)
    side_start(1)

    apart = (1 - kind[0]).astype(f32) * masked_value
    slopes = [s * LOG2E for s in head_slopes(me, heads)]
    two = 2 * block
    pairs = rows // two
    attended = pltpu.make_async_copy(a_in.at[:, at_cols(me, width)], dqkv.at[:, 0:width], wg_sems.at[2])
    attended.start()
    attended.wait()

    def fill(i, _):
        for h in range(heads):
            cols = slice(h * HEAD_DIM, (h + 1) * HEAD_DIM)
            both = grad_heads[at_rows(i), cols].astype(f32) * dqkv[at_rows(i), cols].astype(f32)
            delta[i, h : h + 1, :] = jnp.sum(both.T, axis=0, keepdims=True)
        return 0

    lax.fori_loop(0, n, fill, 0)

    def load_normed(h, m):
        at = (h * pairs + pairs - 1 - m) % 2
        return [
            pltpu.make_async_copy(
                normed_in.at[at_rows(2 * m + p), :], slots.at[2 * at + p], slot_sems.at[2 * at + p]
            )
            for p in range(2)
        ]

    for copy in load_normed(0, pairs - 1):
        copy.start()

    key_place = lax.broadcasted_iota(jnp.int32, (block, two), 0)
    query_place = lax.broadcasted_iota(jnp.int32, (block, two), 1)

    def head_cols(h, k):
        return pl.ds(pl.multiple_of(k * width + h * HEAD_DIM, HEAD_DIM), HEAD_DIM)

    def sweep(h, service):
        own_cols = pl.ds(pl.multiple_of(h * HEAD_DIM, HEAD_DIM), HEAD_DIM)
        slope = slopes[h]
        dk_acc[...] = jnp.zeros_like(dk_acc)
        dv_acc[...] = jnp.zeros_like(dv_acc)

        def tile(m, j, single):
            q_size = block if single else two
            start = 2 * m + 1 if single else 2 * m
            at = pl.ds(pl.multiple_of(start * block, block), q_size)
            q = qkv[at, head_cols(h, 0)]
            g = grad_heads[at, own_cols]
            k = qkv[at_rows(j), head_cols(h, 1)]
            v = qkv[at_rows(j), head_cols(h, 2)]
            keys, queries = key_place[:, :q_size], query_place[:, :q_size]
            if single:
                place = keys.astype(f32) * slope
                allowed = keys <= queries
                lse, dlt = logsum[start, h : h + 1, :], delta[start, h : h + 1, :]
            else:
                second = (queries >= block).astype(jnp.int32)
                offset = (j - start) * block
                place = (keys + offset - second * block).astype(f32) * slope
                allowed = keys + offset <= queries
                place += jnp.where(second + start == j, 0.0, apart)
                lse = jnp.concatenate([logsum[start, h : h + 1, :], logsum[start + 1, h : h + 1, :]], 1)
                dlt = jnp.concatenate([delta[start, h : h + 1, :], delta[start + 1, h : h + 1, :]], 1)
            s = dot(k, q, NT) * (SCALE * LOG2E) + place
            p = jnp.where(allowed, jnp.exp2(s - lse), 0.0)
            ds = (p * (dot(v, g, NT) - dlt)).astype(bf16)
            dv_acc[at_rows(j), :] += dot(p.astype(bf16), g)
            dk_acc[at_rows(j), :] += dot(ds, q)
            if single:
                dq_acc[:, block:] += dot(k, ds, TN)
            else:
                dq_acc[...] += dot(k, ds, TN)

        def outer(step, _):
            m = pairs - 1 - step
            dq_acc[...] = jnp.zeros_like(dq_acc)

            def inner(j, _):
                service(step, j)
                tile(m, j, False)
                return 0

            lax.fori_loop(0, 2 * m + 1, inner, 0)
            tile(m, 2 * m + 1, True)
            for copy in load_normed(h, m):
                copy.wait()

            @pl.when(step + 1 < pairs)
            def _():
                for copy in load_normed(h, m - 1):
                    copy.start()

            if h + 1 < heads:
                @pl.when(step + 1 == pairs)
                def _():
                    for copy in load_normed(h + 1, pairs - 1):
                        copy.start()

            at = pl.ds(pl.multiple_of(m * two, two), two)
            dq = (dq_acc[...] * SCALE).T.astype(bf16)
            dk = (dk_acc[at, :] * SCALE).astype(bf16)
            dv = dv_acc[at, :].astype(bf16)
            dqkv[at, head_cols(h, 0)] = dq
            dqkv[at, head_cols(h, 1)] = dk
            dqkv[at, head_cols(h, 2)] = dv
            slot = (h * pairs + step) % 2
            low = jnp.concatenate([slots[2 * slot], slots[2 * slot + 1]], 0)
            part = dot(low, jnp.concatenate([dq, dk, dv], 1), TN)

            @pl.when(step == 0)
            def _():
                wgrad[...] = part

            @pl.when(step > 0)
            def _():
                wgrad[...] += part

            return 0

        lax.fori_loop(0, pairs, outer, 0)

    todo = {}

    def tiles_of():
        return [(step, j) for step in range(pairs) for j in range(2 * (pairs - 1 - step) + 1)]

    places = [(h, step, j) for h in range(heads) for step, j in tiles_of()]
    spread_out = len(places) / (n_side + 2.0)
    for c in range(n_side + 2):
        at = min(int((c + 0.7) * spread_out), len(places) - 1)
        todo.setdefault(places[at], []).append(functools.partial(side_step, c))
    if scatter_inside:
        for s in range(steps - 1):
            for scatter, share in ((wide_rs, 0.45 + 0.25 * s), (narrow_rs, 0.72 + 0.2 * s)):
                def go(scatter=scatter, s=s):
                    scatter.arrive(s)
                    scatter.start(s + 1)

                at = min(int(share * len(places)), len(places) - 1)
                todo.setdefault(places[at], []).append(go)

    def service_of(h):
        def service(step, j):
            for (hh, at_step, at_j), actions in todo.items():
                if hh == h:
                    @pl.when((step == at_step) & (j == at_j))
                    def _(actions=actions):
                        for action in actions:
                            action()

        return service

    first_sum = DpSum(pay_a, recv_a, sum_a, masks, a_sems, keep_sems.at[0])
    second_sum = DpSum(pay_b, recv_b, sum_b, masks, b_sems, keep_sems.at[1])
    sweep(0, service_of(0))
    pay_a[:, 0 : 3 * HEAD_DIM] = wgrad[...].astype(bf16)
    first_sum.start()
    sweep(1, service_of(1))
    pay_b[...] = wgrad[...].astype(bf16)
    second_sum.start()

    def load_x(q):
        return pltpu.make_async_copy(x_in.at[at_rows(n - 1 - q), :], slots.at[q % 2], total_sems.at[0, q])

    def load_hid(q):
        return pltpu.make_async_copy(grad_hid.at[at_rows(n - 1 - q), :], slots.at[2 + q % 2], total_sems.at[1, q])

    def last_mine(q, who, k):
        return f_src[q % 2, :, at_cols(who, width)].astype(f32)

    last = HeadSum(width, lambda q: f_src.at[q % 2], last_mine, f_core, lambda q: f_far.at[at_rows(q), :], f_chip, f_sems)

    def last_copy(q):
        return pltpu.make_async_copy(
            dqkv.at[at_rows(n - 1 - q), 0:width], total_sum.at[at_rows(n - 1 - q), :], total_sems.at[2, q]
        )

    load_x(0).start()
    load_hid(0).start()
    small[...] = jnp.zeros_like(small)
    small[0:2, :] = sums_2[...]
    small[4:5, 0:grad_bias.shape[1]] = grad_bias[...]
    small[5:6, 0:width] = grad_bias_reduce[...]

    def last_chunk(q, _):
        load_x(q).wait()
        load_hid(q).wait()

        @pl.when(q + 1 < n)
        def _():
            load_x(q + 1).start()
            load_hid(q + 1).start()

        at = at_rows(n - 1 - q)
        gf = dot(dqkv[at, 0:width], wq[...], NT)
        gf += dot(dqkv[at, width : 2 * width], wk[...], NT)
        gf += dot(dqkv[at, 2 * width :], wv[...], NT)
        x = slots[q % 2].astype(f32)
        centre = x - jnp.sum(x, axis=1, keepdims=True) * (1.0 / features)
        spread = jnp.sum(centre * centre, axis=1, keepdims=True) * (1.0 / features)
        scale = lax.rsqrt(spread + eps)
        centred = centre * scale
        scaled = gf * gain[...]
        mean_scaled = jnp.sum(scaled, axis=1, keepdims=True) * (1.0 / features)
        mean_both = jnp.sum(scaled * centred, axis=1, keepdims=True) * (1.0 / features)
        back = (scaled - mean_scaled - centred * mean_both) * scale
        f_src[q % 2] = (back + slots[2 + q % 2].astype(f32)).astype(bf16)
        last.start(q)
        small[2:3, :] += jnp.sum(gf * centred, axis=0, keepdims=True)
        small[3:4, :] += jnp.sum(gf, axis=0, keepdims=True)
        near = last.middle(q)
        dk_acc[at_rows(q), :] = near[:, 0:HEAD_DIM]
        dv_acc[at_rows(q), :] = near[:, HEAD_DIM:]
        return 0

    half = n // 2
    lax.fori_loop(0, half, last_chunk, 0)
    if scatter_inside:
        wide_rs.arrive(steps - 1)
        wide_sum[...] = wide[:, at_cols(group, local)].astype(f32)
    first_sum.advance(0)
    lax.fori_loop(half, n, last_chunk, 0)
    if scatter_inside:
        narrow_rs.arrive(steps - 1)
        narrow_sum[...] = narrow[:, at_cols(group, local)].astype(f32)

    def small_copy(s):
        where = {"head": partner(me, masks_of(4)[s])} if s < 2 else {"dp": partner(group, masks[s - 2])}
        return send_to(small, small_recv.at[s], small_sems.at[0, s], small_sems.at[1, s], **where)

    def small_step(s):
        small_copy(s).wait()
        if s < 2:
            small[0:4, :] += small_recv[s, 0:4, :]
        else:
            small[...] += small_recv[s]
        if s + 1 < 2 + steps:
            small_copy(s + 1).start()

    def last_finish(q):
        far = last.finish(q)
        at = at_rows(n - 1 - q)
        dqkv[at, 0:HEAD_DIM] = (dk_acc[at_rows(q), :] + far[:, 0:HEAD_DIM]).astype(bf16)
        dqkv[at, HEAD_DIM:width] = (dv_acc[at_rows(q), :] + far[:, HEAD_DIM:]).astype(bf16)
        last_copy(q).start()

    small_copy(0).start()
    for s in range(2 * steps):
        second_sum.advance(s)
        if s + 1 < 2 * steps:
            first_sum.advance(s + 1)
        if s < n:
            last_finish(s)
        if s < 2 + steps:
            small_step(s)
    for s in range(2 * steps, max(n, 2 + steps)):
        if s < n:
            last_finish(s)
        if s < 2 + steps:
            small_step(s)
    first_sum.settle()
    second_sum.settle()
    if scatter_inside:
        wide_rs.sent()
        narrow_rs.sent()
    for c in range(n_side - 2, n_side):
        side_copy(c).wait()
    for q in range(n):
        last_copy(q).wait()


def third(
    kind, qkv, grad_heads, logsum, wq, wk, wv, gain, sums_2, grad_bias, grad_bias_reduce, wide, narrow,
    a, x, normed, grad_hid, ffn, proj, local, dp_size,
):
    rows, width = grad_heads.shape
    features = x.shape[1]
    block = SHORT
    n = rows // block
    heads = width // HEAD_DIM
    masks = masks_of(dp_size)
    inside = local % 128 == 0
    home = local if inside else 128
    any_spec = pl.BlockSpec(memory_space=pl.ANY)
    vmem = pl.BlockSpec(memory_space=pltpu.VMEM)
    blocks = max(dp_size - 1, 1)
    n_side = features // block + n
    cols_a, cols_b = 3 * HEAD_DIM + width, 3 * HEAD_DIM
    part = features // dp_size
    recv_blocks = blocks if inside else 1

    def dma(*shape):
        return pltpu.SemaphoreType.DMA(shape)

    return pl.pallas_call(
        functools.partial(third_kernel, masks, inside),
        in_specs=[pl.BlockSpec(memory_space=pltpu.SMEM)] + [vmem] * 12 + [any_spec] * 6,
        out_specs=[any_spec] * 4 + [vmem] * 3,
        out_shape=[
            jax.ShapeDtypeStruct((rows, width), bf16),
            jax.ShapeDtypeStruct((rows, width), bf16),
            jax.ShapeDtypeStruct((features, cols_a), bf16),
            jax.ShapeDtypeStruct((features, cols_b), bf16),
            jax.ShapeDtypeStruct((features, home), f32),
            jax.ShapeDtypeStruct((features, home), f32),
            jax.ShapeDtypeStruct((8, features), f32),
        ],
        scratch_shapes=[
            pltpu.VMEM((rows, 3 * width), bf16),
            pltpu.VMEM((rows, HEAD_DIM), f32),
            pltpu.VMEM((rows, HEAD_DIM), f32),
            pltpu.VMEM((HEAD_DIM, 2 * block), f32),
            pltpu.VMEM((n, heads, block), f32),
            pltpu.VMEM((features, cols_b), f32),
            pltpu.VMEM((4, block, features), bf16),
            pltpu.VMEM((features, cols_a), bf16),
            pltpu.VMEM((features, cols_b), bf16),
            pltpu.VMEM((blocks, part, cols_a), bf16),
            pltpu.VMEM((blocks, part, cols_b), bf16),
            pltpu.VMEM((recv_blocks, features, home), bf16),
            pltpu.VMEM((recv_blocks, features, home), bf16),
            pltpu.VMEM((n_side * block, 2 * width), bf16),
            pltpu.VMEM((3, block, width), bf16),
            pltpu.VMEM((n_side * block, width), bf16),
            pltpu.VMEM((3, block, width), f32),
            pltpu.VMEM((2, 2, block, width), bf16),
            pltpu.VMEM((2, block, width), bf16),
            pltpu.VMEM((2, block, features), bf16),
            pltpu.VMEM((rows, 2 * width), bf16),
            pltpu.VMEM((rows, width), bf16),
            pltpu.VMEM((rows, width), bf16),
            pltpu.VMEM((2 + len(masks), 8, features), f32),
            dma(3),
            dma(6, n_side),
            dma(2, n_side),
            dma(n_side),
            dma(6, n),
            dma(4, blocks),
            dma(4, blocks),
            dma(2, blocks),
            dma(2, blocks),
            dma(4),
            dma(2),
            dma(2, 2 + len(masks)),
            dma(3, n),
        ],
        compiler_params=pltpu.CompilerParams(
            vmem_limit_bytes=63 * MIB, collective_id=2, has_side_effects=True
        ),
    )(
        kind, qkv, grad_heads, logsum, wq, wk, wv, gain, sums_2, grad_bias, grad_bias_reduce, wide, narrow,
        a, x, normed, grad_hid, ffn, proj,
    )


def shards(
    dp_size,
    layer_in,
    bucket,
    w_query,
    w_key,
    w_value,
    w_proj,
    attn_gain,
    attn_shift,
    ffn_gain,
    ffn_shift,
    w_expand,
    bias_expand,
    w_reduce,
    bias_reduce,
    grad_out,
):
    group = lax.axis_index("dp")
    width = layer_in.shape[1]
    local = w_expand.shape[1]
    gain_1 = attn_gain[None]
    x, a, normed, qkv, proj, expand, reduce, bias, logsum = first(
        bucket, layer_in, w_query, w_key, w_value, gain_1, attn_shift[None], bias_expand, w_proj, w_expand, w_reduce, dp_size
    )
    (
        grad_heads, grad_hid, ffn, hid_own, grad_wide, grad_narrow, proj_part, sums_2, grad_bias, grad_bias_reduce,
    ) = second(
        x, a, grad_out, layer_in, proj, expand, reduce, ffn_gain[None], ffn_shift[None], bias
    )
    ffn_sum, grad_in, sum_a, sum_b, grad_expand, grad_reduce, small = third(
        bucket, qkv, grad_heads, logsum, w_query, w_key, w_value, gain_1, sums_2, grad_bias, grad_bias_reduce,
        grad_wide, grad_narrow, a, x, normed, grad_hid, ffn, proj_part, local, dp_size,
    )
    if local % 128:
        grad_expand = lax.psum_scatter(grad_wide.astype(f32), "dp", scatter_dimension=1, tiled=True)
        grad_reduce = lax.psum_scatter(grad_narrow.astype(f32), "dp", scatter_dimension=1, tiled=True)
    layer_out = hid_own + bias_reduce + ffn_sum.astype(f32)
    head = HEAD_DIM
    grad_query, grad_key, grad_value = (
        jnp.concatenate([sum_a[:, k * head : (k + 1) * head], sum_b[:, k * head : (k + 1) * head]], 1).astype(f32)
        for k in range(3)
    )
    grad_proj = sum_a[:, 3 * head :].astype(f32).T
    return (
        layer_out,
        grad_in.astype(f32),
        grad_query,
        grad_key,
        grad_value,
        grad_proj,
        small[2],
        small[3],
        small[0],
        small[1],
        grad_expand,
        lax.dynamic_slice(small, (4, group * local), (1, local)),
        grad_reduce,
        small[5, :width],
    )


def solution(mesh):
    placed = (
        P("dp", "head"),
        P("dp"),
        P(None, "head"),
        P(None, "head"),
        P(None, "head"),
        P("head", None),
        P(),
        P(),
        P(),
        P(),
        P(None, ("dp", "head")),
        P(None, ("dp", "head")),
        P(None, ("dp", "head")),
        P("head"),
        P("dp", "head"),
    )
    return jax.shard_map(
        functools.partial(shards, mesh.shape["dp"]),
        mesh=mesh,
        in_specs=placed,
        out_specs=(
            P("dp", "head"),
            P("dp", "head"),
            P(None, "head"),
            P(None, "head"),
            P(None, "head"),
            P("head", None),
            P(),
            P(),
            P(),
            P(),
            P(None, ("dp", "head")),
            P(None, ("dp", "head")),
            P(None, ("dp", "head")),
            P("head"),
        ),
        check_vma=False,
    )
```

```python
import functools

import jax
import jax.numpy as jnp
from jax import lax
from jax.experimental import pallas as pl
from jax.experimental.pallas import tpu as pltpu
from jax.sharding import PartitionSpec as P

HEADS = 8
HEAD_DIM = 128
SHORT = 512
eps = 1e-05
masked_value = -1e30
LOG2E = 1.4426950408889634
LN2 = 0.6931471805599453
SCALE = HEAD_DIM ** (-0.5)
MIB = 1024 * 1024
f32 = jnp.float32
bf16 = jnp.bfloat16

NN = (((1,), (0,)), ((), ()))
NT = (((1,), (1,)), ((), ()))
TN = (((0,), (0,)), ((), ()))


def dot(left, right, dims=NN):
    return lax.dot_general(left, right, dims, preferred_element_type=f32)


def full_spec(shape):
    return pl.BlockSpec(shape, lambda *_: (0,) * len(shape))


MESH = pl.DeviceIdType.MESH


def partner(index, mask):
    return index + mask - 2 * mask * ((index // mask) % 2)


def masks_of(size):
    return [1 << k for k in range(size.bit_length() - 1)]


def send_to(src, dst, send, recv, **where):
    return pltpu.make_async_remote_copy(
        src_ref=src, dst_ref=dst, send_sem=send, recv_sem=recv, device_id=where, device_id_type=MESH
    )


def greet(dp_masks):
    me, group = lax.axis_index("head"), lax.axis_index("dp")
    barrier = pltpu.get_barrier_semaphore()
    for mask in (1, 2):
        pl.semaphore_signal(
            barrier, inc=1, device_id={"head": partner(me, mask)}, device_id_type=MESH
        )
    for mask in dp_masks:
        pl.semaphore_signal(
            barrier, inc=1, device_id={"dp": partner(group, mask)}, device_id_type=MESH
        )
    pl.semaphore_wait(barrier, 2 + len(dp_masks))


def at_rows(r, block=SHORT):
    return pl.ds(pl.multiple_of(r * block, block), block)


def at_cols(k, width):
    return pl.ds(pl.multiple_of(k * width, width), width)


class HeadGather:
    def __init__(self, own, full, width, sems):
        self.own, self.full, self.width = own, full, width
        self.me = lax.axis_index("head")
        self.core, self.chip = partner(self.me, 1), partner(self.me, 2)
        self.far = partner(self.core, 2)
        self.sems = sems

    def slot(self, r, who):
        return self.full.at[at_rows(r), at_cols(who, self.width)]

    def copy(self, r, src, owner, kind, **where):
        return send_to(
            src, self.slot(r, owner), self.sems.at[2 * kind, r], self.sems.at[2 * kind + 1, r], **where
        )

    def own_src(self, r):
        return self.own(r) if self.own is not None else self.slot(r, self.me)

    def start(self, r):
        self.copy(r, self.own_src(r), self.me, 0, head=self.chip).start()
        self.copy(r, self.own_src(r), self.me, 1, head=self.core).start()

    def forward(self, r):
        self.copy(r, self.slot(r, self.chip), self.chip, 0, head=self.chip).wait_recv()
        self.copy(r, self.slot(r, self.chip), self.chip, 2, head=self.core).start()

    def arrive(self, r):
        self.copy(r, self.slot(r, self.core), self.core, 1, head=self.core).wait_recv()
        self.copy(r, self.slot(r, self.far), self.far, 2, head=self.core).wait_recv()

    def sent(self, r):
        self.copy(r, self.own_src(r), self.me, 0, head=self.chip).wait_send()
        self.copy(r, self.own_src(r), self.me, 1, head=self.core).wait_send()
        self.copy(r, self.slot(r, self.chip), self.chip, 2, head=self.core).wait_send()


class DpSpread:
    def __init__(self, own, slot_of, masks, send, recv):
        self.own, self.slot_of, self.masks = own, slot_of, masks
        self.group = lax.axis_index("dp")
        self.send, self.recv = send, recv
        held, self.plan, at = [0], [], 0
        for mask in self.masks:
            self.plan.append((mask, [(k, at + p) for p, k in enumerate(held)]))
            at += len(held)
            held = held + [k ^ mask for k in held]

    def block(self, k):
        who = self.group
        for mask in self.masks:
            if k & mask:
                who = partner(who, mask)
        return self.slot_of(who)

    def copies(self, step, there):
        mask, items = self.plan[step]
        out = []
        for k, sem in items:
            if there:
                src, at = (self.own if k == 0 else self.block(k)), self.block(k)
            else:
                src = at = self.block(k ^ mask)
            out.append(
                send_to(src, at, self.send.at[sem], self.recv.at[sem], dp=partner(self.group, mask))
            )
        return out

    def start(self, step):
        for copy in self.copies(step, True):
            copy.start()

    def arrive(self, step):
        for copy in self.copies(step, False):
            copy.wait_recv()

    def sent(self):
        for step in range(len(self.plan)):
            for copy in self.copies(step, True):
                copy.wait_send()


def head_slopes(me, heads, n_head=4):
    slopes = []
    for h in range(heads):
        value = jnp.float32(0.0)
        for k in range(n_head):
            value = jnp.where(me == k, jnp.float32(2.0 ** (-8.0 * (k * heads + h + 1) / HEADS)), value)
        slopes.append(value)
    return slopes


def first_kernel(
    masks, gather,
    kind, layer_in, wq, wk, wv, gain, shift, bias_expand, w_proj, w_expand, w_reduce,
    x_out, a_out, normed_out, qkv_out, proj_out, expand_out, reduce_out, bias_out, logsum,
    x_buf, normed_buf, qkv_buf, a_buf, bias_buf, total, x_sems, a_sems, p_sems, local_sems, copy_sems,
    e_send, e_recv, r_send, r_recv, b_send, b_recv, q_send, q_recv,
):
    rows, width = layer_in.shape
    features = 4 * width
    block = SHORT
    n = rows // block
    heads = width // HEAD_DIM
    me, group = lax.axis_index("head"), lax.axis_index("dp")
    core, chip = partner(me, 1), partner(me, 2)
    greet(masks if gather else [])

    x_gather = HeadGather(None, x_buf, width, x_sems)
    a_gather = HeadGather(lambda r: a_buf.at[at_rows(r), :], a_out, width, a_sems)

    def p_copy(src, owner, k, **where):
        return send_to(src, proj_out.at[at_cols(owner, width), :], p_sems.at[2 * k], p_sems.at[2 * k + 1], **where)

    piece = width // (1 << len(masks))

    def p_rows(owner, k):
        return proj_out.at[pl.ds(pl.multiple_of(owner * width + k * piece, piece), piece), :]

    def p_piece(owner, to):
        return send_to(
            w_proj.at[pl.ds(pl.multiple_of(group * piece, piece), piece), :], p_rows(owner, group),
            p_sems.at[0], p_sems.at[1], head=to,
        )

    far_rows = DpSpread(p_rows(chip, group), lambda k: p_rows(chip, k), masks[::-1], q_send, q_recv)

    if gather:
        bias_buf[...] = jnp.broadcast_to(bias_expand[...], bias_buf.shape)

        def columns_of(ref):
            return lambda k: ref.at[:, at_cols(k, w_expand.shape[1])]

        far_first, near_first = masks[::-1], masks[:1] + masks[1:][::-1]
        expand = DpSpread(w_expand, columns_of(expand_out), far_first, e_send, e_recv)
        bias = DpSpread(bias_buf, columns_of(bias_out), far_first, b_send, b_recv)
        reduce = DpSpread(w_reduce, columns_of(reduce_out), near_first, r_send, r_recv)
        expand.start(0)
        bias.start(0)
        reduce.start(0)

    def own_chunk(r):
        x_buf[at_rows(r), at_cols(me, width)] = layer_in[at_rows(r), :].astype(bf16)
        x_gather.start(r)

    if gather:
        p_piece(me, chip).start()
        p_copy(w_proj, me, 1, head=core).start()
    own_chunk(0)
    own_chunk(1)
    own_chunk(2)
    keeps = [pltpu.make_async_copy(w_proj, proj_out.at[at_cols(me, width), :], local_sems.at[0])]
    if gather:
        own_cols = at_cols(group, w_expand.shape[1])
        keeps.append(pltpu.make_async_copy(w_expand, expand_out.at[:, own_cols], local_sems.at[1]))
        keeps.append(pltpu.make_async_copy(w_reduce, reduce_out.at[:, own_cols], local_sems.at[2]))
        keeps.append(pltpu.make_async_copy(bias_buf, bias_out.at[:, own_cols], local_sems.at[3]))
    for keep in keeps:
        keep.start()

    slopes = [s * LOG2E for s in head_slopes(me, heads)]
    apart = (1 - kind[0]).astype(f32) * masked_value
    key_place = lax.broadcasted_iota(jnp.int32, (block, block), 0)
    query_place = lax.broadcasted_iota(jnp.int32, (block, block), 1)

    def normed_copy(r):
        return pltpu.make_async_copy(normed_buf.at[r % 2], normed_out.at[at_rows(r), :], copy_sems.at[0, r])

    def x_copy(r):
        return pltpu.make_async_copy(x_buf.at[at_rows(r), :], x_out.at[at_rows(r), :], copy_sems.at[1, r])

    def qkv_copy(r):
        return pltpu.make_async_copy(qkv_buf.at[at_rows(r), :], qkv_out.at[at_rows(r), :], copy_sems.at[2, r])

    def a_copy(r):
        return pltpu.make_async_copy(
            a_buf.at[at_rows(r), :], a_out.at[at_rows(r), at_cols(me, width)], copy_sems.at[3, r]
        )

    def chunk(i):
        x_gather.arrive(i)
        x_copy(i).start()
        x = x_buf[at_rows(i), :].astype(f32)
        centre = x - jnp.sum(x, axis=1, keepdims=True) * (1.0 / features)
        spread = jnp.sum(centre * centre, axis=1, keepdims=True) * (1.0 / features)
        low = (centre * lax.rsqrt(spread + eps) * gain[...] + shift[...]).astype(bf16)

        @pl.when(i >= 2)
        def _():
            normed_copy(i - 2).wait()

        normed_buf[i % 2] = low
        normed_copy(i).start()
        for k, w in enumerate((wq, wk, wv)):
            qkv_buf[at_rows(i), k * width : (k + 1) * width] = dot(low, w[...]).astype(bf16)
        qkv_copy(i).start()

        def scores(h, j):
            q = qkv_buf[at_rows(i), h * HEAD_DIM : (h + 1) * HEAD_DIM]
            k = qkv_buf[at_rows(j), width + h * HEAD_DIM : width + (h + 1) * HEAD_DIM]
            v = qkv_buf[at_rows(j), 2 * width + h * HEAD_DIM : 2 * width + (h + 1) * HEAD_DIM]
            place = (key_place + (j - i) * block).astype(f32) * slopes[h]
            return dot(k, q, NT) * (SCALE * LOG2E) + place, v

        carry = []
        for h in range(heads):
            s, v = scores(h, i)
            s = jnp.where(key_place <= query_place, s, masked_value)
            m = jnp.max(s, axis=0, keepdims=True)
            p = jnp.exp2(s - m)
            carry += [m, jnp.sum(p, axis=0, keepdims=True)]
            total[h] = dot(v, p.astype(bf16), TN)

        def step(j, carry):
            new = []
            for h in range(heads):
                m, l = carry[2 * h], carry[2 * h + 1]
                s, v = scores(h, j)
                s = s + apart
                m_new = jnp.maximum(m, jnp.max(s, axis=0, keepdims=True))
                p = jnp.exp2(s - m_new)
                fade = jnp.exp2(m - m_new)
                new += [m_new, l * fade + jnp.sum(p, axis=0, keepdims=True)]
                total[h] = total[h] * fade + dot(v, p.astype(bf16), TN)
            return tuple(new)

        carry = lax.fori_loop(0, i, step, tuple(carry))
        for h in range(heads):
            m, l = carry[2 * h], carry[2 * h + 1]
            a_buf[at_rows(i), h * HEAD_DIM : (h + 1) * HEAD_DIM] = (total[h] * (1.0 / l)).T.astype(bf16)
            logsum[i, h : h + 1, :] = m + jnp.log(l) * LOG2E
        a_gather.start(i)
        a_copy(i).start()

    steps = len(masks)

    def body(r, _):
        @pl.when(r < n)
        def _():
            x_gather.forward(r)

            @pl.when(r + 3 < n)
            def _():
                own_chunk(r + 3)

            if not gather:
                @pl.when(r + 2 == n)
                def _():
                    p_copy(w_proj, me, 0, head=chip).start()
                    p_copy(w_proj, me, 1, head=core).start()

        if gather:
            @pl.when(r == 2)
            def _():
                p_piece(chip, chip).wait_recv()
                far_rows.start(0)

            for s in range(1, steps):
                @pl.when(r == min(s + 3, n))
                def _(s=s):
                    far_rows.arrive(s - 1)
                    far_rows.start(s)

                @pl.when(r == min(2 * s + 1, n - 1))
                def _(s=s):
                    expand.arrive(s - 1)
                    bias.arrive(s - 1)
                    expand.start(s)
                    bias.start(s)

                @pl.when(r == min(4 * s - 3, n))
                def _(s=s):
                    reduce.arrive(s - 1)
                    reduce.start(s)

        @pl.when(r >= 1)
        def _():
            chunk(r - 1)

        return 0

    lax.fori_loop(0, n + 1, body, 0)

    if gather:
        far_rows.arrive(steps - 1)
    else:
        p_copy(w_proj, chip, 0, head=chip).wait_recv()
    p_forward = p_copy(proj_out.at[at_cols(chip, width), :], chip, 2, head=core)
    p_forward.start()

    def pass_on(r, _):
        a_gather.forward(r)
        return 0

    lax.fori_loop(0, n, pass_on, 0)

    def settle(r, _):
        a_gather.arrive(r)
        a_gather.sent(r)
        x_gather.sent(r)
        x_copy(r).wait()
        qkv_copy(r).wait()
        a_copy(r).wait()

        @pl.when(r >= n - 2)
        def _():
            normed_copy(r).wait()

        return 0

    lax.fori_loop(0, n, settle, 0)
    p_copy(w_proj, core, 1, head=core).wait_recv()
    p_copy(w_proj, partner(core, 2), 2, head=core).wait_recv()
    if gather:
        p_piece(me, chip).wait_send()
        far_rows.sent()
    else:
        p_copy(w_proj, me, 0, head=chip).wait_send()
    p_copy(w_proj, me, 1, head=core).wait_send()
    p_forward.wait_send()
    for keep in keeps:
        keep.wait()
    if gather:
        expand.arrive(steps - 1)
        reduce.arrive(steps - 1)
        bias.arrive(steps - 1)
        expand.sent()
        reduce.sent()
        bias.sent()


def first(kind, layer_in, wq, wk, wv, gain, shift, bias_expand, w_proj, w_expand, w_reduce, dp_size):
    rows, width = layer_in.shape
    features = 4 * width
    block = SHORT
    n = rows // block
    heads = width // HEAD_DIM
    masks = masks_of(dp_size)
    local = w_expand.shape[1]
    gather = local % 128 == 0 and (width // dp_size) % 16 == 0
    units = local * dp_size if gather else 128
    any_spec = pl.BlockSpec(memory_space=pl.ANY)
    vmem = pl.BlockSpec(memory_space=pltpu.VMEM)
    blocks = max(dp_size - 1, 1)
    outs = pl.pallas_call(
        functools.partial(first_kernel, masks, gather),
        in_specs=[pl.BlockSpec(memory_space=pltpu.SMEM)] + [vmem] * 7 + [any_spec] * 3,
        out_specs=[any_spec] * 8 + [vmem],
        out_shape=[
            jax.ShapeDtypeStruct((rows, features), bf16),
            jax.ShapeDtypeStruct((rows, features), bf16),
            jax.ShapeDtypeStruct((rows, features), bf16),
            jax.ShapeDtypeStruct((rows, 3 * width), bf16),
            jax.ShapeDtypeStruct((features, features), bf16),
            jax.ShapeDtypeStruct((features, units), bf16),
            jax.ShapeDtypeStruct((features, units), bf16),
            jax.ShapeDtypeStruct((16, units), bf16),
            jax.ShapeDtypeStruct((n, heads, block), f32),
        ],
        scratch_shapes=[
            pltpu.VMEM((rows, features), bf16),
            pltpu.VMEM((2, block, features), bf16),
            pltpu.VMEM((rows, 3 * width), bf16),
            pltpu.VMEM((rows, width), bf16),
            pltpu.VMEM((16, local), bf16),
            pltpu.VMEM((heads, HEAD_DIM, block), f32),
            pltpu.SemaphoreType.DMA((6, n)),
            pltpu.SemaphoreType.DMA((6, n)),
            pltpu.SemaphoreType.DMA((6,)),
            pltpu.SemaphoreType.DMA((4,)),
            pltpu.SemaphoreType.DMA((4, n)),
        ]
        + [pltpu.SemaphoreType.DMA((blocks,))] * 8,
        compiler_params=pltpu.CompilerParams(
            vmem_limit_bytes=56 * MIB, collective_id=0, has_side_effects=True
        ),
    )(kind, layer_in, wq, wk, wv, gain, shift, bias_expand, w_proj, w_expand, w_reduce)
    x, a, normed, qkv, proj, expand, reduce, bias, logsum = outs
    bias = bias[:1]
    if not gather:
        bias = lax.all_gather(bias_expand, "dp", axis=1, tiled=True)
        expand = lax.all_gather(w_expand, "dp", axis=1, tiled=True)
        reduce = lax.all_gather(w_reduce, "dp", axis=1, tiled=True)
    return x, a, normed, qkv, proj, expand, reduce, bias.astype(f32), logsum


class HeadScatter:
    def __init__(self, width, src, from_core, far, near, from_chip, sems):
        self.width, self.src, self.from_core, self.far = width, src, from_core, far
        self.near, self.from_chip, self.sems = near, from_chip, sems
        self.me = lax.axis_index("head")
        self.core, self.chip = partner(self.me, 1), partner(self.me, 2)

    def to_core(self, r, k):
        who = self.core if k == 0 else partner(self.core, 2)
        return send_to(
            self.src(r).at[:, at_cols(who, self.width)],
            self.from_core.at[at_rows(r), k * self.width : (k + 1) * self.width],
            self.sems.at[2 * k, r],
            self.sems.at[2 * k + 1, r],
            head=self.core,
        )

    def to_chip(self, r):
        return send_to(
            self.far.at[r % 2],
            self.from_chip.at[at_rows(r), :],
            self.sems.at[4, r],
            self.sems.at[5, r],
            head=self.chip,
        )

    def start(self, r):
        self.to_core(r, 1).start()
        self.to_core(r, 0).start()

    def middle(self, r):
        src = self.src(r)
        self.to_core(r, 1).wait()
        self.far[r % 2] = (
            src[:, at_cols(self.chip, self.width)].astype(f32)
            + self.from_core[at_rows(r), self.width :].astype(f32)
        ).astype(bf16)
        self.to_chip(r).start()
        self.to_core(r, 0).wait()
        self.near[r % 2] = (
            src[:, at_cols(self.me, self.width)].astype(f32)
            + self.from_core[at_rows(r), : self.width].astype(f32)
        )

    def finish(self, r):
        self.to_chip(r).wait()
        return self.near[r % 2] + self.from_chip[at_rows(r), :].astype(f32)


GELU_C = 0.7978845608028654


def second_kernel(
    x_in, a_in, layer_in, w_proj_in, w_expand_in, w_reduce_in, grad_out, gain, shift, bias,
    grad_heads, grad_hid_out, ffn_out, hid_own, wide_out, narrow_out, proj_out, sums, grad_bias, grad_bias_reduce,
    g_buf, x_buf, a_buf, hid_buf, own_buf, ffn_buf, gh_buf, from_core, far_buf, near_buf, from_chip, wide, narrow, proj,
    w_proj, w_expand, w_reduce, in_buf, g_sems, s_sems, copy_sems, final_sems, load_sems,
):
    rows, width = layer_in.shape
    features = 4 * width
    block = SHORT
    n = rows // block
    me = lax.axis_index("head")
    greet([])

    g_gather = HeadGather(None, g_buf, width, g_sems)
    scatter = HeadScatter(width, lambda r: gh_buf.at[r % 2], from_core, far_buf, near_buf, from_chip, s_sems)

    def own_chunk(r):
        chunk = grad_out[at_rows(r), :]
        g_buf[at_rows(r), at_cols(me, width)] = chunk.astype(bf16)
        g_gather.start(r)
        return chunk

    loads = [
        pltpu.make_async_copy(src, dst, load_sems.at[k])
        for k, (src, dst) in enumerate(
            ((w_proj_in, w_proj), (w_expand_in, w_expand), (w_reduce_in, w_reduce))
        )
    ]

    def load_in(r):
        return pltpu.make_async_copy(layer_in.at[at_rows(r), :], in_buf.at[r % 2], copy_sems.at[5, r])

    def load_x(r):
        return pltpu.make_async_copy(x_in.at[at_rows(r), :], x_buf.at[r % 2], copy_sems.at[0, r])

    def load_a(r):
        return pltpu.make_async_copy(a_in.at[at_rows(r), :], a_buf.at[r % 2], copy_sems.at[1, r])

    def store_hid(r):
        return pltpu.make_async_copy(hid_buf.at[r % 2], grad_hid_out.at[at_rows(r), :], copy_sems.at[2, r])

    def store_ffn(r):
        return pltpu.make_async_copy(ffn_buf.at[r % 2], ffn_out.at[at_rows(r), :], copy_sems.at[3, r])

    def store_own(r):
        return pltpu.make_async_copy(own_buf.at[r % 2], hid_own.at[at_rows(r), :], copy_sems.at[4, r])

    def final(k, slot, buf, out):
        half = features // 2
        return pltpu.make_async_copy(
            buf.at[slot], out.at[slot * half : (slot + 1) * half, :], final_sems.at[k, slot]
        )

    own_chunk(0)
    own_chunk(1)
    load_a(0).start()
    loads[0].start()
    load_x(0).start()
    load_in(0).start()
    loads[1].start()
    loads[2].start()
    wide[...] = jnp.zeros_like(wide)
    narrow[...] = jnp.zeros_like(narrow)
    proj[...] = jnp.zeros_like(proj)
    sums[...] = jnp.zeros_like(sums)
    grad_bias[...] = jnp.zeros_like(grad_bias)
    grad_bias_reduce[...] = jnp.sum(grad_out[...], axis=0, keepdims=True)

    def body(r, _):
        g_gather.forward(r)

        @pl.when(r + 2 < n)
        def _():
            own_chunk(r + 2)

        load_x(r).wait()
        load_a(r).wait()
        load_in(r).wait()

        @pl.when(r == 0)
        def _():
            loads[0].wait()

        @pl.when(r + 1 < n)
        def _():
            load_x(r + 1).start()
            load_a(r + 1).start()
            load_in(r + 1).start()

        @pl.when(r >= 2)
        def _():
            store_hid(r - 2).wait()
            store_ffn(r - 2).wait()
            store_own(r - 2).wait()

        slot = r % 2
        a = a_buf[slot]
        attn = dot(a, w_proj[...])
        hidden = attn + x_buf[slot].astype(f32)
        own_buf[slot] = dot(a, w_proj[:, at_cols(me, width)]) + in_buf[slot]
        store_own(r).start()
        centre = hidden - jnp.sum(hidden, axis=1, keepdims=True) * (1.0 / features)
        spread = jnp.sum(centre * centre, axis=1, keepdims=True) * (1.0 / features)
        scale = lax.rsqrt(spread + eps)
        centred = centre * scale
        low = (centred * gain[...] + shift[...]).astype(bf16)

        @pl.when(r == 0)
        def _():
            loads[1].wait()
            loads[2].wait()

        z = dot(low, w_expand[...]) + bias[...]
        z2 = z * z
        t = jnp.tanh(z * (GELU_C + (GELU_C * 0.044715) * z2))
        half = 0.5 + 0.5 * t
        activated = (z * half).astype(bf16)
        slope = half + (0.5 * z) * (1.0 - t * t) * (GELU_C + (3.0 * GELU_C * 0.044715) * z2)
        g_gather.arrive(r)
        g = g_buf[at_rows(r), :]
        gp = slope * dot(g, w_reduce[...])
        gp_low = gp.astype(bf16)
        gn = dot(gp_low, w_expand[...], NT)
        scaled = gn * gain[...]
        mean_scaled = jnp.sum(scaled, axis=1, keepdims=True) * (1.0 / features)
        mean_both = jnp.sum(scaled * centred, axis=1, keepdims=True) * (1.0 / features)
        back = (scaled - mean_scaled - centred * mean_both) * scale
        back_low = (back + 0.25 * g.astype(f32)).astype(bf16)
        hid_buf[slot] = back_low
        store_hid(r).start()
        gh_buf[slot] = dot(back_low, w_proj[...], NT).astype(bf16)
        scatter.start(r)
        sums[0:1, :] += jnp.sum(gn * centred, axis=0, keepdims=True)
        sums[1:2, :] += jnp.sum(gn, axis=0, keepdims=True)
        grad_bias[...] += jnp.sum(gp_low.astype(f32), axis=0, keepdims=True)
        ffn_buf[slot] = dot(activated, w_reduce[...], NT).astype(bf16)
        store_ffn(r).start()
        wide[...] += dot(low, gp_low, TN)
        scatter.middle(r)
        narrow[...] += dot(g, activated, TN)
        proj[...] += dot(back_low, a, TN)

        @pl.when(r >= 1)
        def _():
            grad_heads[at_rows(r - 1), :] = scatter.finish(r - 1).astype(bf16)

        return 0

    lax.fori_loop(0, n, body, 0)
    for k, (full, buf, out) in enumerate(
        ((wide, ffn_buf, wide_out), (narrow, x_buf, narrow_out), (proj, hid_buf, proj_out))
    ):
        for p in range(2):
            if buf is ffn_buf:
                store_ffn(n - 2 + p).wait()
            if buf is hid_buf:
                store_hid(n - 2 + p).wait()
            half = features // 2
            slot = (n - 2 + p) % 2
            buf[slot] = full[slot * half : (slot + 1) * half, :].astype(bf16)
            final(k, slot, buf, out).start()
    grad_heads[at_rows(n - 1), :] = scatter.finish(n - 1).astype(bf16)
    for k, (buf, out) in enumerate(((ffn_buf, wide_out), (x_buf, narrow_out), (hid_buf, proj_out))):
        for slot in range(2):
            final(k, slot, buf, out).wait()

    def settle(r, _):
        g_gather.sent(r)

        @pl.when(r >= n - 2)
        def _():
            store_own(r).wait()

        return 0

    lax.fori_loop(0, n, settle, 0)


def second(x, a, grad_out, layer_in, w_proj, w_expand, w_reduce, gain, shift, bias):
    rows, width = layer_in.shape
    features = 4 * width
    units = w_expand.shape[1]
    block = SHORT
    n = rows // block
    any_spec = pl.BlockSpec(memory_space=pl.ANY)
    vmem = pl.BlockSpec(memory_space=pltpu.VMEM)
    return pl.pallas_call(
        second_kernel,
        in_specs=[any_spec] * 6 + [vmem] * 4,
        out_specs=[vmem] + [any_spec] * 6 + [vmem] * 3,
        out_shape=[
            jax.ShapeDtypeStruct((rows, width), bf16),
            jax.ShapeDtypeStruct((rows, features), bf16),
            jax.ShapeDtypeStruct((rows, features), bf16),
            jax.ShapeDtypeStruct((rows, width), f32),
            jax.ShapeDtypeStruct((features, units), bf16),
            jax.ShapeDtypeStruct((features, units), bf16),
            jax.ShapeDtypeStruct((features, features), bf16),
            jax.ShapeDtypeStruct((2, features), f32),
            jax.ShapeDtypeStruct((1, units), f32),
            jax.ShapeDtypeStruct((1, width), f32),
        ],
        scratch_shapes=[
            pltpu.VMEM((rows, features), bf16),
            pltpu.VMEM((2, block, features), bf16),
            pltpu.VMEM((2, block, features), bf16),
            pltpu.VMEM((2, block, features), bf16),
            pltpu.VMEM((2, block, width), f32),
            pltpu.VMEM((2, block, features), bf16),
            pltpu.VMEM((2, block, features), bf16),
            pltpu.VMEM((rows, 2 * width), bf16),
            pltpu.VMEM((2, block, width), bf16),
            pltpu.VMEM((2, block, width), f32),
            pltpu.VMEM((rows, width), bf16),
            pltpu.VMEM((features, units), f32),
            pltpu.VMEM((features, units), f32),
            pltpu.VMEM((features, features), f32),
            pltpu.VMEM((features, features), bf16),
            pltpu.VMEM((features, units), bf16),
            pltpu.VMEM((features, units), bf16),
            pltpu.VMEM((2, block, width), f32),
            pltpu.SemaphoreType.DMA((6, n)),
            pltpu.SemaphoreType.DMA((6, n)),
            pltpu.SemaphoreType.DMA((6, n)),
            pltpu.SemaphoreType.DMA((3, 2)),
            pltpu.SemaphoreType.DMA((3,)),
        ],
        compiler_params=pltpu.CompilerParams(
            vmem_limit_bytes=62 * MIB, collective_id=1, has_side_effects=True
        ),
    )(x, a, layer_in, w_proj, w_expand, w_reduce, grad_out, gain, shift, bias)


class DpScatter:
    def __init__(self, part, recv_buf, masks, send, recv, first_part=None):
        self.part, self.recv_buf, self.masks = part, recv_buf, masks
        self.first_part = first_part or part
        self.group = lax.axis_index("dp")
        self.send, self.recv = send, recv
        size = 1 << len(masks)
        left, at = list(range(size)), 0
        self.plan = []
        for mask in masks:
            mine = [k for k in left if not k & mask]
            self.plan.append((mask, [(k, at + p) for p, k in enumerate(mine)]))
            at += len(mine)
            left = mine

    def where(self, k, part):
        who = self.group
        for mask in self.masks:
            if k & mask:
                who = partner(who, mask)
        return part(who)

    def copy(self, mask, k, slot):
        part = self.first_part if mask == self.masks[0] else self.part
        return send_to(
            self.where(k ^ mask, part), self.recv_buf.at[slot], self.send.at[slot], self.recv.at[slot],
            dp=partner(self.group, mask),
        )

    def start(self, step):
        mask, items = self.plan[step]
        for k, slot in items:
            self.copy(mask, k, slot).start()

    def arrive(self, step):
        mask, items = self.plan[step]
        for k, slot in items:
            self.copy(mask, k, slot).wait_recv()
            ref = self.where(k, self.part)
            ref[...] = (ref[...].astype(f32) + self.recv_buf[slot].astype(f32)).astype(bf16)

    def sent(self):
        for mask, items in self.plan:
            for k, slot in items:
                self.copy(mask, k, slot).wait_send()


class DpSum:
    def __init__(self, buf, recv_buf, out, masks, sems, keep_sem):
        size = 1 << len(masks)
        rows = buf.shape[0] // size
        self.steps = len(masks)
        self.scatter = DpScatter(lambda k: buf.at[at_rows(k, rows), :], recv_buf, masks, sems.at[0], sems.at[1])
        me = lax.axis_index("dp")
        own = buf.at[at_rows(me, rows), :]
        self.keep = pltpu.make_async_copy(own, out.at[at_rows(me, rows), :], keep_sem)
        self.spread = DpSpread(
            own, lambda k: out.at[at_rows(k, rows), :], masks[::-1], sems.at[2], sems.at[3]
        )

    def start(self):
        self.scatter.start(0)

    def advance(self, step):
        if step < self.steps:
            self.scatter.arrive(step)
            if step + 1 < self.steps:
                self.scatter.start(step + 1)
            else:
                self.keep.start()
                self.spread.start(0)
        else:
            self.spread.arrive(step - self.steps)
            if step + 1 < 2 * self.steps:
                self.spread.start(step - self.steps + 1)

    def settle(self):
        self.scatter.sent()
        self.spread.sent()
        self.keep.wait()


class HeadSum:
    def __init__(self, width, src, mine, from_core, far, from_chip, sems):
        self.width, self.src, self.mine = width, src, mine
        self.from_core, self.far, self.from_chip, self.sems = from_core, far, from_chip, sems
        self.me = lax.axis_index("head")
        self.core, self.chip = partner(self.me, 1), partner(self.me, 2)

    def to_core(self, r, k):
        who = self.core if k == 0 else partner(self.core, 2)
        return send_to(
            self.src(r).at[:, at_cols(who, self.width)],
            self.from_core.at[at_rows(r), k * self.width : (k + 1) * self.width],
            self.sems.at[2 * k, r],
            self.sems.at[2 * k + 1, r],
            head=self.core,
        )

    def to_chip(self, r):
        return send_to(
            self.far(r), self.from_chip.at[at_rows(r), :], self.sems.at[4, r], self.sems.at[5, r], head=self.chip
        )

    def start(self, r):
        self.to_core(r, 1).start()
        self.to_core(r, 0).start()

    def middle(self, r):
        self.to_core(r, 1).wait()
        self.far(r)[...] = (
            self.mine(r, self.chip, 1) + self.from_core[at_rows(r), self.width :].astype(f32)
        ).astype(bf16)
        self.to_chip(r).start()
        self.to_core(r, 0).wait()
        return self.mine(r, self.me, 0) + self.from_core[at_rows(r), : self.width].astype(f32)

    def finish(self, r):
        self.to_chip(r).wait()
        return self.from_chip[at_rows(r), :].astype(f32)


def third_kernel(
    masks, scatter_inside,
    kind, qkv, grad_heads, logsum, wq, wk, wv, gain, sums_2, grad_bias, grad_bias_reduce,
    wide_in, narrow_in, a_in, x_in, normed_in, grad_hid, ffn, proj,
    ffn_sum, total_sum, sum_p, sum_a, sum_b, wide_sum, narrow_sum, small,
    dqkv, dk_acc, dv_acc, dq_acc, delta, wgrad, slots, wide, narrow, pay_p, pay_a, pay_b,
    recv_p, recv_a, recv_b, recv_w, recv_n,
    s_core, s_far, s_chip, s_near, s_mine, s_out, f_src, f_core, f_far, f_chip, small_recv,
    wg_sems, s_sems, mine_sems, out_sems, f_sems, p_sems, a_sems, b_sems, w_sems, n_sems, slot_sems, keep_sems, small_sems, total_sems,
):
    rows = qkv.shape[0]
    width = grad_heads.shape[1]
    features = x_in.shape[1]
    block = SHORT
    n = rows // block
    heads = width // HEAD_DIM
    me = lax.axis_index("head")
    group = lax.axis_index("dp")
    steps = len(masks)
    greet(masks)

    agenda = []

    def due(time, action, *args):
        agenda.append((time, len(agenda), functools.partial(action, *args)))

    turned = masks[1:2] + masks[:1] + masks[2:]

    if scatter_inside:
        local = wide_sum.shape[1]

        def columns_of(ref):
            return lambda k: ref.at[:, at_cols(k, local)]

        wide_rs = DpScatter(columns_of(wide), recv_w, masks, w_sems.at[0], w_sems.at[1], columns_of(wide_in))
        narrow_rs = DpScatter(columns_of(narrow), recv_n, turned, n_sems.at[0], n_sems.at[1], columns_of(narrow_in))
        wide_rs.start(0)
        narrow_rs.start(0)
        loads = [
            pltpu.make_async_copy(wide_in, wide, keep_sems.at[3]),
            pltpu.make_async_copy(narrow_in, narrow, keep_sems.at[4]),
        ]

        def scatter_step(scatter, load, out, s):
            if s == 0:
                load.wait()
            scatter.arrive(s)
            if s + 1 < steps:
                scatter.start(s + 1)
            else:
                out[...] = scatter.part(group)[...].astype(f32)

        for s in range(steps):
            due((63, 70.5, 85)[min(s, 2)] + max(s - 2, 0), scatter_step, wide_rs, loads[0], wide_sum, s)
            due((28.5, 51.5, 66)[min(s, 2)] + max(s - 2, 0), scatter_step, narrow_rs, loads[1], narrow_sum, s)

    n_proj = features // block
    n_side = n_proj + n

    def side_src(c):
        return proj.at[at_rows(c), :] if c < n_proj else ffn.at[at_rows(c - n_proj), :]

    def side_load(c, k):
        who = me if k == 0 else partner(me, 2)
        return pltpu.make_async_copy(
            side_src(c).at[:, at_cols(who, width)], s_mine.at[c % 2, k], mine_sems.at[k, c]
        )

    def side_mine(c, who, k):
        side_load(c, k).wait()
        return s_mine[c % 2, k].astype(f32)

    side = HeadSum(width, side_src, side_mine, s_core, lambda c: s_far.at[c % 3], s_chip, s_sems)

    def side_copy(c):
        return pltpu.make_async_copy(s_out.at[c % 2], ffn_sum.at[at_rows(c - n_proj), :], out_sems.at[c])

    def side_start(c):
        side_load(c, 1).start()
        side_load(c, 0).start()
        side.start(c)

    def side_finish(c):
        value = (s_near[c % 3] + side.finish(c)).astype(bf16)
        if c < n_proj:
            pay_p[c * block : (c + 1) * block, :] = value
        else:
            if c - 2 >= n_proj:
                side_copy(c - 2).wait()
            s_out[c % 2] = value
            side_copy(c).start()

    def side_step(c):
        if c < n_side:
            s_near[c % 3] = side.middle(c)
            if c + 2 < n_side:
                side_start(c + 2)
        if 0 <= c - 2 < n_side:
            side_finish(c - 2)

    side_start(0)
    side_start(1)
    for c in range(n_side + 2):
        due((4.1, 7.0, 15.6, 23.0, 35.4, 40.5, 47.5, 52.2, 75, 80.5)[min(c, 9)] + max(c - 9, 0), side_step, c)
    if scatter_inside:
        for load in loads:
            load.start()

    proj_sum = DpSum(pay_p, recv_p, sum_p, masks, p_sems, keep_sems.at[0])
    first_sum = DpSum(pay_a, recv_a, sum_a, turned, a_sems, keep_sems.at[1])
    second_sum = DpSum(pay_b, recv_b, sum_b, masks, b_sems, keep_sems.at[2])
    due(25, proj_sum.start)
    for which, times in (
        (proj_sum, (36, 40.5, 45, 57, 63, 81)),
        (first_sum, (41, 48, 60, 66, 77, 100)),
        (second_sum, (59.5, 63, 66, 68, 78, 300)),
    ):
        for s in range(2 * steps):
            due(times[min(s * 3 // steps, 5)] + 0.01 * s, which.advance, s)

    apart = (1 - kind[0]).astype(f32) * masked_value
    slopes = [s * LOG2E for s in head_slopes(me, heads)]
    two = 2 * block
    pairs = rows // two
    attended = pltpu.make_async_copy(a_in.at[:, at_cols(me, width)], dqkv.at[:, 0:width], wg_sems.at[2])
    attended.start()
    attended.wait()

    def fill(i, _):
        for h in range(heads):
            cols = slice(h * HEAD_DIM, (h + 1) * HEAD_DIM)
            both = grad_heads[at_rows(i), cols].astype(f32) * dqkv[at_rows(i), cols].astype(f32)
            delta[i, h : h + 1, :] = jnp.sum(both.T, axis=0, keepdims=True)
        return 0

    lax.fori_loop(0, n, fill, 0)

    def load_normed(h, m):
        at = (h * pairs + pairs - 1 - m) % 2
        return [
            pltpu.make_async_copy(
                normed_in.at[at_rows(2 * m + p), :], slots.at[2 * at + p], slot_sems.at[2 * at + p]
            )
            for p in range(2)
        ]

    for copy in load_normed(0, pairs - 1):
        copy.start()

    key_place = lax.broadcasted_iota(jnp.int32, (block, two), 0)
    query_place = lax.broadcasted_iota(jnp.int32, (block, two), 1)

    def head_cols(h, k):
        return pl.ds(pl.multiple_of(k * width + h * HEAD_DIM, HEAD_DIM), HEAD_DIM)

    def sweep(h, service):
        own_cols = pl.ds(pl.multiple_of(h * HEAD_DIM, HEAD_DIM), HEAD_DIM)
        slope = slopes[h]
        dk_acc[...] = jnp.zeros_like(dk_acc)
        dv_acc[...] = jnp.zeros_like(dv_acc)

        def tile(m, j, single):
            q_size = block if single else two
            start = 2 * m + 1 if single else 2 * m
            at = pl.ds(pl.multiple_of(start * block, block), q_size)
            q = qkv[at, head_cols(h, 0)]
            g = grad_heads[at, own_cols]
            k = qkv[at_rows(j), head_cols(h, 1)]
            v = qkv[at_rows(j), head_cols(h, 2)]
            keys, queries = key_place[:, :q_size], query_place[:, :q_size]
            if single:
                place = keys.astype(f32) * slope
                allowed = keys <= queries
                lse, dlt = logsum[start, h : h + 1, :], delta[start, h : h + 1, :]
            else:
                second = (queries >= block).astype(jnp.int32)
                offset = (j - start) * block
                place = (keys + offset - second * block).astype(f32) * slope
                allowed = keys + offset <= queries
                place += jnp.where(second + start == j, 0.0, apart)
                lse = jnp.concatenate([logsum[start, h : h + 1, :], logsum[start + 1, h : h + 1, :]], 1)
                dlt = jnp.concatenate([delta[start, h : h + 1, :], delta[start + 1, h : h + 1, :]], 1)
            s = dot(k, q, NT) * (SCALE * LOG2E) + place
            p = jnp.where(allowed, jnp.exp2(s - lse), 0.0)
            ds = (p * (dot(v, g, NT) - dlt)).astype(bf16)
            dv_acc[at_rows(j), :] += dot(p.astype(bf16), g)
            dk_acc[at_rows(j), :] += dot(ds, q)
            if single:
                dq_acc[:, block:] += dot(k, ds, TN)
            else:
                dq_acc[...] += dot(k, ds, TN)

        def outer(step, _):
            m = pairs - 1 - step
            dq_acc[...] = jnp.zeros_like(dq_acc)

            def inner(j, _):
                service(step, j)
                tile(m, j, False)
                return 0

            lax.fori_loop(0, 2 * m + 1, inner, 0)
            service(step, 2 * m + 1)
            tile(m, 2 * m + 1, True)
            for copy in load_normed(h, m):
                copy.wait()

            @pl.when(step + 1 < pairs)
            def _():
                for copy in load_normed(h, m - 1):
                    copy.start()

            if h + 1 < heads:
                @pl.when(step + 1 == pairs)
                def _():
                    for copy in load_normed(h + 1, pairs - 1):
                        copy.start()

            at = pl.ds(pl.multiple_of(m * two, two), two)
            dq = (dq_acc[...] * SCALE).T.astype(bf16)
            dk = (dk_acc[at, :] * SCALE).astype(bf16)
            dv = dv_acc[at, :].astype(bf16)
            dqkv[at, head_cols(h, 0)] = dq
            dqkv[at, head_cols(h, 1)] = dk
            dqkv[at, head_cols(h, 2)] = dv
            slot = (h * pairs + step) % 2
            low = jnp.concatenate([slots[2 * slot], slots[2 * slot + 1]], 0)
            part = dot(low, jnp.concatenate([dq, dk, dv], 1), TN)

            @pl.when(step == 0)
            def _():
                wgrad[...] = part

            @pl.when(step > 0)
            def _():
                wgrad[...] += part

            return 0

        lax.fori_loop(0, pairs, outer, 0)

    places, clock = [], 3.0
    for h in range(heads):
        for step in range(pairs):
            tiles = 2 * (pairs - 1 - step) + 2
            for j in range(tiles):
                places.append((clock, h, step, j))
                clock += 1.9 if j + 1 < tiles else 1.1
            clock += 1.6
    finish_clock, finish_time = clock, 2.7

    def events(start, end):
        return [action for time, _, action in sorted(agenda, key=lambda e: e[:2]) if start <= time < end]

    def run(actions):
        for action in actions:
            action()

    def service_of(h):
        def service(step, j):
            for k, (time, at_h, at_step, at_j) in enumerate(places):
                earlier = places[k - 1][0] if k else -1.0
                actions = events(earlier + 1e-6, time + 1e-6)
                if at_h == h and actions:
                    @pl.when((step == at_step) & (j == at_j))
                    def _(actions=actions):
                        run(actions)

        return service

    sweep(0, service_of(0))
    pay_a[...] = wgrad[...].astype(bf16)
    first_sum.start()
    sweep(1, service_of(1))
    pay_b[...] = wgrad[...].astype(bf16)
    second_sum.start()

    def load_x(q):
        return pltpu.make_async_copy(x_in.at[at_rows(n - 1 - q), :], slots.at[q % 2], total_sems.at[0, q])

    def load_hid(q):
        return pltpu.make_async_copy(grad_hid.at[at_rows(n - 1 - q), :], slots.at[2 + q % 2], total_sems.at[1, q])

    def last_mine(q, who, k):
        return f_src[q % 2, :, at_cols(who, width)].astype(f32)

    last = HeadSum(width, lambda q: f_src.at[q % 2], last_mine, f_core, lambda q: f_far.at[at_rows(q), :], f_chip, f_sems)

    def last_copy(q):
        return pltpu.make_async_copy(
            dqkv.at[at_rows(n - 1 - q), 0:width], total_sum.at[at_rows(n - 1 - q), :], total_sems.at[2, q]
        )

    load_x(0).start()
    load_hid(0).start()
    small[...] = jnp.zeros_like(small)
    small[0:2, :] = sums_2[...]
    small[4:5, 0:grad_bias.shape[1]] = grad_bias[...]
    small[5:6, 0:width] = grad_bias_reduce[...]

    def last_middle(q):
        near = last.middle(q)
        dk_acc[at_rows(q), :] = near[:, 0:HEAD_DIM]
        dv_acc[at_rows(q), :] = near[:, HEAD_DIM:]

    def last_chunk(q, _):
        load_x(q).wait()
        load_hid(q).wait()

        @pl.when(q + 1 < n)
        def _():
            load_x(q + 1).start()
            load_hid(q + 1).start()

        at = at_rows(n - 1 - q)
        gf = dot(dqkv[at, 0:width], wq[...], NT)
        gf += dot(dqkv[at, width : 2 * width], wk[...], NT)
        gf += dot(dqkv[at, 2 * width :], wv[...], NT)
        x = slots[q % 2].astype(f32)
        centre = x - jnp.sum(x, axis=1, keepdims=True) * (1.0 / features)
        spread = jnp.sum(centre * centre, axis=1, keepdims=True) * (1.0 / features)
        scale = lax.rsqrt(spread + eps)
        centred = centre * scale
        scaled = gf * gain[...]
        mean_scaled = jnp.sum(scaled, axis=1, keepdims=True) * (1.0 / features)
        mean_both = jnp.sum(scaled * centred, axis=1, keepdims=True) * (1.0 / features)
        back = (scaled - mean_scaled - centred * mean_both) * scale
        f_src[q % 2] = (back + slots[2 + q % 2].astype(f32)).astype(bf16)
        last.start(q)
        small[2:3, :] += jnp.sum(gf * centred, axis=0, keepdims=True)
        small[3:4, :] += jnp.sum(gf, axis=0, keepdims=True)
        @pl.when(q >= 1)
        def _():
            last_middle(q - 1)

        return 0

    done = places[-1][0] + 1e-6

    def last_step(q, _):
        for k in range(n):
            start = done if k == 0 else finish_clock + (k - 1) * finish_time
            actions = events(start, finish_clock + k * finish_time)
            if actions:
                @pl.when(q == k)
                def _(actions=actions):
                    run(actions)

        return last_chunk(q, _)

    lax.fori_loop(0, n, last_step, 0)
    last_middle(n - 1)
    done = finish_clock + (n - 1) * finish_time

    def small_copy(s):
        where = {"head": partner(me, masks_of(4)[s])} if s < 2 else {"dp": partner(group, masks[s - 2])}
        return send_to(small, small_recv.at[s], small_sems.at[0, s], small_sems.at[1, s], **where)

    def small_step(s):
        small_copy(s).wait()
        if s < 2:
            small[0:4, :] += small_recv[s, 0:4, :]
        else:
            small[...] += small_recv[s]
        if s + 1 < 2 + steps:
            small_copy(s + 1).start()

    def last_finish(q):
        far = last.finish(q)
        at = at_rows(n - 1 - q)
        dqkv[at, 0:HEAD_DIM] = (dk_acc[at_rows(q), :] + far[:, 0:HEAD_DIM]).astype(bf16)
        dqkv[at, HEAD_DIM:width] = (dv_acc[at_rows(q), :] + far[:, HEAD_DIM:]).astype(bf16)
        last_copy(q).start()

    small_copy(0).start()
    for s in range(2 + steps):
        due(done + 2.5 * (s + 1), small_step, s)
    for q in range(n):
        due(max(done, finish_clock + 6.1 * (q + 1) + 4.0), last_finish, q)
    run(events(done, 1e9))
    proj_sum.settle()
    first_sum.settle()
    second_sum.settle()
    if scatter_inside:
        wide_rs.sent()
        narrow_rs.sent()
    for c in range(n_side - 2, n_side):
        side_copy(c).wait()
    for q in range(n):
        last_copy(q).wait()


def third(
    kind, qkv, grad_heads, logsum, wq, wk, wv, gain, sums_2, grad_bias, grad_bias_reduce, wide, narrow,
    a, x, normed, grad_hid, ffn, proj, local, dp_size,
):
    rows, width = grad_heads.shape
    features = x.shape[1]
    block = SHORT
    n = rows // block
    heads = width // HEAD_DIM
    masks = masks_of(dp_size)
    inside = local % 128 == 0
    home = local if inside else 128
    any_spec = pl.BlockSpec(memory_space=pl.ANY)
    vmem = pl.BlockSpec(memory_space=pltpu.VMEM)
    blocks = max(dp_size - 1, 1)
    n_side = features // block + n
    cols = 3 * HEAD_DIM
    part = features // dp_size
    recv_blocks = blocks if inside else 1

    def dma(*shape):
        return pltpu.SemaphoreType.DMA(shape)

    return pl.pallas_call(
        functools.partial(third_kernel, masks, inside),
        in_specs=[pl.BlockSpec(memory_space=pltpu.SMEM)] + [vmem] * 10 + [any_spec] * 8,
        out_specs=[any_spec] * 5 + [vmem] * 3,
        out_shape=[
            jax.ShapeDtypeStruct((rows, width), bf16),
            jax.ShapeDtypeStruct((rows, width), bf16),
            jax.ShapeDtypeStruct((features, width), bf16),
            jax.ShapeDtypeStruct((features, cols), bf16),
            jax.ShapeDtypeStruct((features, cols), bf16),
            jax.ShapeDtypeStruct((features, home), f32),
            jax.ShapeDtypeStruct((features, home), f32),
            jax.ShapeDtypeStruct((8, features), f32),
        ],
        scratch_shapes=[
            pltpu.VMEM((rows, 3 * width), bf16),
            pltpu.VMEM((rows, HEAD_DIM), f32),
            pltpu.VMEM((rows, HEAD_DIM), f32),
            pltpu.VMEM((HEAD_DIM, 2 * block), f32),
            pltpu.VMEM((n, heads, block), f32),
            pltpu.VMEM((features, cols), f32),
            pltpu.VMEM((4, block, features), bf16),
            pltpu.VMEM(wide.shape if inside else (16, 128), bf16),
            pltpu.VMEM(narrow.shape if inside else (16, 128), bf16),
            pltpu.VMEM((features, width), bf16),
            pltpu.VMEM((features, cols), bf16),
            pltpu.VMEM((features, cols), bf16),
            pltpu.VMEM((blocks, part, width), bf16),
            pltpu.VMEM((blocks, part, cols), bf16),
            pltpu.VMEM((blocks, part, cols), bf16),
            pltpu.VMEM((recv_blocks, features, home), bf16),
            pltpu.VMEM((recv_blocks, features, home), bf16),
            pltpu.VMEM((n_side * block, 2 * width), bf16),
            pltpu.VMEM((3, block, width), bf16),
            pltpu.VMEM((n_side * block, width), bf16),
            pltpu.VMEM((3, block, width), f32),
            pltpu.VMEM((2, 2, block, width), bf16),
            pltpu.VMEM((2, block, width), bf16),
            pltpu.VMEM((2, block, features), bf16),
            pltpu.VMEM((rows, 2 * width), bf16),
            pltpu.VMEM((rows, width), bf16),
            pltpu.VMEM((rows, width), bf16),
            pltpu.VMEM((2 + len(masks), 8, features), f32),
            dma(3),
            dma(6, n_side),
            dma(2, n_side),
            dma(n_side),
            dma(6, n),
            dma(4, blocks),
            dma(4, blocks),
            dma(4, blocks),
            dma(2, blocks),
            dma(2, blocks),
            dma(4),
            dma(5),
            dma(2, 2 + len(masks)),
            dma(3, n),
        ],
        compiler_params=pltpu.CompilerParams(
            vmem_limit_bytes=63 * MIB, collective_id=2, has_side_effects=True
        ),
    )(
        kind, qkv, grad_heads, logsum, wq, wk, wv, gain, sums_2, grad_bias, grad_bias_reduce, wide, narrow,
        a, x, normed, grad_hid, ffn, proj,
    )


def shards(
    dp_size,
    layer_in,
    bucket,
    w_query,
    w_key,
    w_value,
    w_proj,
    attn_gain,
    attn_shift,
    ffn_gain,
    ffn_shift,
    w_expand,
    bias_expand,
    w_reduce,
    bias_reduce,
    grad_out,
):
    group = lax.axis_index("dp")
    width = layer_in.shape[1]
    local = w_expand.shape[1]
    gain_1 = attn_gain[None]
    x, a, normed, qkv, proj, expand, reduce, bias, logsum = first(
        bucket, layer_in, w_query, w_key, w_value, gain_1, attn_shift[None], bias_expand, w_proj, w_expand, w_reduce, dp_size
    )
    (
        grad_heads, grad_hid, ffn, hid_own, grad_wide, grad_narrow, proj_part, sums_2, grad_bias, grad_bias_reduce,
    ) = second(
        x, a, grad_out, layer_in, proj, expand, reduce, ffn_gain[None], ffn_shift[None], bias
    )
    ffn_sum, grad_in, sum_p, sum_a, sum_b, grad_expand, grad_reduce, small = third(
        bucket, qkv, grad_heads, logsum, w_query, w_key, w_value, gain_1, sums_2, grad_bias, grad_bias_reduce,
        grad_wide, grad_narrow, a, x, normed, grad_hid, ffn, proj_part, local, dp_size,
    )
    if local % 128:
        grad_expand = lax.psum_scatter(grad_wide.astype(f32), "dp", scatter_dimension=1, tiled=True)
        grad_reduce = lax.psum_scatter(grad_narrow.astype(f32), "dp", scatter_dimension=1, tiled=True)
    layer_out = hid_own + bias_reduce + ffn_sum.astype(f32)
    head = HEAD_DIM
    grad_query, grad_key, grad_value = (
        jnp.concatenate([sum_a[:, k * head : (k + 1) * head], sum_b[:, k * head : (k + 1) * head]], 1).astype(f32)
        for k in range(3)
    )
    grad_proj = sum_p.astype(f32).T
    return (
        layer_out,
        grad_in.astype(f32),
        grad_query,
        grad_key,
        grad_value,
        grad_proj,
        small[2],
        small[3],
        small[0],
        small[1],
        grad_expand,
        lax.dynamic_slice(small, (4, group * local), (1, local)),
        grad_reduce,
        small[5, :width],
    )


def solution(mesh):
    placed = (
        P("dp", "head"),
        P("dp"),
        P(None, "head"),
        P(None, "head"),
        P(None, "head"),
        P("head", None),
        P(),
        P(),
        P(),
        P(),
        P(None, ("dp", "head")),
        P(None, ("dp", "head")),
        P(None, ("dp", "head")),
        P("head"),
        P("dp", "head"),
    )
    return jax.shard_map(
        functools.partial(shards, mesh.shape["dp"]),
        mesh=mesh,
        in_specs=placed,
        out_specs=(
            P("dp", "head"),
            P("dp", "head"),
            P(None, "head"),
            P(None, "head"),
            P(None, "head"),
            P("head", None),
            P(),
            P(),
            P(),
            P(),
            P(None, ("dp", "head")),
            P(None, ("dp", "head")),
            P(None, ("dp", "head")),
            P("head"),
        ),
        check_vma=False,
    )
```

```python
import functools

import jax
import jax.numpy as jnp
from jax import lax
from jax.experimental import pallas as pl
from jax.experimental.pallas import tpu as pltpu
from jax.sharding import PartitionSpec as P

HEADS = 8
HEAD_DIM = 128
SHORT = 512
eps = 1e-05
masked_value = -1e30
LOG2E = 1.4426950408889634
LN2 = 0.6931471805599453
SCALE = HEAD_DIM ** (-0.5)
MIB = 1024 * 1024
f32 = jnp.float32
bf16 = jnp.bfloat16

NN = (((1,), (0,)), ((), ()))
NT = (((1,), (1,)), ((), ()))
TN = (((0,), (0,)), ((), ()))


def dot(left, right, dims=NN):
    return lax.dot_general(left, right, dims, preferred_element_type=f32)


def full_spec(shape):
    return pl.BlockSpec(shape, lambda *_: (0,) * len(shape))


MESH = pl.DeviceIdType.MESH


def partner(index, mask):
    return index + mask - 2 * mask * ((index // mask) % 2)


def masks_of(size):
    return [1 << k for k in range(size.bit_length() - 1)]


def send_to(src, dst, send, recv, **where):
    return pltpu.make_async_remote_copy(
        src_ref=src, dst_ref=dst, send_sem=send, recv_sem=recv, device_id=where, device_id_type=MESH
    )


def greet(dp_masks):
    me, group = lax.axis_index("head"), lax.axis_index("dp")
    barrier = pltpu.get_barrier_semaphore()
    for mask in (1, 2):
        pl.semaphore_signal(
            barrier, inc=1, device_id={"head": partner(me, mask)}, device_id_type=MESH
        )
    for mask in dp_masks:
        pl.semaphore_signal(
            barrier, inc=1, device_id={"dp": partner(group, mask)}, device_id_type=MESH
        )
    pl.semaphore_wait(barrier, 2 + len(dp_masks))


def at_rows(r, block=SHORT):
    return pl.ds(pl.multiple_of(r * block, block), block)


def at_cols(k, width):
    return pl.ds(pl.multiple_of(k * width, width), width)


class HeadGather:
    def __init__(self, own, full, width, sems):
        self.own, self.full, self.width = own, full, width
        self.me = lax.axis_index("head")
        self.core, self.chip = partner(self.me, 1), partner(self.me, 2)
        self.far = partner(self.core, 2)
        self.sems = sems

    def slot(self, r, who):
        return self.full.at[at_rows(r), at_cols(who, self.width)]

    def copy(self, r, src, owner, kind, **where):
        return send_to(
            src, self.slot(r, owner), self.sems.at[2 * kind, r], self.sems.at[2 * kind + 1, r], **where
        )

    def own_src(self, r):
        return self.own(r) if self.own is not None else self.slot(r, self.me)

    def start(self, r):
        self.copy(r, self.own_src(r), self.me, 0, head=self.chip).start()
        self.copy(r, self.own_src(r), self.me, 1, head=self.core).start()

    def forward(self, r):
        self.copy(r, self.slot(r, self.chip), self.chip, 0, head=self.chip).wait_recv()
        self.copy(r, self.slot(r, self.chip), self.chip, 2, head=self.core).start()

    def arrive(self, r):
        self.copy(r, self.slot(r, self.core), self.core, 1, head=self.core).wait_recv()
        self.copy(r, self.slot(r, self.far), self.far, 2, head=self.core).wait_recv()

    def sent(self, r):
        self.copy(r, self.own_src(r), self.me, 0, head=self.chip).wait_send()
        self.copy(r, self.own_src(r), self.me, 1, head=self.core).wait_send()
        self.copy(r, self.slot(r, self.chip), self.chip, 2, head=self.core).wait_send()


class DpSpread:
    def __init__(self, own, slot_of, masks, send, recv):
        self.own, self.slot_of, self.masks = own, slot_of, masks
        self.group = lax.axis_index("dp")
        self.send, self.recv = send, recv
        held, self.plan, at = [0], [], 0
        for mask in self.masks:
            self.plan.append((mask, [(k, at + p) for p, k in enumerate(held)]))
            at += len(held)
            held = held + [k ^ mask for k in held]

    def block(self, k):
        who = self.group
        for mask in self.masks:
            if k & mask:
                who = partner(who, mask)
        return self.slot_of(who)

    def copies(self, step, there):
        mask, items = self.plan[step]
        out = []
        for k, sem in items:
            if there:
                src, at = (self.own if k == 0 else self.block(k)), self.block(k)
            else:
                src = at = self.block(k ^ mask)
            out.append(
                send_to(src, at, self.send.at[sem], self.recv.at[sem], dp=partner(self.group, mask))
            )
        return out

    def start(self, step):
        for copy in self.copies(step, True):
            copy.start()

    def arrive(self, step):
        for copy in self.copies(step, False):
            copy.wait_recv()

    def sent(self):
        for step in range(len(self.plan)):
            for copy in self.copies(step, True):
                copy.wait_send()


def head_slopes(me, heads, n_head=4):
    slopes = []
    for h in range(heads):
        value = jnp.float32(0.0)
        for k in range(n_head):
            value = jnp.where(me == k, jnp.float32(2.0 ** (-8.0 * (k * heads + h + 1) / HEADS)), value)
        slopes.append(value)
    return slopes


def first_kernel(
    masks, gather,
    kind, layer_in, wq, wk, wv, gain, shift, bias_expand, w_proj, w_expand, w_reduce,
    x_out, a_out, normed_out, qkv_out, proj_out, expand_out, reduce_out, bias_out, logsum,
    x_buf, normed_buf, qkv_buf, a_buf, bias_buf, total, x_sems, a_sems, p_sems, local_sems, copy_sems,
    e_send, e_recv, r_send, r_recv, b_send, b_recv, q_send, q_recv,
):
    rows, width = layer_in.shape
    features = 4 * width
    block = SHORT
    n = rows // block
    heads = width // HEAD_DIM
    me, group = lax.axis_index("head"), lax.axis_index("dp")
    core, chip = partner(me, 1), partner(me, 2)
    greet(masks if gather else [])

    x_gather = HeadGather(None, x_buf, width, x_sems)
    a_gather = HeadGather(lambda r: a_buf.at[at_rows(r), :], a_out, width, a_sems)

    def p_copy(src, owner, k, **where):
        return send_to(src, proj_out.at[at_cols(owner, width), :], p_sems.at[2 * k], p_sems.at[2 * k + 1], **where)

    piece = width // (1 << len(masks))

    def p_rows(owner, k):
        return proj_out.at[pl.ds(pl.multiple_of(owner * width + k * piece, piece), piece), :]

    def p_piece(owner, to):
        return send_to(
            w_proj.at[pl.ds(pl.multiple_of(group * piece, piece), piece), :], p_rows(owner, group),
            p_sems.at[0], p_sems.at[1], head=to,
        )

    far_rows = DpSpread(p_rows(chip, group), lambda k: p_rows(chip, k), masks[::-1], q_send, q_recv)

    if gather:
        bias_buf[...] = jnp.broadcast_to(bias_expand[...], bias_buf.shape)

        def columns_of(ref):
            return lambda k: ref.at[:, at_cols(k, w_expand.shape[1])]

        far_first, near_first = masks[::-1], masks[:1] + masks[1:][::-1]
        expand = DpSpread(w_expand, columns_of(expand_out), far_first, e_send, e_recv)
        bias = DpSpread(bias_buf, columns_of(bias_out), far_first, b_send, b_recv)
        reduce = DpSpread(w_reduce, columns_of(reduce_out), near_first, r_send, r_recv)
        expand.start(0)
        bias.start(0)
        reduce.start(0)

    def own_chunk(r):
        x_buf[at_rows(r), at_cols(me, width)] = layer_in[at_rows(r), :].astype(bf16)
        x_gather.start(r)

    if gather:
        p_piece(me, chip).start()
        p_copy(w_proj, me, 1, head=core).start()
    own_chunk(0)
    own_chunk(1)
    own_chunk(2)
    keeps = [pltpu.make_async_copy(w_proj, proj_out.at[at_cols(me, width), :], local_sems.at[0])]
    if gather:
        own_cols = at_cols(group, w_expand.shape[1])
        keeps.append(pltpu.make_async_copy(w_expand, expand_out.at[:, own_cols], local_sems.at[1]))
        keeps.append(pltpu.make_async_copy(w_reduce, reduce_out.at[:, own_cols], local_sems.at[2]))
        keeps.append(pltpu.make_async_copy(bias_buf, bias_out.at[:, own_cols], local_sems.at[3]))
    for keep in keeps:
        keep.start()

    slopes = [s * LOG2E for s in head_slopes(me, heads)]
    apart = (1 - kind[0]).astype(f32) * masked_value
    key_place = lax.broadcasted_iota(jnp.int32, (block, block), 0)
    query_place = lax.broadcasted_iota(jnp.int32, (block, block), 1)

    def normed_copy(r):
        return pltpu.make_async_copy(normed_buf.at[r % 2], normed_out.at[at_rows(r), :], copy_sems.at[0, r])

    def x_copy(r):
        return pltpu.make_async_copy(x_buf.at[at_rows(r), :], x_out.at[at_rows(r), :], copy_sems.at[1, r])

    def qkv_copy(r):
        return pltpu.make_async_copy(qkv_buf.at[at_rows(r), :], qkv_out.at[at_rows(r), :], copy_sems.at[2, r])

    def a_copy(r):
        return pltpu.make_async_copy(
            a_buf.at[at_rows(r), :], a_out.at[at_rows(r), at_cols(me, width)], copy_sems.at[3, r]
        )

    def chunk(i):
        x_gather.arrive(i)
        x_copy(i).start()
        x = x_buf[at_rows(i), :].astype(f32)
        centre = x - jnp.sum(x, axis=1, keepdims=True) * (1.0 / features)
        spread = jnp.sum(centre * centre, axis=1, keepdims=True) * (1.0 / features)
        low = (centre * lax.rsqrt(spread + eps) * gain[...] + shift[...]).astype(bf16)

        @pl.when(i >= 2)
        def _():
            normed_copy(i - 2).wait()

        normed_buf[i % 2] = low
        normed_copy(i).start()
        for k, w in enumerate((wq, wk, wv)):
            qkv_buf[at_rows(i), k * width : (k + 1) * width] = dot(low, w[...]).astype(bf16)
        qkv_copy(i).start()

        def scores(h, j):
            q = qkv_buf[at_rows(i), h * HEAD_DIM : (h + 1) * HEAD_DIM]
            k = qkv_buf[at_rows(j), width + h * HEAD_DIM : width + (h + 1) * HEAD_DIM]
            v = qkv_buf[at_rows(j), 2 * width + h * HEAD_DIM : 2 * width + (h + 1) * HEAD_DIM]
            place = (key_place + (j - i) * block).astype(f32) * slopes[h]
            return dot(k, q, NT) * (SCALE * LOG2E) + place, v

        carry = []
        for h in range(heads):
            s, v = scores(h, i)
            s = jnp.where(key_place <= query_place, s, masked_value)
            m = jnp.max(s, axis=0, keepdims=True)
            p = jnp.exp2(s - m)
            carry += [m, jnp.sum(p, axis=0, keepdims=True)]
            total[h] = dot(v, p.astype(bf16), TN)

        def step(j, carry):
            new = []
            for h in range(heads):
                m, l = carry[2 * h], carry[2 * h + 1]
                s, v = scores(h, j)
                s = s + apart
                m_new = jnp.maximum(m, jnp.max(s, axis=0, keepdims=True))
                p = jnp.exp2(s - m_new)
                fade = jnp.exp2(m - m_new)
                new += [m_new, l * fade + jnp.sum(p, axis=0, keepdims=True)]
                total[h] = total[h] * fade + dot(v, p.astype(bf16), TN)
            return tuple(new)

        carry = lax.fori_loop(0, i, step, tuple(carry))
        for h in range(heads):
            m, l = carry[2 * h], carry[2 * h + 1]
            a_buf[at_rows(i), h * HEAD_DIM : (h + 1) * HEAD_DIM] = (total[h] * (1.0 / l)).T.astype(bf16)
            logsum[i, h : h + 1, :] = m + jnp.log(l) * LOG2E
        a_gather.start(i)
        a_copy(i).start()

    steps = len(masks)

    def body(r, _):
        @pl.when(r < n)
        def _():
            x_gather.forward(r)

            @pl.when(r + 3 < n)
            def _():
                own_chunk(r + 3)

            if not gather:
                @pl.when(r + 2 == n)
                def _():
                    p_copy(w_proj, me, 0, head=chip).start()
                    p_copy(w_proj, me, 1, head=core).start()

        if gather:
            @pl.when(r == 2)
            def _():
                p_piece(chip, chip).wait_recv()
                far_rows.start(0)

            for s in range(1, steps):
                @pl.when(r == min(s + 3, n))
                def _(s=s):
                    far_rows.arrive(s - 1)
                    far_rows.start(s)

                @pl.when(r == min(2 * s + 1, n - 1))
                def _(s=s):
                    expand.arrive(s - 1)
                    bias.arrive(s - 1)
                    expand.start(s)
                    bias.start(s)

                @pl.when(r == min(4 * s - 3, n))
                def _(s=s):
                    reduce.arrive(s - 1)
                    reduce.start(s)

        @pl.when(r >= 1)
        def _():
            chunk(r - 1)

        return 0

    lax.fori_loop(0, n + 1, body, 0)

    if gather:
        far_rows.arrive(steps - 1)
    else:
        p_copy(w_proj, chip, 0, head=chip).wait_recv()
    p_forward = p_copy(proj_out.at[at_cols(chip, width), :], chip, 2, head=core)
    p_forward.start()

    def pass_on(r, _):
        a_gather.forward(r)
        return 0

    lax.fori_loop(0, n, pass_on, 0)

    def settle(r, _):
        a_gather.arrive(r)
        a_gather.sent(r)
        x_gather.sent(r)
        x_copy(r).wait()
        qkv_copy(r).wait()
        a_copy(r).wait()

        @pl.when(r >= n - 2)
        def _():
            normed_copy(r).wait()

        return 0

    lax.fori_loop(0, n, settle, 0)
    p_copy(w_proj, core, 1, head=core).wait_recv()
    p_copy(w_proj, partner(core, 2), 2, head=core).wait_recv()
    if gather:
        p_piece(me, chip).wait_send()
        far_rows.sent()
    else:
        p_copy(w_proj, me, 0, head=chip).wait_send()
    p_copy(w_proj, me, 1, head=core).wait_send()
    p_forward.wait_send()
    for keep in keeps:
        keep.wait()
    if gather:
        expand.arrive(steps - 1)
        reduce.arrive(steps - 1)
        bias.arrive(steps - 1)
        expand.sent()
        reduce.sent()
        bias.sent()


def first(kind, layer_in, wq, wk, wv, gain, shift, bias_expand, w_proj, w_expand, w_reduce, dp_size):
    rows, width = layer_in.shape
    features = 4 * width
    block = SHORT
    n = rows // block
    heads = width // HEAD_DIM
    masks = masks_of(dp_size)
    local = w_expand.shape[1]
    gather = local % 128 == 0 and (width // dp_size) % 16 == 0
    units = local * dp_size if gather else 128
    any_spec = pl.BlockSpec(memory_space=pl.ANY)
    vmem = pl.BlockSpec(memory_space=pltpu.VMEM)
    blocks = max(dp_size - 1, 1)
    outs = pl.pallas_call(
        functools.partial(first_kernel, masks, gather),
        in_specs=[pl.BlockSpec(memory_space=pltpu.SMEM)] + [vmem] * 7 + [any_spec] * 3,
        out_specs=[any_spec] * 8 + [vmem],
        out_shape=[
            jax.ShapeDtypeStruct((rows, features), bf16),
            jax.ShapeDtypeStruct((rows, features), bf16),
            jax.ShapeDtypeStruct((rows, features), bf16),
            jax.ShapeDtypeStruct((rows, 3 * width), bf16),
            jax.ShapeDtypeStruct((features, features), bf16),
            jax.ShapeDtypeStruct((features, units), bf16),
            jax.ShapeDtypeStruct((features, units), bf16),
            jax.ShapeDtypeStruct((16, units), bf16),
            jax.ShapeDtypeStruct((n, heads, block), f32),
        ],
        scratch_shapes=[
            pltpu.VMEM((rows, features), bf16),
            pltpu.VMEM((2, block, features), bf16),
            pltpu.VMEM((rows, 3 * width), bf16),
            pltpu.VMEM((rows, width), bf16),
            pltpu.VMEM((16, local), bf16),
            pltpu.VMEM((heads, HEAD_DIM, block), f32),
            pltpu.SemaphoreType.DMA((6, n)),
            pltpu.SemaphoreType.DMA((6, n)),
            pltpu.SemaphoreType.DMA((6,)),
            pltpu.SemaphoreType.DMA((4,)),
            pltpu.SemaphoreType.DMA((4, n)),
        ]
        + [pltpu.SemaphoreType.DMA((blocks,))] * 8,
        compiler_params=pltpu.CompilerParams(
            vmem_limit_bytes=56 * MIB, collective_id=0, has_side_effects=True
        ),
    )(kind, layer_in, wq, wk, wv, gain, shift, bias_expand, w_proj, w_expand, w_reduce)
    x, a, normed, qkv, proj, expand, reduce, bias, logsum = outs
    if not gather:
        bias = jnp.broadcast_to(lax.all_gather(bias_expand, "dp", axis=1, tiled=True), (16, local * dp_size))
        expand = lax.all_gather(w_expand, "dp", axis=1, tiled=True)
        reduce = lax.all_gather(w_reduce, "dp", axis=1, tiled=True)
    return x, a, normed, qkv, proj, expand, reduce, bias, logsum


class HeadScatter:
    def __init__(self, width, src, from_core, far, near, from_chip, sems):
        self.width, self.src, self.from_core, self.far = width, src, from_core, far
        self.near, self.from_chip, self.sems = near, from_chip, sems
        self.me = lax.axis_index("head")
        self.core, self.chip = partner(self.me, 1), partner(self.me, 2)

    def to_core(self, r, k):
        who = self.core if k == 0 else partner(self.core, 2)
        return send_to(
            self.src(r).at[:, at_cols(who, self.width)],
            self.from_core.at[at_rows(r), k * self.width : (k + 1) * self.width],
            self.sems.at[2 * k, r],
            self.sems.at[2 * k + 1, r],
            head=self.core,
        )

    def to_chip(self, r):
        return send_to(
            self.far.at[r % 2],
            self.from_chip.at[at_rows(r), :],
            self.sems.at[4, r],
            self.sems.at[5, r],
            head=self.chip,
        )

    def start(self, r):
        self.to_core(r, 1).start()
        self.to_core(r, 0).start()

    def middle(self, r):
        src = self.src(r)
        self.to_core(r, 1).wait()
        self.far[r % 2] = (
            src[:, at_cols(self.chip, self.width)].astype(f32)
            + self.from_core[at_rows(r), self.width :].astype(f32)
        ).astype(bf16)
        self.to_chip(r).start()
        self.to_core(r, 0).wait()
        self.near[r % 2] = (
            src[:, at_cols(self.me, self.width)].astype(f32)
            + self.from_core[at_rows(r), : self.width].astype(f32)
        )

    def finish(self, r):
        self.to_chip(r).wait()
        return self.near[r % 2] + self.from_chip[at_rows(r), :].astype(f32)


GELU_C = 0.7978845608028654


def second_kernel(
    x_in, a_in, layer_in, w_proj_in, w_expand_in, w_reduce_in, grad_out, gain, shift, bias,
    grad_heads, grad_hid_out, ffn_out, hid_own, wide_out, narrow_out, proj_out, sums, grad_bias, grad_bias_reduce,
    g_buf, x_buf, a_buf, hid_buf, own_buf, ffn_buf, gh_buf, from_core, far_buf, near_buf, from_chip, wide, narrow, proj,
    w_proj, w_expand, w_reduce, in_buf, g_sems, s_sems, copy_sems, final_sems, load_sems,
):
    rows, width = layer_in.shape
    features = 4 * width
    block = SHORT
    n = rows // block
    me = lax.axis_index("head")
    greet([])

    g_gather = HeadGather(None, g_buf, width, g_sems)
    scatter = HeadScatter(width, lambda r: gh_buf.at[r % 2], from_core, far_buf, near_buf, from_chip, s_sems)

    def own_chunk(r):
        chunk = grad_out[at_rows(r), :]
        g_buf[at_rows(r), at_cols(me, width)] = chunk.astype(bf16)
        g_gather.start(r)
        return chunk

    loads = [
        pltpu.make_async_copy(src, dst, load_sems.at[k])
        for k, (src, dst) in enumerate(
            ((w_proj_in, w_proj), (w_expand_in, w_expand), (w_reduce_in, w_reduce))
        )
    ]

    def load_in(r):
        return pltpu.make_async_copy(layer_in.at[at_rows(r), :], in_buf.at[r % 2], copy_sems.at[5, r])

    def load_x(r):
        return pltpu.make_async_copy(x_in.at[at_rows(r), :], x_buf.at[r % 2], copy_sems.at[0, r])

    def load_a(r):
        return pltpu.make_async_copy(a_in.at[at_rows(r), :], a_buf.at[r % 2], copy_sems.at[1, r])

    def store_hid(r):
        return pltpu.make_async_copy(hid_buf.at[r % 2], grad_hid_out.at[at_rows(r), :], copy_sems.at[2, r])

    def store_ffn(r):
        return pltpu.make_async_copy(ffn_buf.at[r % 2], ffn_out.at[at_rows(r), :], copy_sems.at[3, r])

    def store_own(r):
        return pltpu.make_async_copy(own_buf.at[r % 2], hid_own.at[at_rows(r), :], copy_sems.at[4, r])

    def final(k, slot, buf, out):
        half = features // 2
        return pltpu.make_async_copy(
            buf.at[slot], out.at[slot * half : (slot + 1) * half, :], final_sems.at[k, slot]
        )

    own_chunk(0)
    own_chunk(1)
    load_a(0).start()
    loads[0].start()
    load_x(0).start()
    load_in(0).start()
    loads[1].start()
    loads[2].start()
    wide[...] = jnp.zeros_like(wide)
    narrow[...] = jnp.zeros_like(narrow)
    proj[...] = jnp.zeros_like(proj)
    sums[...] = jnp.zeros_like(sums)
    grad_bias[...] = jnp.zeros_like(grad_bias)
    grad_bias_reduce[...] = jnp.sum(grad_out[...], axis=0, keepdims=True)

    def body(r, _):
        g_gather.forward(r)

        @pl.when(r + 2 < n)
        def _():
            own_chunk(r + 2)

        load_x(r).wait()
        load_a(r).wait()
        load_in(r).wait()

        @pl.when(r == 0)
        def _():
            loads[0].wait()

        @pl.when(r + 1 < n)
        def _():
            load_x(r + 1).start()
            load_a(r + 1).start()
            load_in(r + 1).start()

        @pl.when(r >= 2)
        def _():
            store_hid(r - 2).wait()
            store_ffn(r - 2).wait()
            store_own(r - 2).wait()

        slot = r % 2
        a = a_buf[slot]
        attn = dot(a, w_proj[...])
        hidden = attn + x_buf[slot].astype(f32)
        own = attn[:, 0:width]
        for k in range(1, 4):
            own = jnp.where(me == k, attn[:, k * width : (k + 1) * width], own)
        own_buf[slot] = own + in_buf[slot]
        store_own(r).start()
        centre = hidden - jnp.sum(hidden, axis=1, keepdims=True) * (1.0 / features)
        spread = jnp.sum(centre * centre, axis=1, keepdims=True) * (1.0 / features)
        scale = lax.rsqrt(spread + eps)
        centred = centre * scale
        low = (centred * gain[...] + shift[...]).astype(bf16)

        @pl.when(r == 0)
        def _():
            loads[1].wait()
            loads[2].wait()

        z = dot(low, w_expand[...]) + bias[0:1, :].astype(f32)
        z2 = z * z
        t = jnp.tanh(z * (GELU_C + (GELU_C * 0.044715) * z2))
        half = 0.5 + 0.5 * t
        activated = (z * half).astype(bf16)
        slope = half + (0.5 * z) * (1.0 - t * t) * (GELU_C + (3.0 * GELU_C * 0.044715) * z2)
        g_gather.arrive(r)
        g = g_buf[at_rows(r), :]
        gp = slope * dot(g, w_reduce[...])
        gp_low = gp.astype(bf16)
        gn = dot(gp_low, w_expand[...], NT)
        scaled = gn * gain[...]
        mean_scaled = jnp.sum(scaled, axis=1, keepdims=True) * (1.0 / features)
        mean_both = jnp.sum(scaled * centred, axis=1, keepdims=True) * (1.0 / features)
        back = (scaled - mean_scaled - centred * mean_both) * scale
        back_low = (back + 0.25 * g.astype(f32)).astype(bf16)
        hid_buf[slot] = back_low
        store_hid(r).start()
        gh_buf[slot] = dot(back_low, w_proj[...], NT).astype(bf16)
        scatter.start(r)
        sums[0:1, :] += jnp.sum(gn * centred, axis=0, keepdims=True)
        sums[1:2, :] += jnp.sum(gn, axis=0, keepdims=True)
        grad_bias[...] += jnp.sum(gp_low.astype(f32), axis=0, keepdims=True)
        ffn_buf[slot] = dot(activated, w_reduce[...], NT).astype(bf16)
        store_ffn(r).start()
        wide[...] += dot(low, gp_low, TN)
        scatter.middle(r)
        narrow[...] += dot(g, activated, TN)
        proj[...] += dot(back_low, a, TN)

        @pl.when(r >= 1)
        def _():
            grad_heads[at_rows(r - 1), :] = scatter.finish(r - 1).astype(bf16)

        return 0

    lax.fori_loop(0, n, body, 0)
    for k, (full, buf, out) in enumerate(
        ((wide, ffn_buf, wide_out), (narrow, x_buf, narrow_out), (proj, hid_buf, proj_out))
    ):
        for p in range(2):
            if buf is ffn_buf:
                store_ffn(n - 2 + p).wait()
            if buf is hid_buf:
                store_hid(n - 2 + p).wait()
            half = features // 2
            slot = (n - 2 + p) % 2
            buf[slot] = full[slot * half : (slot + 1) * half, :].astype(bf16)
            final(k, slot, buf, out).start()
    grad_heads[at_rows(n - 1), :] = scatter.finish(n - 1).astype(bf16)
    for k, (buf, out) in enumerate(((ffn_buf, wide_out), (x_buf, narrow_out), (hid_buf, proj_out))):
        for slot in range(2):
            final(k, slot, buf, out).wait()

    def settle(r, _):
        g_gather.sent(r)

        @pl.when(r >= n - 2)
        def _():
            store_own(r).wait()

        return 0

    lax.fori_loop(0, n, settle, 0)


def second(x, a, grad_out, layer_in, w_proj, w_expand, w_reduce, gain, shift, bias):
    rows, width = layer_in.shape
    features = 4 * width
    units = w_expand.shape[1]
    block = SHORT
    n = rows // block
    any_spec = pl.BlockSpec(memory_space=pl.ANY)
    vmem = pl.BlockSpec(memory_space=pltpu.VMEM)
    return pl.pallas_call(
        second_kernel,
        in_specs=[any_spec] * 6 + [vmem] * 4,
        out_specs=[vmem] + [any_spec] * 6 + [vmem] * 3,
        out_shape=[
            jax.ShapeDtypeStruct((rows, width), bf16),
            jax.ShapeDtypeStruct((rows, features), bf16),
            jax.ShapeDtypeStruct((rows, features), bf16),
            jax.ShapeDtypeStruct((rows, width), f32),
            jax.ShapeDtypeStruct((features, units), bf16),
            jax.ShapeDtypeStruct((features, units), bf16),
            jax.ShapeDtypeStruct((features, features), bf16),
            jax.ShapeDtypeStruct((2, features), f32),
            jax.ShapeDtypeStruct((1, units), f32),
            jax.ShapeDtypeStruct((1, width), f32),
        ],
        scratch_shapes=[
            pltpu.VMEM((rows, features), bf16),
            pltpu.VMEM((2, block, features), bf16),
            pltpu.VMEM((2, block, features), bf16),
            pltpu.VMEM((2, block, features), bf16),
            pltpu.VMEM((2, block, width), f32),
            pltpu.VMEM((2, block, features), bf16),
            pltpu.VMEM((2, block, features), bf16),
            pltpu.VMEM((rows, 2 * width), bf16),
            pltpu.VMEM((2, block, width), bf16),
            pltpu.VMEM((2, block, width), f32),
            pltpu.VMEM((rows, width), bf16),
            pltpu.VMEM((features, units), f32),
            pltpu.VMEM((features, units), f32),
            pltpu.VMEM((features, features), f32),
            pltpu.VMEM((features, features), bf16),
            pltpu.VMEM((features, units), bf16),
            pltpu.VMEM((features, units), bf16),
            pltpu.VMEM((2, block, width), f32),
            pltpu.SemaphoreType.DMA((6, n)),
            pltpu.SemaphoreType.DMA((6, n)),
            pltpu.SemaphoreType.DMA((6, n)),
            pltpu.SemaphoreType.DMA((3, 2)),
            pltpu.SemaphoreType.DMA((3,)),
        ],
        compiler_params=pltpu.CompilerParams(
            vmem_limit_bytes=62 * MIB, collective_id=1, has_side_effects=True
        ),
    )(x, a, layer_in, w_proj, w_expand, w_reduce, grad_out, gain, shift, bias)


EARLY = 0
TIMES = {
    "start": 25.4,
    "middle": (8.4, 12.6, 20.2, 21.1, 21.7, 26.6, 31.4, 38.8),
    "finish": (15.8, 22.4, 56.4, 76.2, 79.1, 82.6, 86.4, 87.9),
    "wide": (59.1, 71.4, 94.0),
    "narrow": (33.3, 51.5, 80.5),
    "proj": (36.2, 40.5, 49.8, 56.8, 66.6, 82.7),
    "first": (44.3, 56.8, 61.0, 67.5, 74.8, 81.6),
    "first_turned": (39.4, 47.3, 60.2, 69.7, 69.7, 86.4),
    "second": (56.5, 60.1, 68.3, 72.2, 74.9, 312.3),
    "second_turned": (61.0, 63.4, 68.6, 72.3, 78.2, 407.9),
    "small": (73.9, 74.9, 76.7, 77.5, 78.5),
}


class DpScatter:
    def __init__(self, part, recv_buf, masks, send, recv, first_part=None):
        self.part, self.recv_buf, self.masks = part, recv_buf, masks
        self.first_part = first_part or part
        self.group = lax.axis_index("dp")
        self.send, self.recv = send, recv
        size = 1 << len(masks)
        left, at = list(range(size)), 0
        self.plan = []
        for mask in masks:
            mine = [k for k in left if not k & mask]
            self.plan.append((mask, [(k, at + p) for p, k in enumerate(mine)]))
            at += len(mine)
            left = mine

    def where(self, k, part):
        who = self.group
        for mask in self.masks:
            if k & mask:
                who = partner(who, mask)
        return part(who)

    def copy(self, mask, k, slot):
        part = self.first_part if mask == self.masks[0] else self.part
        return send_to(
            self.where(k ^ mask, part), self.recv_buf.at[slot], self.send.at[slot], self.recv.at[slot],
            dp=partner(self.group, mask),
        )

    def start(self, step):
        mask, items = self.plan[step]
        for k, slot in items:
            self.copy(mask, k, slot).start()

    def arrive(self, step):
        mask, items = self.plan[step]
        for k, slot in items:
            self.copy(mask, k, slot).wait_recv()
            ref = self.where(k, self.part)
            ref[...] = (ref[...].astype(f32) + self.recv_buf[slot].astype(f32)).astype(bf16)

    def sent(self):
        for mask, items in self.plan:
            for k, slot in items:
                self.copy(mask, k, slot).wait_send()


class DpSum:
    def __init__(self, buf, recv_buf, out, masks, sems, keep_sem):
        size = 1 << len(masks)
        rows = buf.shape[0] // size
        self.steps = len(masks)
        self.scatter = DpScatter(lambda k: buf.at[at_rows(k, rows), :], recv_buf, masks, sems.at[0], sems.at[1])
        me = lax.axis_index("dp")
        own = buf.at[at_rows(me, rows), :]
        self.keep = pltpu.make_async_copy(own, out.at[at_rows(me, rows), :], keep_sem)
        self.spread = DpSpread(
            own, lambda k: out.at[at_rows(k, rows), :], masks[::-1], sems.at[2], sems.at[3]
        )

    def start(self):
        self.scatter.start(0)

    def advance(self, step):
        if step < self.steps:
            self.scatter.arrive(step)
            if step + 1 < self.steps:
                self.scatter.start(step + 1)
            else:
                self.keep.start()
                self.spread.start(0)
        else:
            self.spread.arrive(step - self.steps)
            if step + 1 < 2 * self.steps:
                self.spread.start(step - self.steps + 1)

    def settle(self):
        self.scatter.sent()
        self.spread.sent()
        self.keep.wait()


class HeadSum:
    def __init__(self, width, src, mine, from_core, from_chip, sems):
        self.width, self.src, self.mine = width, src, mine
        self.from_core, self.from_chip, self.sems = from_core, from_chip, sems
        self.me = lax.axis_index("head")
        self.core, self.chip = partner(self.me, 1), partner(self.me, 2)

    def place(self, r, k):
        return self.from_core.at[at_rows(r), k * self.width : (k + 1) * self.width]

    def to_core(self, r, k):
        who = self.core if k == 0 else partner(self.core, 2)
        return send_to(
            self.src(r).at[:, at_cols(who, self.width)], self.place(r, k),
            self.sems.at[2 * k, r], self.sems.at[2 * k + 1, r], head=self.core,
        )

    def to_chip(self, r):
        return send_to(
            self.place(r, 1), self.from_chip.at[at_rows(r), :], self.sems.at[4, r], self.sems.at[5, r], head=self.chip
        )

    def start(self, r):
        self.to_core(r, 1).start()
        self.to_core(r, 0).start()

    def middle(self, r):
        for k, who in ((1, self.chip), (0, self.me)):
            self.to_core(r, k).wait()
            place = self.place(r, k)
            place[...] = (self.mine(r, who, k) + place[...].astype(f32)).astype(bf16)
            if k == 1:
                self.to_chip(r).start()

    def finish(self, r):
        self.to_chip(r).wait()
        return self.place(r, 0)[...].astype(f32) + self.from_chip[at_rows(r), :].astype(f32)


def third_kernel(
    masks, scatter_inside,
    kind, qkv, grad_heads, logsum, wq, wk, wv, gain, sums_2, grad_bias, grad_bias_reduce,
    wide_in, narrow_in, a_in, x_in, normed_in, grad_hid, ffn, proj,
    ffn_sum, total_sum, sum_p, sum_a, sum_b, wide_sum, narrow_sum, small,
    dqkv, dk_acc, dv_acc, dq_acc, delta, wgrad, slots, wide, narrow, pay_p, pay_a, pay_b,
    recv_p, recv_a, recv_b, recv_w, recv_n,
    s_core, s_chip, s_mine, s_out, f_src, f_core, f_chip, f_slots, small_recv,
    wg_sems, s_sems, mine_sems, out_sems, f_sems, p_sems, a_sems, b_sems, w_sems, n_sems, slot_sems, keep_sems, small_sems, total_sems,
):
    rows = qkv.shape[0]
    width = grad_heads.shape[1]
    features = x_in.shape[1]
    block = SHORT
    n = rows // block
    heads = width // HEAD_DIM
    me = lax.axis_index("head")
    group = lax.axis_index("dp")
    steps = len(masks)
    greet(masks)

    agenda = []

    def due(time, action, *args):
        agenda.append((time, len(agenda), functools.partial(action, *args)))

    turned = masks[1:2] + masks[:1] + masks[2:]

    if scatter_inside:
        local = wide_sum.shape[1]

        def columns_of(ref):
            return lambda k: ref.at[:, at_cols(k, local)]

        wide_rs = DpScatter(columns_of(wide), recv_w, masks, w_sems.at[0], w_sems.at[1], columns_of(wide_in))
        narrow_rs = DpScatter(columns_of(narrow), recv_n, turned, n_sems.at[0], n_sems.at[1], columns_of(narrow_in))
        wide_rs.start(0)
        narrow_rs.start(0)
        loads = [
            pltpu.make_async_copy(wide_in, wide, keep_sems.at[5]),
            pltpu.make_async_copy(narrow_in, narrow, keep_sems.at[6]),
        ]

        def scatter_step(scatter, load, out, s):
            if s == 0:
                load.wait()
            scatter.arrive(s)
            if s + 1 < steps:
                scatter.start(s + 1)
            else:
                out[...] = scatter.part(group)[...].astype(f32)

        for s in range(steps):
            due(TIMES["wide"][min(s, 2)] + max(s - 2, 0), scatter_step, wide_rs, loads[0], wide_sum, s)
            due(TIMES["narrow"][min(s, 2)] + max(s - 2, 0), scatter_step, narrow_rs, loads[1], narrow_sum, s)

    n_proj = features // block
    n_side = n_proj + n

    def side_src(c):
        return proj.at[at_rows(c), :] if c < n_proj else ffn.at[at_rows(c - n_proj), :]

    def side_load(c, k):
        who = me if k == 0 else partner(me, 2)
        return pltpu.make_async_copy(
            side_src(c).at[:, at_cols(who, width)], s_mine.at[c % 4, k], mine_sems.at[k, c]
        )

    def side_mine(c, who, k):
        side_load(c, k).wait()
        return s_mine[c % 4, k].astype(f32)

    side = HeadSum(width, side_src, side_mine, s_core, s_chip, s_sems)

    def side_copy(c):
        return pltpu.make_async_copy(s_out.at[c % 2], ffn_sum.at[at_rows(c - n_proj), :], out_sems.at[c])

    def side_start(c):
        side_load(c, 1).start()
        side_load(c, 0).start()

    def side_middle(c):
        side.middle(c)
        if c + 4 < n_side:
            side_start(c + 4)

    def side_finish(c):
        value = side.finish(c).astype(bf16)
        if c < n_proj:
            pay_p[c * block : (c + 1) * block, :] = value
        else:
            if c - 2 >= n_proj:
                side_copy(c - 2).wait()
            s_out[c % 2] = value
            side_copy(c).start()

    for c in range(min(4, n_side)):
        side_start(c)
    for c in range(n_side):
        side.start(c)
        due(TIMES["middle"][min(c, 7)] + 6 * max(c - 7, 0), side_middle, c)
        due(TIMES["finish"][min(c, 7)] + 6 * max(c - 7, 0), side_finish, c)
    if scatter_inside:
        for load in loads:
            load.start()

    proj_sum = DpSum(pay_p, recv_p, sum_p, masks, p_sems, keep_sems.at[0])
    first_sums, second_sums = [], []
    halves = 2 if features % (32 << steps) == 0 else 1
    for p in range(halves):
        at = slice(p * features // halves, (p + 1) * features // halves)
        first_sums.append(
            DpSum(pay_a.at[at], recv_a.at[p], sum_a.at[at], (turned, masks)[p], a_sems.at[p], keep_sems.at[1 + 2 * p])
        )
        second_sums.append(
            DpSum(pay_b.at[at], recv_b.at[p], sum_b.at[at], (masks, turned)[p], b_sems.at[p], keep_sems.at[2 + 2 * p])
        )
    due(TIMES["start"], proj_sum.start)
    for which, times in (
        [(proj_sum, TIMES["proj"])]
        + list(zip(first_sums, (TIMES["first"], TIMES["first_turned"])))
        + list(zip(second_sums, (TIMES["second"], TIMES["second_turned"])))
    ):
        for s in range(2 * steps):
            due(times[min(s * 3 // steps, 5)] + 0.01 * s, which.advance, s)

    apart = (1 - kind[0]).astype(f32) * masked_value
    slopes = [s * LOG2E for s in head_slopes(me, heads)]
    two = 2 * block
    pairs = rows // two
    attended = pltpu.make_async_copy(a_in.at[:, at_cols(me, width)], dqkv.at[:, 0:width], wg_sems.at[2])
    attended.start()
    attended.wait()

    def fill(i, _):
        for h in range(heads):
            cols = slice(h * HEAD_DIM, (h + 1) * HEAD_DIM)
            both = grad_heads[at_rows(i), cols].astype(f32) * dqkv[at_rows(i), cols].astype(f32)
            delta[i, h : h + 1, :] = jnp.sum(both.T, axis=0, keepdims=True)
        return 0

    lax.fori_loop(0, n, fill, 0)

    def load_normed(h, m):
        at = (h * pairs + pairs - 1 - m) % 2
        return [
            pltpu.make_async_copy(
                normed_in.at[at_rows(2 * m + p), :], slots.at[2 * at + p], slot_sems.at[2 * at + p]
            )
            for p in range(2)
        ]

    for copy in load_normed(0, pairs - 1):
        copy.start()

    key_place = lax.broadcasted_iota(jnp.int32, (block, two), 0)
    query_place = lax.broadcasted_iota(jnp.int32, (block, two), 1)

    def head_cols(h, k):
        return pl.ds(pl.multiple_of(k * width + h * HEAD_DIM, HEAD_DIM), HEAD_DIM)

    def load_x(q):
        return pltpu.make_async_copy(x_in.at[at_rows(n - 1 - q), :], f_slots.at[q % 2], total_sems.at[0, q])

    def load_hid(q):
        return pltpu.make_async_copy(grad_hid.at[at_rows(n - 1 - q), :], f_slots.at[2 + q % 2], total_sems.at[1, q])

    def last_mine(q, who, k):
        return f_src[q % 2, :, at_cols(who, width)].astype(f32)

    last = HeadSum(width, lambda q: f_src.at[q % 2], last_mine, f_core, f_chip, f_sems)

    def last_copy(q):
        return pltpu.make_async_copy(
            dqkv.at[at_rows(n - 1 - q), 0:width], total_sum.at[at_rows(n - 1 - q), :], total_sems.at[2, q]
        )

    load_x(0).start()
    load_hid(0).start()
    small[...] = jnp.zeros_like(small)
    small[0:2, :] = sums_2[...]
    small[4:5, 0:grad_bias.shape[1]] = grad_bias[...]
    small[5:6, 0:width] = grad_bias_reduce[...]

    def last_chunk(q, _):
        load_x(q).wait()
        load_hid(q).wait()

        @pl.when(q + 1 < n)
        def _():
            load_x(q + 1).start()
            load_hid(q + 1).start()

        at = at_rows(n - 1 - q)
        gf = dot(dqkv[at, 0:width], wq[...], NT)
        gf += dot(dqkv[at, width : 2 * width], wk[...], NT)
        gf += dot(dqkv[at, 2 * width :], wv[...], NT)
        x = f_slots[q % 2].astype(f32)
        centre = x - jnp.sum(x, axis=1, keepdims=True) * (1.0 / features)
        spread = jnp.sum(centre * centre, axis=1, keepdims=True) * (1.0 / features)
        scale = lax.rsqrt(spread + eps)
        centred = centre * scale
        scaled = gf * gain[...]
        mean_scaled = jnp.sum(scaled, axis=1, keepdims=True) * (1.0 / features)
        mean_both = jnp.sum(scaled * centred, axis=1, keepdims=True) * (1.0 / features)
        back = (scaled - mean_scaled - centred * mean_both) * scale
        f_src[q % 2] = (back + f_slots[2 + q % 2].astype(f32)).astype(bf16)
        last.start(q)
        small[2:3, :] += jnp.sum(gf * centred, axis=0, keepdims=True)
        small[3:4, :] += jnp.sum(gf, axis=0, keepdims=True)
        @pl.when(q >= 1)
        def _():
            last.middle(q - 1)

        return 0

    def sweep(h, service):
        own_cols = pl.ds(pl.multiple_of(h * HEAD_DIM, HEAD_DIM), HEAD_DIM)
        slope = slopes[h]
        dk_acc[...] = jnp.zeros_like(dk_acc)
        dv_acc[...] = jnp.zeros_like(dv_acc)

        def tile(m, j, single):
            q_size = block if single else two
            start = 2 * m + 1 if single else 2 * m
            at = pl.ds(pl.multiple_of(start * block, block), q_size)
            q = qkv[at, head_cols(h, 0)]
            g = grad_heads[at, own_cols]
            k = qkv[at_rows(j), head_cols(h, 1)]
            v = qkv[at_rows(j), head_cols(h, 2)]
            keys, queries = key_place[:, :q_size], query_place[:, :q_size]
            if single:
                place = keys.astype(f32) * slope
                allowed = keys <= queries
                lse, dlt = logsum[start, h : h + 1, :], delta[start, h : h + 1, :]
            else:
                second = (queries >= block).astype(jnp.int32)
                offset = (j - start) * block
                place = (keys + offset - second * block).astype(f32) * slope
                allowed = keys + offset <= queries
                place += jnp.where(second + start == j, 0.0, apart)
                lse = jnp.concatenate([logsum[start, h : h + 1, :], logsum[start + 1, h : h + 1, :]], 1)
                dlt = jnp.concatenate([delta[start, h : h + 1, :], delta[start + 1, h : h + 1, :]], 1)
            s = dot(k, q, NT) * (SCALE * LOG2E) + place
            p = jnp.where(allowed, jnp.exp2(s - lse), 0.0)
            ds = (p * (dot(v, g, NT) - dlt)).astype(bf16)
            dv_acc[at_rows(j), :] += dot(p.astype(bf16), g)
            dk_acc[at_rows(j), :] += dot(ds, q)
            if single:
                dq_acc[:, block:] += dot(k, ds, TN)
            else:
                dq_acc[...] += dot(k, ds, TN)

        def outer(step, _):
            m = pairs - 1 - step
            dq_acc[...] = jnp.zeros_like(dq_acc)

            def inner(j, _):
                service(step, j)
                tile(m, j, False)
                return 0

            lax.fori_loop(0, 2 * m + 1, inner, 0)
            service(step, 2 * m + 1)
            tile(m, 2 * m + 1, True)
            for copy in load_normed(h, m):
                copy.wait()

            @pl.when(step + 1 < pairs)
            def _():
                for copy in load_normed(h, m - 1):
                    copy.start()

            if h + 1 < heads:
                @pl.when(step + 1 == pairs)
                def _():
                    for copy in load_normed(h + 1, pairs - 1):
                        copy.start()

            at = pl.ds(pl.multiple_of(m * two, two), two)
            dq = (dq_acc[...] * SCALE).T.astype(bf16)
            dk = (dk_acc[at, :] * SCALE).astype(bf16)
            dv = dv_acc[at, :].astype(bf16)
            dqkv[at, head_cols(h, 0)] = dq
            dqkv[at, head_cols(h, 1)] = dk
            dqkv[at, head_cols(h, 2)] = dv
            slot = (h * pairs + step) % 2
            low = jnp.concatenate([slots[2 * slot], slots[2 * slot + 1]], 0)
            part = dot(low, jnp.concatenate([dq, dk, dv], 1), TN)

            @pl.when(step == 0)
            def _():
                wgrad[...] = part

            @pl.when(step > 0)
            def _():
                wgrad[...] += part

            if h + 1 == heads:
                for early in range(EARLY):
                    @pl.when(step == early)
                    def _(early=early):
                        lax.fori_loop(2 * early, 2 * early + 2, last_chunk, 0)

            return 0

        lax.fori_loop(0, pairs, outer, 0)

    places, clock = [], 3.0
    for h in range(heads):
        for step in range(pairs):
            tiles = 2 * (pairs - 1 - step) + 2
            for j in range(tiles):
                places.append((clock, h, step, j))
                clock += 1.9 if j + 1 < tiles else 1.1
            clock += 1.6 + (5.4 if h + 1 == heads and step < EARLY else 0.0)
    finish_clock, finish_time = clock, 2.7
    begun = 2 * EARLY

    def events(start, end):
        return [action for time, _, action in sorted(agenda, key=lambda e: e[:2]) if start <= time < end]

    def run(actions):
        for action in actions:
            action()

    def service_of(h):
        def service(step, j):
            for k, (time, at_h, at_step, at_j) in enumerate(places):
                earlier = places[k - 1][0] if k else -1.0
                actions = events(earlier + 1e-6, time + 1e-6)
                if at_h == h and actions:
                    @pl.when((step == at_step) & (j == at_j))
                    def _(actions=actions):
                        run(actions)

        return service

    sweep(0, service_of(0))
    pay_a[...] = wgrad[...].astype(bf16)
    for which in first_sums:
        which.start()
    sweep(1, service_of(1))
    pay_b[...] = wgrad[...].astype(bf16)
    for which in second_sums:
        which.start()

    done = places[-1][0] + 1e-6

    def last_step(q, _):
        for k in range(begun, n):
            start = done if k == begun else finish_clock + (k - begun - 1) * finish_time
            actions = events(start, finish_clock + (k - begun) * finish_time)
            if actions:
                @pl.when(q == k)
                def _(actions=actions):
                    run(actions)

        return last_chunk(q, _)

    lax.fori_loop(begun, n, last_step, 0)
    last.middle(n - 1)
    done = finish_clock + (n - begun - 1) * finish_time

    def small_copy(s):
        where = {"head": partner(me, masks_of(4)[s])} if s < 2 else {"dp": partner(group, masks[s - 2])}
        return send_to(small, small_recv.at[s], small_sems.at[0, s], small_sems.at[1, s], **where)

    def small_step(s):
        small_copy(s).wait()
        if s < 2:
            small[0:4, :] += small_recv[s, 0:4, :]
        else:
            small[...] += small_recv[s]
        if s + 1 < 2 + steps:
            small_copy(s + 1).start()

    def last_finish(q):
        dqkv[at_rows(n - 1 - q), 0:width] = last.finish(q).astype(bf16)
        last_copy(q).start()

    small_copy(0).start()
    for s in range(2 + steps):
        due(max(done, TIMES["small"][min(s, 4)]) + max(s - 4, 0), small_step, s)
    for q in range(n):
        due(max(done, finish_clock + 6.1 * (q - begun + 1) + 4.0), last_finish, q)
    run(events(done, 1e9))
    proj_sum.settle()
    for which in first_sums + second_sums:
        which.settle()
    if scatter_inside:
        wide_rs.sent()
        narrow_rs.sent()
    for c in range(n_side - 2, n_side):
        side_copy(c).wait()
    for q in range(n):
        last_copy(q).wait()


def third(
    kind, qkv, grad_heads, logsum, wq, wk, wv, gain, sums_2, grad_bias, grad_bias_reduce, wide, narrow,
    a, x, normed, grad_hid, ffn, proj, local, dp_size,
):
    rows, width = grad_heads.shape
    features = x.shape[1]
    block = SHORT
    n = rows // block
    heads = width // HEAD_DIM
    masks = masks_of(dp_size)
    inside = local % 128 == 0
    home = local if inside else 128
    any_spec = pl.BlockSpec(memory_space=pl.ANY)
    vmem = pl.BlockSpec(memory_space=pltpu.VMEM)
    blocks = max(dp_size - 1, 1)
    n_side = features // block + n
    cols = 3 * HEAD_DIM
    part = features // dp_size
    halves = 2 if features % (32 * dp_size) == 0 else 1
    recv_blocks = blocks if inside else 1

    def dma(*shape):
        return pltpu.SemaphoreType.DMA(shape)

    return pl.pallas_call(
        functools.partial(third_kernel, masks, inside),
        in_specs=[pl.BlockSpec(memory_space=pltpu.SMEM)] + [vmem] * 10 + [any_spec] * 8,
        out_specs=[any_spec] * 5 + [vmem] * 3,
        out_shape=[
            jax.ShapeDtypeStruct((rows, width), bf16),
            jax.ShapeDtypeStruct((rows, width), bf16),
            jax.ShapeDtypeStruct((features, width), bf16),
            jax.ShapeDtypeStruct((features, cols), bf16),
            jax.ShapeDtypeStruct((features, cols), bf16),
            jax.ShapeDtypeStruct((features, home), f32),
            jax.ShapeDtypeStruct((features, home), f32),
            jax.ShapeDtypeStruct((8, features), f32),
        ],
        scratch_shapes=[
            pltpu.VMEM((rows, 3 * width), bf16),
            pltpu.VMEM((rows, HEAD_DIM), f32),
            pltpu.VMEM((rows, HEAD_DIM), f32),
            pltpu.VMEM((HEAD_DIM, 2 * block), f32),
            pltpu.VMEM((n, heads, block), f32),
            pltpu.VMEM((features, cols), f32),
            pltpu.VMEM((4, block, features), bf16),
            pltpu.VMEM(wide.shape if inside else (16, 128), bf16),
            pltpu.VMEM(narrow.shape if inside else (16, 128), bf16),
            pltpu.VMEM((features, width), bf16),
            pltpu.VMEM((features, cols), bf16),
            pltpu.VMEM((features, cols), bf16),
            pltpu.VMEM((blocks, part, width), bf16),
            pltpu.VMEM((halves, blocks, part // halves, cols), bf16),
            pltpu.VMEM((halves, blocks, part // halves, cols), bf16),
            pltpu.VMEM((recv_blocks, features, home), bf16),
            pltpu.VMEM((recv_blocks, features, home), bf16),
            pltpu.VMEM((n_side * block, 2 * width), bf16),
            pltpu.VMEM((n_side * block, width), bf16),
            pltpu.VMEM((4, 2, block, width), bf16),
            pltpu.VMEM((2, block, width), bf16),
            pltpu.VMEM((2, block, features), bf16),
            pltpu.VMEM((rows, 2 * width), bf16),
            pltpu.VMEM((rows, width), bf16),
            pltpu.VMEM((4, block, features), bf16),
            pltpu.VMEM((2 + len(masks), 8, features), f32),
            dma(3),
            dma(6, n_side),
            dma(2, n_side),
            dma(n_side),
            dma(6, n),
            dma(4, blocks),
            dma(halves, 4, blocks),
            dma(halves, 4, blocks),
            dma(2, blocks),
            dma(2, blocks),
            dma(4),
            dma(7),
            dma(2, 2 + len(masks)),
            dma(3, n),
        ],
        compiler_params=pltpu.CompilerParams(
            vmem_limit_bytes=63 * MIB, collective_id=2, has_side_effects=True
        ),
    )(
        kind, qkv, grad_heads, logsum, wq, wk, wv, gain, sums_2, grad_bias, grad_bias_reduce, wide, narrow,
        a, x, normed, grad_hid, ffn, proj,
    )


def output_kernel(
    hid_own, ffn_sum, total, bias_reduce, sum_p, sum_a, sum_b, wide_sum, narrow_sum, small,
    layer_out, grad_in, grad_q, grad_k, grad_v, grad_proj, grad_expand, grad_reduce,
    attn_gain, attn_shift, ffn_gain, ffn_shift, grad_bias_reduce, *grad_bias,
):
    layer_out[...] = hid_own[...] + bias_reduce[...] + ffn_sum[...].astype(f32)
    grad_in[...] = total[...].astype(f32)
    for k, out in enumerate((grad_q, grad_k, grad_v)):
        cols = slice(k * HEAD_DIM, (k + 1) * HEAD_DIM)
        out[:, 0:HEAD_DIM] = sum_a[:, cols].astype(f32)
        out[:, HEAD_DIM:] = sum_b[:, cols].astype(f32)
    grad_proj[...] = sum_p[...].astype(f32).T
    grad_expand[...] = wide_sum[...]
    grad_reduce[...] = narrow_sum[...]
    for k, out in ((2, attn_gain), (3, attn_shift), (0, ffn_gain), (1, ffn_shift)):
        out[...] = small[k, :]
    grad_bias_reduce[...] = small[5, 0 : grad_bias_reduce.shape[0]]
    for out in grad_bias:
        out[...] = small[4:5, at_cols(lax.axis_index("dp"), out.shape[1])]


def outputs(hid_own, ffn_sum, total, bias_reduce, sum_p, sum_a, sum_b, wide_sum, narrow_sum, small, inside):
    rows, width = hid_own.shape
    features = sum_p.shape[0]
    block = 2 * SHORT
    part = features // 2
    home = wide_sum.shape[1]

    def by_rows(columns):
        return pl.BlockSpec((block, columns), lambda i: (i, 0))

    def by_part(columns):
        return pl.BlockSpec((part, columns), lambda i: (jnp.minimum(i, 1), 0))

    def of(*shape):
        return jax.ShapeDtypeStruct(shape, f32)

    return pl.pallas_call(
        output_kernel,
        grid=(rows // block,),
        in_specs=[
            by_rows(width), by_rows(width), by_rows(width), full_spec(bias_reduce.shape), by_part(width),
            by_part(sum_a.shape[1]), by_part(sum_b.shape[1]), by_part(home), by_part(home), full_spec(small.shape),
        ],
        out_specs=[by_rows(width)] * 2
        + [by_part(width)] * 3
        + [pl.BlockSpec((width, part), lambda i: (0, jnp.minimum(i, 1)))]
        + [by_part(home)] * 2
        + [full_spec((features,))] * 4
        + [full_spec((width,))]
        + [full_spec((1, home))] * inside,
        out_shape=[of(rows, width)] * 2
        + [of(features, width)] * 3
        + [of(width, features)]
        + [of(features, home)] * 2
        + [of(features)] * 4
        + [of(width)]
        + [of(1, home)] * inside,
        compiler_params=pltpu.CompilerParams(vmem_limit_bytes=62 * MIB),
    )(hid_own, ffn_sum, total, bias_reduce, sum_p, sum_a, sum_b, wide_sum, narrow_sum, small)


def shards(
    dp_size,
    layer_in,
    bucket,
    w_query,
    w_key,
    w_value,
    w_proj,
    attn_gain,
    attn_shift,
    ffn_gain,
    ffn_shift,
    w_expand,
    bias_expand,
    w_reduce,
    bias_reduce,
    grad_out,
):
    group = lax.axis_index("dp")
    width = layer_in.shape[1]
    local = w_expand.shape[1]
    gain_1 = attn_gain[None]
    x, a, normed, qkv, proj, expand, reduce, bias, logsum = first(
        bucket, layer_in, w_query, w_key, w_value, gain_1, attn_shift[None], bias_expand, w_proj, w_expand, w_reduce, dp_size
    )
    (
        grad_heads, grad_hid, ffn, hid_own, grad_wide, grad_narrow, proj_part, sums_2, grad_bias, grad_bias_reduce,
    ) = second(
        x, a, grad_out, layer_in, proj, expand, reduce, ffn_gain[None], ffn_shift[None], bias
    )
    ffn_sum, total, sum_p, sum_a, sum_b, wide_sum, narrow_sum, small = third(
        bucket, qkv, grad_heads, logsum, w_query, w_key, w_value, gain_1, sums_2, grad_bias, grad_bias_reduce,
        grad_wide, grad_narrow, a, x, normed, grad_hid, ffn, proj_part, local, dp_size,
    )
    if local % 128:
        wide_sum = lax.psum_scatter(grad_wide.astype(f32), "dp", scatter_dimension=1, tiled=True)
        narrow_sum = lax.psum_scatter(grad_narrow.astype(f32), "dp", scatter_dimension=1, tiled=True)
    (
        layer_out, grad_in, grad_query, grad_key, grad_value, grad_proj, grad_expand, grad_reduce,
        grad_attn_gain, grad_attn_shift, grad_ffn_gain, grad_ffn_shift, grad_bias_reduce, *grad_bias_expand,
    ) = outputs(
        hid_own, ffn_sum, total, bias_reduce[None], sum_p, sum_a, sum_b, wide_sum, narrow_sum, small, int(local % 128 == 0)
    )
    if local % 128:
        grad_bias_expand = [lax.dynamic_slice(small, (4, group * local), (1, local))]
    return (
        layer_out,
        grad_in,
        grad_query,
        grad_key,
        grad_value,
        grad_proj,
        grad_attn_gain,
        grad_attn_shift,
        grad_ffn_gain,
        grad_ffn_shift,
        grad_expand,
        grad_bias_expand[0],
        grad_reduce,
        grad_bias_reduce,
    )


def solution(mesh):
    placed = (
        P("dp", "head"),
        P("dp"),
        P(None, "head"),
        P(None, "head"),
        P(None, "head"),
        P("head", None),
        P(),
        P(),
        P(),
        P(),
        P(None, ("dp", "head")),
        P(None, ("dp", "head")),
        P(None, ("dp", "head")),
        P("head"),
        P("dp", "head"),
    )
    return jax.shard_map(
        functools.partial(shards, mesh.shape["dp"]),
        mesh=mesh,
        in_specs=placed,
        out_specs=(
            P("dp", "head"),
            P("dp", "head"),
            P(None, "head"),
            P(None, "head"),
            P(None, "head"),
            P("head", None),
            P(),
            P(),
            P(),
            P(),
            P(None, ("dp", "head")),
            P(None, ("dp", "head")),
            P(None, ("dp", "head")),
            P("head"),
        ),
        check_vma=False,
    )
```

```python
import functools

import jax
import jax.numpy as jnp
from jax import lax
from jax.experimental import pallas as pl
from jax.experimental.pallas import tpu as pltpu
from jax.sharding import PartitionSpec as P

HEADS = 8
HEAD_DIM = 128
SHORT = 512
eps = 1e-05
masked_value = -1e30
LOG2E = 1.4426950408889634
LN2 = 0.6931471805599453
SCALE = HEAD_DIM ** (-0.5)
MIB = 1024 * 1024
f32 = jnp.float32
bf16 = jnp.bfloat16

NN = (((1,), (0,)), ((), ()))
NT = (((1,), (1,)), ((), ()))
TN = (((0,), (0,)), ((), ()))


def dot(left, right, dims=NN):
    return lax.dot_general(left, right, dims, preferred_element_type=f32)


def full_spec(shape):
    return pl.BlockSpec(shape, lambda *_: (0,) * len(shape))


MESH = pl.DeviceIdType.MESH


def partner(index, mask):
    return index + mask - 2 * mask * ((index // mask) % 2)


def masks_of(size):
    return [1 << k for k in range(size.bit_length() - 1)]


def send_to(src, dst, send, recv, **where):
    return pltpu.make_async_remote_copy(
        src_ref=src, dst_ref=dst, send_sem=send, recv_sem=recv, device_id=where, device_id_type=MESH
    )


def greet(dp_masks):
    me, group = lax.axis_index("head"), lax.axis_index("dp")
    barrier = pltpu.get_barrier_semaphore()
    for mask in (1, 2):
        pl.semaphore_signal(
            barrier, inc=1, device_id={"head": partner(me, mask)}, device_id_type=MESH
        )
    for mask in dp_masks:
        pl.semaphore_signal(
            barrier, inc=1, device_id={"dp": partner(group, mask)}, device_id_type=MESH
        )
    pl.semaphore_wait(barrier, 2 + len(dp_masks))


def at_rows(r, block=SHORT):
    return pl.ds(pl.multiple_of(r * block, block), block)


def at_cols(k, width):
    return pl.ds(pl.multiple_of(k * width, width), width)


class HeadGather:
    def __init__(self, own, full, width, sems):
        self.own, self.full, self.width = own, full, width
        self.me = lax.axis_index("head")
        self.core, self.chip = partner(self.me, 1), partner(self.me, 2)
        self.far = partner(self.core, 2)
        self.sems = sems

    def slot(self, r, who):
        return self.full.at[at_rows(r), at_cols(who, self.width)]

    def copy(self, r, src, owner, kind, **where):
        return send_to(
            src, self.slot(r, owner), self.sems.at[2 * kind, r], self.sems.at[2 * kind + 1, r], **where
        )

    def own_src(self, r):
        return self.own(r) if self.own is not None else self.slot(r, self.me)

    def start(self, r):
        self.copy(r, self.own_src(r), self.me, 0, head=self.chip).start()
        self.copy(r, self.own_src(r), self.me, 1, head=self.core).start()

    def forward(self, r):
        self.copy(r, self.slot(r, self.chip), self.chip, 0, head=self.chip).wait_recv()
        self.copy(r, self.slot(r, self.chip), self.chip, 2, head=self.core).start()

    def arrive(self, r):
        self.copy(r, self.slot(r, self.core), self.core, 1, head=self.core).wait_recv()
        self.copy(r, self.slot(r, self.far), self.far, 2, head=self.core).wait_recv()

    def sent(self, r):
        self.copy(r, self.own_src(r), self.me, 0, head=self.chip).wait_send()
        self.copy(r, self.own_src(r), self.me, 1, head=self.core).wait_send()
        self.copy(r, self.slot(r, self.chip), self.chip, 2, head=self.core).wait_send()


class DpSpread:
    def __init__(self, own, slot_of, masks, send, recv):
        self.own, self.slot_of, self.masks = own, slot_of, masks
        self.group = lax.axis_index("dp")
        self.send, self.recv = send, recv
        held, self.plan, at = [0], [], 0
        for mask in self.masks:
            self.plan.append((mask, [(k, at + p) for p, k in enumerate(held)]))
            at += len(held)
            held = held + [k ^ mask for k in held]

    def block(self, k):
        who = self.group
        for mask in self.masks:
            if k & mask:
                who = partner(who, mask)
        return self.slot_of(who)

    def copies(self, step, there):
        mask, items = self.plan[step]
        out = []
        for k, sem in items:
            if there:
                src, at = (self.own if k == 0 else self.block(k)), self.block(k)
            else:
                src = at = self.block(k ^ mask)
            out.append(
                send_to(src, at, self.send.at[sem], self.recv.at[sem], dp=partner(self.group, mask))
            )
        return out

    def start(self, step):
        for copy in self.copies(step, True):
            copy.start()

    def arrive(self, step):
        for copy in self.copies(step, False):
            copy.wait_recv()

    def sent(self):
        for step in range(len(self.plan)):
            for copy in self.copies(step, True):
                copy.wait_send()


def head_slopes(me, heads, n_head=4):
    slopes = []
    for h in range(heads):
        value = jnp.float32(0.0)
        for k in range(n_head):
            value = jnp.where(me == k, jnp.float32(2.0 ** (-8.0 * (k * heads + h + 1) / HEADS)), value)
        slopes.append(value)
    return slopes


def first_kernel(
    masks, gather,
    kind, layer_in, wq, wk, wv, gain, shift, bias_expand, w_proj, w_expand, w_reduce,
    x_out, a_out, normed_out, qkv_out, proj_out, expand_out, reduce_out, bias_out, logsum,
    x_buf, normed_buf, qkv_buf, a_buf, bias_buf, total, x_sems, a_sems, p_sems, local_sems, copy_sems,
    e_send, e_recv, r_send, r_recv, b_send, b_recv, q_send, q_recv,
):
    rows, width = layer_in.shape
    features = 4 * width
    block = SHORT
    n = rows // block
    heads = width // HEAD_DIM
    me, group = lax.axis_index("head"), lax.axis_index("dp")
    core, chip = partner(me, 1), partner(me, 2)
    greet(masks if gather else [])

    x_gather = HeadGather(None, x_buf, width, x_sems)
    a_gather = HeadGather(lambda r: a_buf.at[at_rows(r), :], a_out, width, a_sems)

    def p_copy(src, owner, k, **where):
        return send_to(src, proj_out.at[at_cols(owner, width), :], p_sems.at[2 * k], p_sems.at[2 * k + 1], **where)

    piece = width // (1 << len(masks))

    def p_rows(owner, k):
        return proj_out.at[pl.ds(pl.multiple_of(owner * width + k * piece, piece), piece), :]

    def p_piece(owner, to):
        return send_to(
            w_proj.at[pl.ds(pl.multiple_of(group * piece, piece), piece), :], p_rows(owner, group),
            p_sems.at[0], p_sems.at[1], head=to,
        )

    far_rows = DpSpread(p_rows(chip, group), lambda k: p_rows(chip, k), masks[::-1], q_send, q_recv)

    if gather:
        bias_buf[...] = jnp.broadcast_to(bias_expand[...], bias_buf.shape)

        def columns_of(ref):
            return lambda k: ref.at[:, at_cols(k, w_expand.shape[1])]

        far_first, near_first = masks[::-1], masks[:1] + masks[1:][::-1]
        expand = DpSpread(w_expand, columns_of(expand_out), far_first, e_send, e_recv)
        bias = DpSpread(bias_buf, columns_of(bias_out), far_first, b_send, b_recv)
        reduce = DpSpread(w_reduce, columns_of(reduce_out), near_first, r_send, r_recv)
        expand.start(0)
        bias.start(0)
        reduce.start(0)

    def own_chunk(r):
        x_buf[at_rows(r), at_cols(me, width)] = layer_in[at_rows(r), :].astype(bf16)
        x_gather.start(r)

    if gather:
        p_piece(me, chip).start()
        p_copy(w_proj, me, 1, head=core).start()
    own_chunk(0)
    own_chunk(1)
    own_chunk(2)
    keeps = [pltpu.make_async_copy(w_proj, proj_out.at[at_cols(me, width), :], local_sems.at[0])]
    if gather:
        own_cols = at_cols(group, w_expand.shape[1])
        keeps.append(pltpu.make_async_copy(w_expand, expand_out.at[:, own_cols], local_sems.at[1]))
        keeps.append(pltpu.make_async_copy(w_reduce, reduce_out.at[:, own_cols], local_sems.at[2]))
        keeps.append(pltpu.make_async_copy(bias_buf, bias_out.at[:, own_cols], local_sems.at[3]))
    for keep in keeps:
        keep.start()

    slopes = [s * LOG2E for s in head_slopes(me, heads)]
    apart = (1 - kind[0]).astype(f32) * masked_value
    key_place = lax.broadcasted_iota(jnp.int32, (block, block), 0)
    query_place = lax.broadcasted_iota(jnp.int32, (block, block), 1)

    def normed_copy(r):
        return pltpu.make_async_copy(normed_buf.at[r % 2], normed_out.at[at_rows(r), :], copy_sems.at[0, r])

    def x_copy(r):
        return pltpu.make_async_copy(x_buf.at[at_rows(r), :], x_out.at[at_rows(r), :], copy_sems.at[1, r])

    def qkv_copy(r):
        return pltpu.make_async_copy(qkv_buf.at[at_rows(r), :], qkv_out.at[at_rows(r), :], copy_sems.at[2, r])

    def a_copy(r):
        return pltpu.make_async_copy(
            a_buf.at[at_rows(r), :], a_out.at[at_rows(r), at_cols(me, width)], copy_sems.at[3, r]
        )

    def chunk(i):
        x_gather.arrive(i)
        x_copy(i).start()
        x = x_buf[at_rows(i), :].astype(f32)
        centre = x - jnp.sum(x, axis=1, keepdims=True) * (1.0 / features)
        spread = jnp.sum(centre * centre, axis=1, keepdims=True) * (1.0 / features)
        low = (centre * lax.rsqrt(spread + eps) * gain[...] + shift[...]).astype(bf16)

        @pl.when(i >= 2)
        def _():
            normed_copy(i - 2).wait()

        normed_buf[i % 2] = low
        normed_copy(i).start()
        for k, w in enumerate((wq, wk, wv)):
            qkv_buf[at_rows(i), k * width : (k + 1) * width] = dot(low, w[...]).astype(bf16)
        qkv_copy(i).start()

        def scores(h, j):
            q = qkv_buf[at_rows(i), h * HEAD_DIM : (h + 1) * HEAD_DIM]
            k = qkv_buf[at_rows(j), width + h * HEAD_DIM : width + (h + 1) * HEAD_DIM]
            v = qkv_buf[at_rows(j), 2 * width + h * HEAD_DIM : 2 * width + (h + 1) * HEAD_DIM]
            place = (key_place + (j - i) * block).astype(f32) * slopes[h]
            return dot(k, q, NT) * (SCALE * LOG2E) + place, v

        carry = []
        for h in range(heads):
            s, v = scores(h, i)
            s = jnp.where(key_place <= query_place, s, masked_value)
            m = jnp.max(s, axis=0, keepdims=True)
            p = jnp.exp2(s - m)
            carry += [m, jnp.sum(p, axis=0, keepdims=True)]
            total[h] = dot(v, p.astype(bf16), TN)

        def step(j, carry):
            new = []
            for h in range(heads):
                m, l = carry[2 * h], carry[2 * h + 1]
                s, v = scores(h, j)
                s = s + apart
                m_new = jnp.maximum(m, jnp.max(s, axis=0, keepdims=True))
                p = jnp.exp2(s - m_new)
                fade = jnp.exp2(m - m_new)
                new += [m_new, l * fade + jnp.sum(p, axis=0, keepdims=True)]
                total[h] = total[h] * fade + dot(v, p.astype(bf16), TN)
            return tuple(new)

        carry = lax.fori_loop(0, i, step, tuple(carry))
        for h in range(heads):
            m, l = carry[2 * h], carry[2 * h + 1]
            a_buf[at_rows(i), h * HEAD_DIM : (h + 1) * HEAD_DIM] = (total[h] * (1.0 / l)).T.astype(bf16)
            logsum[i, h : h + 1, :] = m + jnp.log(l) * LOG2E
        a_gather.start(i)
        a_copy(i).start()

    steps = len(masks)

    def body(r, _):
        @pl.when(r < n)
        def _():
            x_gather.forward(r)

            @pl.when(r + 3 < n)
            def _():
                own_chunk(r + 3)

            if not gather:
                @pl.when(r + 2 == n)
                def _():
                    p_copy(w_proj, me, 0, head=chip).start()
                    p_copy(w_proj, me, 1, head=core).start()

        if gather:
            @pl.when(r == 2)
            def _():
                p_piece(chip, chip).wait_recv()
                far_rows.start(0)

            for s in range(1, steps):
                @pl.when(r == min(s + 3, n))
                def _(s=s):
                    far_rows.arrive(s - 1)
                    far_rows.start(s)

                @pl.when(r == min(2 * s + 1, n - 1))
                def _(s=s):
                    expand.arrive(s - 1)
                    bias.arrive(s - 1)
                    expand.start(s)
                    bias.start(s)

                @pl.when(r == min(4 * s - 3, n))
                def _(s=s):
                    reduce.arrive(s - 1)
                    reduce.start(s)

        @pl.when(r >= 1)
        def _():
            chunk(r - 1)

        return 0

    lax.fori_loop(0, n + 1, body, 0)

    if gather:
        far_rows.arrive(steps - 1)
    else:
        p_copy(w_proj, chip, 0, head=chip).wait_recv()
    p_forward = p_copy(proj_out.at[at_cols(chip, width), :], chip, 2, head=core)
    p_forward.start()

    def pass_on(r, _):
        a_gather.forward(r)
        return 0

    lax.fori_loop(0, n, pass_on, 0)

    def settle(r, _):
        a_gather.arrive(r)
        a_gather.sent(r)
        x_gather.sent(r)
        x_copy(r).wait()
        qkv_copy(r).wait()
        a_copy(r).wait()

        @pl.when(r >= n - 2)
        def _():
            normed_copy(r).wait()

        return 0

    lax.fori_loop(0, n, settle, 0)
    p_copy(w_proj, core, 1, head=core).wait_recv()
    p_copy(w_proj, partner(core, 2), 2, head=core).wait_recv()
    if gather:
        p_piece(me, chip).wait_send()
        far_rows.sent()
    else:
        p_copy(w_proj, me, 0, head=chip).wait_send()
    p_copy(w_proj, me, 1, head=core).wait_send()
    p_forward.wait_send()
    for keep in keeps:
        keep.wait()
    if gather:
        expand.arrive(steps - 1)
        reduce.arrive(steps - 1)
        bias.arrive(steps - 1)
        expand.sent()
        reduce.sent()
        bias.sent()


def first(kind, layer_in, wq, wk, wv, gain, shift, bias_expand, w_proj, w_expand, w_reduce, dp_size):
    rows, width = layer_in.shape
    features = 4 * width
    block = SHORT
    n = rows // block
    heads = width // HEAD_DIM
    masks = masks_of(dp_size)
    local = w_expand.shape[1]
    gather = local % 128 == 0 and (width // dp_size) % 16 == 0
    units = local * dp_size if gather else 128
    any_spec = pl.BlockSpec(memory_space=pl.ANY)
    vmem = pl.BlockSpec(memory_space=pltpu.VMEM)
    blocks = max(dp_size - 1, 1)
    outs = pl.pallas_call(
        functools.partial(first_kernel, masks, gather),
        in_specs=[pl.BlockSpec(memory_space=pltpu.SMEM)] + [vmem] * 7 + [any_spec] * 3,
        out_specs=[any_spec] * 8 + [vmem],
        out_shape=[
            jax.ShapeDtypeStruct((rows, features), bf16),
            jax.ShapeDtypeStruct((rows, features), bf16),
            jax.ShapeDtypeStruct((rows, features), bf16),
            jax.ShapeDtypeStruct((rows, 3 * width), bf16),
            jax.ShapeDtypeStruct((features, features), bf16),
            jax.ShapeDtypeStruct((features, units), bf16),
            jax.ShapeDtypeStruct((features, units), bf16),
            jax.ShapeDtypeStruct((16, units), bf16),
            jax.ShapeDtypeStruct((n, heads, block), f32),
        ],
        scratch_shapes=[
            pltpu.VMEM((rows, features), bf16),
            pltpu.VMEM((2, block, features), bf16),
            pltpu.VMEM((rows, 3 * width), bf16),
            pltpu.VMEM((rows, width), bf16),
            pltpu.VMEM((16, local), bf16),
            pltpu.VMEM((heads, HEAD_DIM, block), f32),
            pltpu.SemaphoreType.DMA((6, n)),
            pltpu.SemaphoreType.DMA((6, n)),
            pltpu.SemaphoreType.DMA((6,)),
            pltpu.SemaphoreType.DMA((4,)),
            pltpu.SemaphoreType.DMA((4, n)),
        ]
        + [pltpu.SemaphoreType.DMA((blocks,))] * 8,
        compiler_params=pltpu.CompilerParams(
            vmem_limit_bytes=56 * MIB, collective_id=0, has_side_effects=True
        ),
    )(kind, layer_in, wq, wk, wv, gain, shift, bias_expand, w_proj, w_expand, w_reduce)
    x, a, normed, qkv, proj, expand, reduce, bias, logsum = outs
    if not gather:
        bias = jnp.broadcast_to(lax.all_gather(bias_expand, "dp", axis=1, tiled=True), (16, local * dp_size))
        expand = lax.all_gather(w_expand, "dp", axis=1, tiled=True)
        reduce = lax.all_gather(w_reduce, "dp", axis=1, tiled=True)
    return x, a, normed, qkv, proj, expand, reduce, bias, logsum


class HeadScatter:
    def __init__(self, width, src, from_core, far, near, from_chip, sems):
        self.width, self.src, self.from_core, self.far = width, src, from_core, far
        self.near, self.from_chip, self.sems = near, from_chip, sems
        self.me = lax.axis_index("head")
        self.core, self.chip = partner(self.me, 1), partner(self.me, 2)

    def to_core(self, r, k):
        who = self.core if k == 0 else partner(self.core, 2)
        return send_to(
            self.src(r).at[:, at_cols(who, self.width)],
            self.from_core.at[at_rows(r), k * self.width : (k + 1) * self.width],
            self.sems.at[2 * k, r],
            self.sems.at[2 * k + 1, r],
            head=self.core,
        )

    def to_chip(self, r):
        return send_to(
            self.far.at[r % 2],
            self.from_chip.at[at_rows(r), :],
            self.sems.at[4, r],
            self.sems.at[5, r],
            head=self.chip,
        )

    def start(self, r):
        self.to_core(r, 1).start()
        self.to_core(r, 0).start()

    def middle(self, r):
        src = self.src(r)
        self.to_core(r, 1).wait()
        self.far[r % 2] = (
            src[:, at_cols(self.chip, self.width)].astype(f32)
            + self.from_core[at_rows(r), self.width :].astype(f32)
        ).astype(bf16)
        self.to_chip(r).start()
        self.to_core(r, 0).wait()
        self.near[r % 2] = (
            src[:, at_cols(self.me, self.width)].astype(f32)
            + self.from_core[at_rows(r), : self.width].astype(f32)
        )

    def finish(self, r):
        self.to_chip(r).wait()
        return self.near[r % 2] + self.from_chip[at_rows(r), :].astype(f32)


GELU_C = 0.7978845608028654


def second_kernel(
    x_in, a_in, layer_in, w_proj_in, w_expand_in, w_reduce_in, grad_out, gain, shift, bias,
    grad_heads, grad_hid_out, ffn_out, hid_own, wide_out, narrow_out, proj_out, sums, grad_bias, grad_bias_reduce,
    g_buf, x_buf, a_buf, hid_buf, own_buf, ffn_buf, gh_buf, from_core, far_buf, near_buf, from_chip, wide, narrow, proj,
    w_proj, w_expand, w_reduce, in_buf, g_sems, s_sems, copy_sems, final_sems, load_sems,
):
    rows, width = layer_in.shape
    features = 4 * width
    block = SHORT
    n = rows // block
    me = lax.axis_index("head")
    greet([])

    g_gather = HeadGather(None, g_buf, width, g_sems)
    scatter = HeadScatter(width, lambda r: gh_buf.at[r % 2], from_core, far_buf, near_buf, from_chip, s_sems)

    def own_chunk(r):
        chunk = grad_out[at_rows(r), :]
        g_buf[at_rows(r), at_cols(me, width)] = chunk.astype(bf16)
        g_gather.start(r)
        return chunk

    loads = [
        pltpu.make_async_copy(src, dst, load_sems.at[k])
        for k, (src, dst) in enumerate(
            ((w_proj_in, w_proj), (w_expand_in, w_expand), (w_reduce_in, w_reduce))
        )
    ]

    def load_in(r):
        return pltpu.make_async_copy(layer_in.at[at_rows(r), :], in_buf.at[r % 2], copy_sems.at[5, r])

    def load_x(r):
        return pltpu.make_async_copy(x_in.at[at_rows(r), :], x_buf.at[r % 2], copy_sems.at[0, r])

    def load_a(r):
        return pltpu.make_async_copy(a_in.at[at_rows(r), :], a_buf.at[r % 2], copy_sems.at[1, r])

    def store_hid(r):
        return pltpu.make_async_copy(hid_buf.at[r % 2], grad_hid_out.at[at_rows(r), :], copy_sems.at[2, r])

    def store_ffn(r):
        return pltpu.make_async_copy(ffn_buf.at[r % 2], ffn_out.at[at_rows(r), :], copy_sems.at[3, r])

    def store_own(r):
        return pltpu.make_async_copy(own_buf.at[r % 2], hid_own.at[at_rows(r), :], copy_sems.at[4, r])

    def final(k, slot, buf, out):
        half = features // 2
        return pltpu.make_async_copy(
            buf.at[slot], out.at[slot * half : (slot + 1) * half, :], final_sems.at[k, slot]
        )

    own_chunk(0)
    own_chunk(1)
    load_a(0).start()
    loads[0].start()
    load_x(0).start()
    load_in(0).start()
    loads[1].start()
    loads[2].start()
    wide[...] = jnp.zeros_like(wide)
    narrow[...] = jnp.zeros_like(narrow)
    proj[...] = jnp.zeros_like(proj)
    sums[...] = jnp.zeros_like(sums)
    grad_bias[...] = jnp.zeros_like(grad_bias)
    grad_bias_reduce[...] = jnp.sum(grad_out[...], axis=0, keepdims=True)

    def body(r, _):
        g_gather.forward(r)

        @pl.when(r + 2 < n)
        def _():
            own_chunk(r + 2)

        load_x(r).wait()
        load_a(r).wait()
        load_in(r).wait()

        @pl.when(r == 0)
        def _():
            loads[0].wait()

        @pl.when(r + 1 < n)
        def _():
            load_x(r + 1).start()
            load_a(r + 1).start()
            load_in(r + 1).start()

        @pl.when(r >= 2)
        def _():
            store_hid(r - 2).wait()
            store_ffn(r - 2).wait()
            store_own(r - 2).wait()

        slot = r % 2
        a = a_buf[slot]
        attn = dot(a, w_proj[...])
        hidden = attn + x_buf[slot].astype(f32)
        own = attn[:, 0:width]
        for k in range(1, 4):
            own = jnp.where(me == k, attn[:, k * width : (k + 1) * width], own)
        own_buf[slot] = own + in_buf[slot]
        store_own(r).start()
        centre = hidden - jnp.sum(hidden, axis=1, keepdims=True) * (1.0 / features)
        spread = jnp.sum(centre * centre, axis=1, keepdims=True) * (1.0 / features)
        scale = lax.rsqrt(spread + eps)
        centred = centre * scale
        low = (centred * gain[...] + shift[...]).astype(bf16)

        @pl.when(r == 0)
        def _():
            loads[1].wait()
            loads[2].wait()

        z = dot(low, w_expand[...]) + bias[0:1, :].astype(f32)
        z2 = z * z
        t = jnp.tanh(z * (GELU_C + (GELU_C * 0.044715) * z2))
        half = 0.5 + 0.5 * t
        activated = (z * half).astype(bf16)
        slope = half + (0.5 * z) * (1.0 - t * t) * (GELU_C + (3.0 * GELU_C * 0.044715) * z2)
        g_gather.arrive(r)
        g = g_buf[at_rows(r), :]
        gp = slope * dot(g, w_reduce[...])
        gp_low = gp.astype(bf16)
        gn = dot(gp_low, w_expand[...], NT)
        scaled = gn * gain[...]
        mean_scaled = jnp.sum(scaled, axis=1, keepdims=True) * (1.0 / features)
        mean_both = jnp.sum(scaled * centred, axis=1, keepdims=True) * (1.0 / features)
        back = (scaled - mean_scaled - centred * mean_both) * scale
        back_low = (back + 0.25 * g.astype(f32)).astype(bf16)
        hid_buf[slot] = back_low
        store_hid(r).start()
        gh_buf[slot] = dot(back_low, w_proj[...], NT).astype(bf16)
        scatter.start(r)
        sums[0:1, :] += jnp.sum(gn * centred, axis=0, keepdims=True)
        sums[1:2, :] += jnp.sum(gn, axis=0, keepdims=True)
        grad_bias[...] += jnp.sum(gp_low.astype(f32), axis=0, keepdims=True)
        ffn_buf[slot] = dot(activated, w_reduce[...], NT).astype(bf16)
        store_ffn(r).start()
        wide[...] += dot(low, gp_low, TN)
        scatter.middle(r)
        narrow[...] += dot(g, activated, TN)
        proj[...] += dot(back_low, a, TN)

        @pl.when(r >= 1)
        def _():
            grad_heads[at_rows(r - 1), :] = scatter.finish(r - 1).astype(bf16)

        return 0

    lax.fori_loop(0, n, body, 0)
    for k, (full, buf, out) in enumerate(
        ((wide, ffn_buf, wide_out), (narrow, x_buf, narrow_out), (proj, hid_buf, proj_out))
    ):
        for p in range(2):
            if buf is ffn_buf:
                store_ffn(n - 2 + p).wait()
            if buf is hid_buf:
                store_hid(n - 2 + p).wait()
            half = features // 2
            slot = (n - 2 + p) % 2
            buf[slot] = full[slot * half : (slot + 1) * half, :].astype(bf16)
            final(k, slot, buf, out).start()
    grad_heads[at_rows(n - 1), :] = scatter.finish(n - 1).astype(bf16)
    for k, (buf, out) in enumerate(((ffn_buf, wide_out), (x_buf, narrow_out), (hid_buf, proj_out))):
        for slot in range(2):
            final(k, slot, buf, out).wait()

    def settle(r, _):
        g_gather.sent(r)

        @pl.when(r >= n - 2)
        def _():
            store_own(r).wait()

        return 0

    lax.fori_loop(0, n, settle, 0)


def second(x, a, grad_out, layer_in, w_proj, w_expand, w_reduce, gain, shift, bias):
    rows, width = layer_in.shape
    features = 4 * width
    units = w_expand.shape[1]
    block = SHORT
    n = rows // block
    any_spec = pl.BlockSpec(memory_space=pl.ANY)
    vmem = pl.BlockSpec(memory_space=pltpu.VMEM)
    return pl.pallas_call(
        second_kernel,
        in_specs=[any_spec] * 6 + [vmem] * 4,
        out_specs=[vmem] + [any_spec] * 6 + [vmem] * 3,
        out_shape=[
            jax.ShapeDtypeStruct((rows, width), bf16),
            jax.ShapeDtypeStruct((rows, features), bf16),
            jax.ShapeDtypeStruct((rows, features), bf16),
            jax.ShapeDtypeStruct((rows, width), f32),
            jax.ShapeDtypeStruct((features, units), bf16),
            jax.ShapeDtypeStruct((features, units), bf16),
            jax.ShapeDtypeStruct((features, features), bf16),
            jax.ShapeDtypeStruct((2, features), f32),
            jax.ShapeDtypeStruct((1, units), f32),
            jax.ShapeDtypeStruct((1, width), f32),
        ],
        scratch_shapes=[
            pltpu.VMEM((rows, features), bf16),
            pltpu.VMEM((2, block, features), bf16),
            pltpu.VMEM((2, block, features), bf16),
            pltpu.VMEM((2, block, features), bf16),
            pltpu.VMEM((2, block, width), f32),
            pltpu.VMEM((2, block, features), bf16),
            pltpu.VMEM((2, block, features), bf16),
            pltpu.VMEM((rows, 2 * width), bf16),
            pltpu.VMEM((2, block, width), bf16),
            pltpu.VMEM((2, block, width), f32),
            pltpu.VMEM((rows, width), bf16),
            pltpu.VMEM((features, units), f32),
            pltpu.VMEM((features, units), f32),
            pltpu.VMEM((features, features), f32),
            pltpu.VMEM((features, features), bf16),
            pltpu.VMEM((features, units), bf16),
            pltpu.VMEM((features, units), bf16),
            pltpu.VMEM((2, block, width), f32),
            pltpu.SemaphoreType.DMA((6, n)),
            pltpu.SemaphoreType.DMA((6, n)),
            pltpu.SemaphoreType.DMA((6, n)),
            pltpu.SemaphoreType.DMA((3, 2)),
            pltpu.SemaphoreType.DMA((3,)),
        ],
        compiler_params=pltpu.CompilerParams(
            vmem_limit_bytes=62 * MIB, collective_id=1, has_side_effects=True
        ),
    )(x, a, layer_in, w_proj, w_expand, w_reduce, grad_out, gain, shift, bias)


EARLY = 0
TIMES = {
    "start": 25.4,
    "middle": (8.4, 12.6, 20.2, 21.1, 21.7, 26.6, 31.4, 38.8),
    "finish": (15.8, 22.4, 56.4, 76.2, 79.1, 82.6, 86.4, 87.9),
    "wide": (59.1, 71.4, 94.0),
    "narrow": (33.3, 51.5, 80.5),
    "proj": (36.2, 40.5, 49.8, 56.8, 66.6, 82.7),
    "first": (44.3, 56.8, 61.0, 67.5, 74.8, 81.6),
    "first_turned": (39.4, 47.3, 60.2, 69.7, 69.7, 86.4),
    "second": (56.5, 60.1, 68.3, 72.2, 74.9, 312.3),
    "second_turned": (61.0, 63.4, 68.6, 72.3, 78.2, 407.9),
    "small": (73.9, 74.9, 76.7, 77.5, 78.5),
}


class DpScatter:
    def __init__(self, part, recv_buf, masks, send, recv, first_part=None):
        self.part, self.recv_buf, self.masks = part, recv_buf, masks
        self.first_part = first_part or part
        self.group = lax.axis_index("dp")
        self.send, self.recv = send, recv
        size = 1 << len(masks)
        left, at = list(range(size)), 0
        self.plan = []
        for mask in masks:
            mine = [k for k in left if not k & mask]
            self.plan.append((mask, [(k, at + p) for p, k in enumerate(mine)]))
            at += len(mine)
            left = mine

    def where(self, k, part):
        who = self.group
        for mask in self.masks:
            if k & mask:
                who = partner(who, mask)
        return part(who)

    def copy(self, mask, k, slot):
        part = self.first_part if mask == self.masks[0] else self.part
        return send_to(
            self.where(k ^ mask, part), self.recv_buf.at[slot], self.send.at[slot], self.recv.at[slot],
            dp=partner(self.group, mask),
        )

    def start(self, step):
        mask, items = self.plan[step]
        for k, slot in items:
            self.copy(mask, k, slot).start()

    def arrive(self, step):
        mask, items = self.plan[step]
        for k, slot in items:
            self.copy(mask, k, slot).wait_recv()
            ref = self.where(k, self.part)
            ref[...] = (ref[...].astype(f32) + self.recv_buf[slot].astype(f32)).astype(bf16)

    def sent(self):
        for mask, items in self.plan:
            for k, slot in items:
                self.copy(mask, k, slot).wait_send()


class DpSum:
    def __init__(self, buf, recv_buf, out, masks, sems, keep_sem):
        size = 1 << len(masks)
        rows = buf.shape[0] // size
        self.steps = len(masks)
        self.scatter = DpScatter(lambda k: buf.at[at_rows(k, rows), :], recv_buf, masks, sems.at[0], sems.at[1])
        me = lax.axis_index("dp")
        own = buf.at[at_rows(me, rows), :]
        self.keep = pltpu.make_async_copy(own, out.at[at_rows(me, rows), :], keep_sem)
        self.spread = DpSpread(
            own, lambda k: out.at[at_rows(k, rows), :], masks[::-1], sems.at[2], sems.at[3]
        )

    def start(self):
        self.scatter.start(0)

    def advance(self, step):
        if step < self.steps:
            self.scatter.arrive(step)
            if step + 1 < self.steps:
                self.scatter.start(step + 1)
            else:
                self.keep.start()
                self.spread.start(0)
        else:
            self.spread.arrive(step - self.steps)
            if step + 1 < 2 * self.steps:
                self.spread.start(step - self.steps + 1)

    def settle(self):
        self.scatter.sent()
        self.spread.sent()
        self.keep.wait()


class HeadSum:
    def __init__(self, width, src, mine, from_core, from_chip, sems):
        self.width, self.src, self.mine = width, src, mine
        self.from_core, self.from_chip, self.sems = from_core, from_chip, sems
        self.me = lax.axis_index("head")
        self.core, self.chip = partner(self.me, 1), partner(self.me, 2)

    def place(self, r, k):
        return self.from_core.at[at_rows(r), k * self.width : (k + 1) * self.width]

    def to_core(self, r, k):
        who = self.core if k == 0 else partner(self.core, 2)
        return send_to(
            self.src(r).at[:, at_cols(who, self.width)], self.place(r, k),
            self.sems.at[2 * k, r], self.sems.at[2 * k + 1, r], head=self.core,
        )

    def to_chip(self, r):
        return send_to(
            self.place(r, 1), self.from_chip.at[at_rows(r), :], self.sems.at[4, r], self.sems.at[5, r], head=self.chip
        )

    def start(self, r):
        self.to_core(r, 1).start()
        self.to_core(r, 0).start()

    def middle(self, r):
        for k, who in ((1, self.chip), (0, self.me)):
            self.to_core(r, k).wait()
            place = self.place(r, k)
            place[...] = (self.mine(r, who, k) + place[...].astype(f32)).astype(bf16)
            if k == 1:
                self.to_chip(r).start()

    def finish(self, r):
        self.to_chip(r).wait()
        return self.place(r, 0)[...].astype(f32) + self.from_chip[at_rows(r), :].astype(f32)


def third_kernel(
    masks, scatter_inside,
    kind, qkv_in, grad_heads, logsum, wq_in, wk_in, wv_in, gain, sums_2, grad_bias, grad_bias_reduce,
    wide_in, narrow_in, a_in, x_in, normed_in, grad_hid, ffn, proj,
    ffn_sum, total_sum, sum_p, sum_a, sum_b, wide_sum, narrow_sum, small,
    dqkv, dk_acc, dv_acc, dq_acc, delta, wgrad, slots, wide, narrow, pay_p, pay_a, pay_b,
    recv_p, recv_a, recv_b, recv_w, recv_n,
    s_core, s_chip, s_mine, s_out, f_src, f_core, f_chip, f_slots, small_recv,
    wg_sems, s_sems, mine_sems, out_sems, f_sems, p_sems, a_sems, b_sems, w_sems, n_sems, slot_sems, keep_sems, small_sems, total_sems,
    qkv, wq, wk, wv, in_sems,
):
    rows = qkv.shape[0]
    width = grad_heads.shape[1]
    features = x_in.shape[1]
    block = SHORT
    n = rows // block
    heads = width // HEAD_DIM
    me = lax.axis_index("head")
    group = lax.axis_index("dp")
    steps = len(masks)
    greet(masks)

    agenda = []

    def due(time, action, *args):
        agenda.append((time, len(agenda), functools.partial(action, *args)))

    turned = masks[1:2] + masks[:1] + masks[2:]

    if scatter_inside:
        local = wide_sum.shape[1]

        def columns_of(ref):
            return lambda k: ref.at[:, at_cols(k, local)]

        wide_rs = DpScatter(columns_of(wide), recv_w, masks, w_sems.at[0], w_sems.at[1], columns_of(wide_in))
        narrow_rs = DpScatter(columns_of(narrow), recv_n, turned, n_sems.at[0], n_sems.at[1], columns_of(narrow_in))
        wide_rs.start(0)
        narrow_rs.start(0)
        loads = [
            pltpu.make_async_copy(wide_in, wide, keep_sems.at[5]),
            pltpu.make_async_copy(narrow_in, narrow, keep_sems.at[6]),
        ]

        def scatter_step(scatter, load, out, s):
            if s == 0:
                load.wait()
            scatter.arrive(s)
            if s + 1 < steps:
                scatter.start(s + 1)
            else:
                out[...] = scatter.part(group)[...].astype(f32)

        for s in range(steps):
            due(TIMES["wide"][min(s, 2)] + max(s - 2, 0), scatter_step, wide_rs, loads[0], wide_sum, s)
            due(TIMES["narrow"][min(s, 2)] + max(s - 2, 0), scatter_step, narrow_rs, loads[1], narrow_sum, s)

    n_proj = features // block
    n_side = n_proj + n

    def side_src(c):
        return proj.at[at_rows(c), :] if c < n_proj else ffn.at[at_rows(c - n_proj), :]

    def side_load(c, k):
        who = me if k == 0 else partner(me, 2)
        return pltpu.make_async_copy(
            side_src(c).at[:, at_cols(who, width)], s_mine.at[c % 4, k], mine_sems.at[k, c]
        )

    def side_mine(c, who, k):
        side_load(c, k).wait()
        return s_mine[c % 4, k].astype(f32)

    side = HeadSum(width, side_src, side_mine, s_core, s_chip, s_sems)

    def side_copy(c):
        return pltpu.make_async_copy(s_out.at[c % 2], ffn_sum.at[at_rows(c - n_proj), :], out_sems.at[c])

    def side_start(c):
        side_load(c, 1).start()
        side_load(c, 0).start()

    def side_middle(c):
        side.middle(c)
        if c + 4 < n_side:
            side_start(c + 4)

    def side_finish(c):
        value = side.finish(c).astype(bf16)
        if c < n_proj:
            pay_p[c * block : (c + 1) * block, :] = value
        else:
            if c - 2 >= n_proj:
                side_copy(c - 2).wait()
            s_out[c % 2] = value
            side_copy(c).start()

    for c in range(min(4, n_side)):
        side_start(c)
    for c in range(n_side):
        side.start(c)
        due(TIMES["middle"][min(c, 7)] + 6 * max(c - 7, 0), side_middle, c)
        due(TIMES["finish"][min(c, 7)] + 6 * max(c - 7, 0), side_finish, c)
    if scatter_inside:
        for load in loads:
            load.start()

    proj_sum = DpSum(pay_p, recv_p, sum_p, masks, p_sems, keep_sems.at[0])
    first_sums, second_sums = [], []
    halves = 2 if features % (32 << steps) == 0 else 1
    for p in range(halves):
        at = slice(p * features // halves, (p + 1) * features // halves)
        first_sums.append(
            DpSum(pay_a.at[at], recv_a.at[p], sum_a.at[at], (turned, masks)[p], a_sems.at[p], keep_sems.at[1 + 2 * p])
        )
        second_sums.append(
            DpSum(pay_b.at[at], recv_b.at[p], sum_b.at[at], (masks, turned)[p], b_sems.at[p], keep_sems.at[2 + 2 * p])
        )
    due(TIMES["start"], proj_sum.start)
    for which, times in (
        [(proj_sum, TIMES["proj"])]
        + list(zip(first_sums, (TIMES["first"], TIMES["first_turned"])))
        + list(zip(second_sums, (TIMES["second"], TIMES["second_turned"])))
    ):
        for s in range(2 * steps):
            due(times[min(s * 3 // steps, 5)] + 0.01 * s, which.advance, s)

    apart = (1 - kind[0]).astype(f32) * masked_value
    slopes = [s * LOG2E for s in head_slopes(me, heads)]
    two = 2 * block
    pairs = rows // two
    attended = pltpu.make_async_copy(a_in.at[:, at_cols(me, width)], dqkv.at[:, 0:width], wg_sems.at[2])
    attended.start()
    ahead = [
        pltpu.make_async_copy(src, dst, in_sems.at[k])
        for k, (src, dst) in enumerate(((qkv_in, qkv), (wq_in, wq), (wk_in, wk), (wv_in, wv)))
    ]
    for load in ahead:
        load.start()
    attended.wait()

    def fill(i, _):
        for h in range(heads):
            cols = slice(h * HEAD_DIM, (h + 1) * HEAD_DIM)
            both = grad_heads[at_rows(i), cols].astype(f32) * dqkv[at_rows(i), cols].astype(f32)
            delta[i, h : h + 1, :] = jnp.sum(both.T, axis=0, keepdims=True)
        return 0

    lax.fori_loop(0, n, fill, 0)
    for load in ahead:
        load.wait()

    def load_normed(h, m):
        at = (h * pairs + pairs - 1 - m) % 2
        return [
            pltpu.make_async_copy(
                normed_in.at[at_rows(2 * m + p), :], slots.at[2 * at + p], slot_sems.at[2 * at + p]
            )
            for p in range(2)
        ]

    for copy in load_normed(0, pairs - 1):
        copy.start()

    key_place = lax.broadcasted_iota(jnp.int32, (block, two), 0)
    query_place = lax.broadcasted_iota(jnp.int32, (block, two), 1)

    def head_cols(h, k):
        return pl.ds(pl.multiple_of(k * width + h * HEAD_DIM, HEAD_DIM), HEAD_DIM)

    def load_x(q):
        return pltpu.make_async_copy(x_in.at[at_rows(n - 1 - q), :], f_slots.at[q % 2], total_sems.at[0, q])

    def load_hid(q):
        return pltpu.make_async_copy(grad_hid.at[at_rows(n - 1 - q), :], f_slots.at[2 + q % 2], total_sems.at[1, q])

    def last_mine(q, who, k):
        return f_src[q % 2, :, at_cols(who, width)].astype(f32)

    last = HeadSum(width, lambda q: f_src.at[q % 2], last_mine, f_core, f_chip, f_sems)

    def last_copy(q):
        return pltpu.make_async_copy(
            dqkv.at[at_rows(n - 1 - q), 0:width], total_sum.at[at_rows(n - 1 - q), :], total_sems.at[2, q]
        )

    load_x(0).start()
    load_hid(0).start()
    small[...] = jnp.zeros_like(small)
    small[0:2, :] = sums_2[...]
    small[4:5, 0:grad_bias.shape[1]] = grad_bias[...]
    small[5:6, 0:width] = grad_bias_reduce[...]

    def last_chunk(q, _):
        load_x(q).wait()
        load_hid(q).wait()

        @pl.when(q + 1 < n)
        def _():
            load_x(q + 1).start()
            load_hid(q + 1).start()

        at = at_rows(n - 1 - q)
        gf = dot(dqkv[at, 0:width], wq[...], NT)
        gf += dot(dqkv[at, width : 2 * width], wk[...], NT)
        gf += dot(dqkv[at, 2 * width :], wv[...], NT)
        x = f_slots[q % 2].astype(f32)
        centre = x - jnp.sum(x, axis=1, keepdims=True) * (1.0 / features)
        spread = jnp.sum(centre * centre, axis=1, keepdims=True) * (1.0 / features)
        scale = lax.rsqrt(spread + eps)
        centred = centre * scale
        scaled = gf * gain[...]
        mean_scaled = jnp.sum(scaled, axis=1, keepdims=True) * (1.0 / features)
        mean_both = jnp.sum(scaled * centred, axis=1, keepdims=True) * (1.0 / features)
        back = (scaled - mean_scaled - centred * mean_both) * scale
        f_src[q % 2] = (back + f_slots[2 + q % 2].astype(f32)).astype(bf16)
        last.start(q)
        small[2:3, :] += jnp.sum(gf * centred, axis=0, keepdims=True)
        small[3:4, :] += jnp.sum(gf, axis=0, keepdims=True)
        @pl.when(q >= 1)
        def _():
            last.middle(q - 1)

        return 0

    def sweep(h, service):
        own_cols = pl.ds(pl.multiple_of(h * HEAD_DIM, HEAD_DIM), HEAD_DIM)
        slope = slopes[h]
        dk_acc[...] = jnp.zeros_like(dk_acc)
        dv_acc[...] = jnp.zeros_like(dv_acc)

        def tile(m, j, single):
            q_size = block if single else two
            start = 2 * m + 1 if single else 2 * m
            at = pl.ds(pl.multiple_of(start * block, block), q_size)
            q = qkv[at, head_cols(h, 0)]
            g = grad_heads[at, own_cols]
            k = qkv[at_rows(j), head_cols(h, 1)]
            v = qkv[at_rows(j), head_cols(h, 2)]
            keys, queries = key_place[:, :q_size], query_place[:, :q_size]
            if single:
                place = keys.astype(f32) * slope
                allowed = keys <= queries
                lse, dlt = logsum[start, h : h + 1, :], delta[start, h : h + 1, :]
            else:
                second = (queries >= block).astype(jnp.int32)
                offset = (j - start) * block
                place = (keys + offset - second * block).astype(f32) * slope
                allowed = keys + offset <= queries
                place += jnp.where(second + start == j, 0.0, apart)
                lse = jnp.concatenate([logsum[start, h : h + 1, :], logsum[start + 1, h : h + 1, :]], 1)
                dlt = jnp.concatenate([delta[start, h : h + 1, :], delta[start + 1, h : h + 1, :]], 1)
            s = dot(k, q, NT) * (SCALE * LOG2E) + place
            p = jnp.where(allowed, jnp.exp2(s - lse), 0.0)
            ds = (p * (dot(v, g, NT) - dlt)).astype(bf16)
            dv_acc[at_rows(j), :] += dot(p.astype(bf16), g)
            dk_acc[at_rows(j), :] += dot(ds, q)
            if single:
                dq_acc[:, block:] += dot(k, ds, TN)
            else:
                dq_acc[...] += dot(k, ds, TN)

        def outer(step, _):
            m = pairs - 1 - step
            dq_acc[...] = jnp.zeros_like(dq_acc)

            def inner(j, _):
                service(step, j)
                tile(m, j, False)
                return 0

            lax.fori_loop(0, 2 * m + 1, inner, 0)
            service(step, 2 * m + 1)
            tile(m, 2 * m + 1, True)
            for copy in load_normed(h, m):
                copy.wait()

            @pl.when(step + 1 < pairs)
            def _():
                for copy in load_normed(h, m - 1):
                    copy.start()

            if h + 1 < heads:
                @pl.when(step + 1 == pairs)
                def _():
                    for copy in load_normed(h + 1, pairs - 1):
                        copy.start()

            at = pl.ds(pl.multiple_of(m * two, two), two)
            dq = (dq_acc[...] * SCALE).T.astype(bf16)
            dk = (dk_acc[at, :] * SCALE).astype(bf16)
            dv = dv_acc[at, :].astype(bf16)
            dqkv[at, head_cols(h, 0)] = dq
            dqkv[at, head_cols(h, 1)] = dk
            dqkv[at, head_cols(h, 2)] = dv
            slot = (h * pairs + step) % 2
            low = jnp.concatenate([slots[2 * slot], slots[2 * slot + 1]], 0)
            part = dot(low, jnp.concatenate([dq, dk, dv], 1), TN)

            @pl.when(step == 0)
            def _():
                wgrad[...] = part

            @pl.when(step > 0)
            def _():
                wgrad[...] += part

            if h + 1 == heads:
                for early in range(EARLY):
                    @pl.when(step == early)
                    def _(early=early):
                        lax.fori_loop(2 * early, 2 * early + 2, last_chunk, 0)

            return 0

        lax.fori_loop(0, pairs, outer, 0)

    places, clock = [], 3.0
    for h in range(heads):
        for step in range(pairs):
            tiles = 2 * (pairs - 1 - step) + 2
            for j in range(tiles):
                places.append((clock, h, step, j))
                clock += 1.9 if j + 1 < tiles else 1.1
            clock += 1.6 + (5.4 if h + 1 == heads and step < EARLY else 0.0)
    finish_clock, finish_time = clock, 2.7
    begun = 2 * EARLY

    def events(start, end):
        return [action for time, _, action in sorted(agenda, key=lambda e: e[:2]) if start <= time < end]

    def run(actions):
        for action in actions:
            action()

    def service_of(h):
        def service(step, j):
            for k, (time, at_h, at_step, at_j) in enumerate(places):
                earlier = places[k - 1][0] if k else -1.0
                actions = events(earlier + 1e-6, time + 1e-6)
                if at_h == h and actions:
                    @pl.when((step == at_step) & (j == at_j))
                    def _(actions=actions):
                        run(actions)

        return service

    sweep(0, service_of(0))
    pay_a[...] = wgrad[...].astype(bf16)
    for which in first_sums:
        which.start()
    sweep(1, service_of(1))
    pay_b[...] = wgrad[...].astype(bf16)
    for which in second_sums:
        which.start()

    done = places[-1][0] + 1e-6

    def last_step(q, _):
        for k in range(begun, n):
            start = done if k == begun else finish_clock + (k - begun - 1) * finish_time
            actions = events(start, finish_clock + (k - begun) * finish_time)
            if actions:
                @pl.when(q == k)
                def _(actions=actions):
                    run(actions)

        return last_chunk(q, _)

    lax.fori_loop(begun, n, last_step, 0)
    last.middle(n - 1)
    done = finish_clock + (n - begun - 1) * finish_time

    def small_copy(s):
        where = {"head": partner(me, masks_of(4)[s])} if s < 2 else {"dp": partner(group, masks[s - 2])}
        return send_to(small, small_recv.at[s], small_sems.at[0, s], small_sems.at[1, s], **where)

    def small_step(s):
        small_copy(s).wait()
        if s < 2:
            small[0:4, :] += small_recv[s, 0:4, :]
        else:
            small[...] += small_recv[s]
        if s + 1 < 2 + steps:
            small_copy(s + 1).start()

    def last_finish(q):
        dqkv[at_rows(n - 1 - q), 0:width] = last.finish(q).astype(bf16)
        last_copy(q).start()

    small_copy(0).start()
    for s in range(2 + steps):
        due(max(done, TIMES["small"][min(s, 4)]) + max(s - 4, 0), small_step, s)
    for q in range(n):
        due(max(done, finish_clock + 6.1 * (q - begun + 1) + 4.0), last_finish, q)
    run(events(done, 1e9))
    proj_sum.settle()
    for which in first_sums + second_sums:
        which.settle()
    if scatter_inside:
        wide_rs.sent()
        narrow_rs.sent()
    for c in range(n_side - 2, n_side):
        side_copy(c).wait()
    for q in range(n):
        last_copy(q).wait()


def third(
    kind, qkv, grad_heads, logsum, wq, wk, wv, gain, sums_2, grad_bias, grad_bias_reduce, wide, narrow,
    a, x, normed, grad_hid, ffn, proj, local, dp_size,
):
    rows, width = grad_heads.shape
    features = x.shape[1]
    block = SHORT
    n = rows // block
    heads = width // HEAD_DIM
    masks = masks_of(dp_size)
    inside = local % 128 == 0
    home = local if inside else 128
    any_spec = pl.BlockSpec(memory_space=pl.ANY)
    vmem = pl.BlockSpec(memory_space=pltpu.VMEM)
    blocks = max(dp_size - 1, 1)
    n_side = features // block + n
    cols = 3 * HEAD_DIM
    part = features // dp_size
    halves = 2 if features % (32 * dp_size) == 0 else 1
    recv_blocks = blocks if inside else 1

    def dma(*shape):
        return pltpu.SemaphoreType.DMA(shape)

    return pl.pallas_call(
        functools.partial(third_kernel, masks, inside),
        in_specs=[pl.BlockSpec(memory_space=pltpu.SMEM), any_spec, vmem, vmem]
        + [any_spec] * 3
        + [vmem] * 4
        + [any_spec] * 8,
        out_specs=[any_spec] * 5 + [vmem] * 3,
        out_shape=[
            jax.ShapeDtypeStruct((rows, width), bf16),
            jax.ShapeDtypeStruct((rows, width), bf16),
            jax.ShapeDtypeStruct((features, width), bf16),
            jax.ShapeDtypeStruct((features, cols), bf16),
            jax.ShapeDtypeStruct((features, cols), bf16),
            jax.ShapeDtypeStruct((features, home), f32),
            jax.ShapeDtypeStruct((features, home), f32),
            jax.ShapeDtypeStruct((8, features), f32),
        ],
        scratch_shapes=[
            pltpu.VMEM((rows, 3 * width), bf16),
            pltpu.VMEM((rows, HEAD_DIM), f32),
            pltpu.VMEM((rows, HEAD_DIM), f32),
            pltpu.VMEM((HEAD_DIM, 2 * block), f32),
            pltpu.VMEM((n, heads, block), f32),
            pltpu.VMEM((features, cols), f32),
            pltpu.VMEM((4, block, features), bf16),
            pltpu.VMEM(wide.shape if inside else (16, 128), bf16),
            pltpu.VMEM(narrow.shape if inside else (16, 128), bf16),
            pltpu.VMEM((features, width), bf16),
            pltpu.VMEM((features, cols), bf16),
            pltpu.VMEM((features, cols), bf16),
            pltpu.VMEM((blocks, part, width), bf16),
            pltpu.VMEM((halves, blocks, part // halves, cols), bf16),
            pltpu.VMEM((halves, blocks, part // halves, cols), bf16),
            pltpu.VMEM((recv_blocks, features, home), bf16),
            pltpu.VMEM((recv_blocks, features, home), bf16),
            pltpu.VMEM((n_side * block, 2 * width), bf16),
            pltpu.VMEM((n_side * block, width), bf16),
            pltpu.VMEM((4, 2, block, width), bf16),
            pltpu.VMEM((2, block, width), bf16),
            pltpu.VMEM((2, block, features), bf16),
            pltpu.VMEM((rows, 2 * width), bf16),
            pltpu.VMEM((rows, width), bf16),
            pltpu.VMEM((4, block, features), bf16),
            pltpu.VMEM((2 + len(masks), 8, features), f32),
            dma(3),
            dma(6, n_side),
            dma(2, n_side),
            dma(n_side),
            dma(6, n),
            dma(4, blocks),
            dma(halves, 4, blocks),
            dma(halves, 4, blocks),
            dma(2, blocks),
            dma(2, blocks),
            dma(4),
            dma(7),
            dma(2, 2 + len(masks)),
            dma(3, n),
            pltpu.VMEM(qkv.shape, bf16),
            pltpu.VMEM(wq.shape, bf16),
            pltpu.VMEM(wk.shape, bf16),
            pltpu.VMEM(wv.shape, bf16),
            dma(4),
        ],
        compiler_params=pltpu.CompilerParams(
            vmem_limit_bytes=63 * MIB, collective_id=2, has_side_effects=True
        ),
    )(
        kind, qkv, grad_heads, logsum, wq, wk, wv, gain, sums_2, grad_bias, grad_bias_reduce, wide, narrow,
        a, x, normed, grad_hid, ffn, proj,
    )


def output_kernel(
    hid_own, ffn_sum, total, bias_reduce, sum_p, sum_a, sum_b, wide_sum, narrow_sum, small,
    layer_out, grad_in, grad_q, grad_k, grad_v, grad_proj, grad_expand, grad_reduce,
    attn_gain, attn_shift, ffn_gain, ffn_shift, grad_bias_reduce, *grad_bias,
):
    layer_out[...] = hid_own[...] + bias_reduce[...] + ffn_sum[...].astype(f32)
    grad_in[...] = total[...].astype(f32)
    for k, out in enumerate((grad_q, grad_k, grad_v)):
        cols = slice(k * HEAD_DIM, (k + 1) * HEAD_DIM)
        out[:, 0:HEAD_DIM] = sum_a[:, cols].astype(f32)
        out[:, HEAD_DIM:] = sum_b[:, cols].astype(f32)
    grad_proj[...] = sum_p[...].astype(f32).T
    grad_expand[...] = wide_sum[...]
    grad_reduce[...] = narrow_sum[...]
    for k, out in ((2, attn_gain), (3, attn_shift), (0, ffn_gain), (1, ffn_shift)):
        out[...] = small[k, :]
    grad_bias_reduce[...] = small[5, 0 : grad_bias_reduce.shape[0]]
    for out in grad_bias:
        out[...] = small[4:5, at_cols(lax.axis_index("dp"), out.shape[1])]


def outputs(hid_own, ffn_sum, total, bias_reduce, sum_p, sum_a, sum_b, wide_sum, narrow_sum, small, inside):
    rows, width = hid_own.shape
    features = sum_p.shape[0]
    block = 2 * SHORT
    part = features // 2
    home = wide_sum.shape[1]

    def by_rows(columns):
        return pl.BlockSpec((block, columns), lambda i: (i, 0))

    def by_part(columns):
        return pl.BlockSpec((part, columns), lambda i: (jnp.minimum(i, 1), 0))

    def of(*shape):
        return jax.ShapeDtypeStruct(shape, f32)

    return pl.pallas_call(
        output_kernel,
        grid=(rows // block,),
        in_specs=[
            by_rows(width), by_rows(width), by_rows(width), full_spec(bias_reduce.shape), by_part(width),
            by_part(sum_a.shape[1]), by_part(sum_b.shape[1]), by_part(home), by_part(home), full_spec(small.shape),
        ],
        out_specs=[by_rows(width)] * 2
        + [by_part(width)] * 3
        + [pl.BlockSpec((width, part), lambda i: (0, jnp.minimum(i, 1)))]
        + [by_part(home)] * 2
        + [full_spec((features,))] * 4
        + [full_spec((width,))]
        + [full_spec((1, home))] * inside,
        out_shape=[of(rows, width)] * 2
        + [of(features, width)] * 3
        + [of(width, features)]
        + [of(features, home)] * 2
        + [of(features)] * 4
        + [of(width)]
        + [of(1, home)] * inside,
        compiler_params=pltpu.CompilerParams(vmem_limit_bytes=62 * MIB),
    )(hid_own, ffn_sum, total, bias_reduce, sum_p, sum_a, sum_b, wide_sum, narrow_sum, small)


def shards(
    dp_size,
    layer_in,
    bucket,
    w_query,
    w_key,
    w_value,
    w_proj,
    attn_gain,
    attn_shift,
    ffn_gain,
    ffn_shift,
    w_expand,
    bias_expand,
    w_reduce,
    bias_reduce,
    grad_out,
):
    group = lax.axis_index("dp")
    width = layer_in.shape[1]
    local = w_expand.shape[1]
    gain_1 = attn_gain[None]
    x, a, normed, qkv, proj, expand, reduce, bias, logsum = first(
        bucket, layer_in, w_query, w_key, w_value, gain_1, attn_shift[None], bias_expand, w_proj, w_expand, w_reduce, dp_size
    )
    (
        grad_heads, grad_hid, ffn, hid_own, grad_wide, grad_narrow, proj_part, sums_2, grad_bias, grad_bias_reduce,
    ) = second(
        x, a, grad_out, layer_in, proj, expand, reduce, ffn_gain[None], ffn_shift[None], bias
    )
    ffn_sum, total, sum_p, sum_a, sum_b, wide_sum, narrow_sum, small = third(
        bucket, qkv, grad_heads, logsum, w_query, w_key, w_value, gain_1, sums_2, grad_bias, grad_bias_reduce,
        grad_wide, grad_narrow, a, x, normed, grad_hid, ffn, proj_part, local, dp_size,
    )
    if local % 128:
        wide_sum = lax.psum_scatter(grad_wide.astype(f32), "dp", scatter_dimension=1, tiled=True)
        narrow_sum = lax.psum_scatter(grad_narrow.astype(f32), "dp", scatter_dimension=1, tiled=True)
    (
        layer_out, grad_in, grad_query, grad_key, grad_value, grad_proj, grad_expand, grad_reduce,
        grad_attn_gain, grad_attn_shift, grad_ffn_gain, grad_ffn_shift, grad_bias_reduce, *grad_bias_expand,
    ) = outputs(
        hid_own, ffn_sum, total, bias_reduce[None], sum_p, sum_a, sum_b, wide_sum, narrow_sum, small, int(local % 128 == 0)
    )
    if local % 128:
        grad_bias_expand = [lax.dynamic_slice(small, (4, group * local), (1, local))]
    return (
        layer_out,
        grad_in,
        grad_query,
        grad_key,
        grad_value,
        grad_proj,
        grad_attn_gain,
        grad_attn_shift,
        grad_ffn_gain,
        grad_ffn_shift,
        grad_expand,
        grad_bias_expand[0],
        grad_reduce,
        grad_bias_reduce,
    )


def solution(mesh):
    placed = (
        P("dp", "head"),
        P("dp"),
        P(None, "head"),
        P(None, "head"),
        P(None, "head"),
        P("head", None),
        P(),
        P(),
        P(),
        P(),
        P(None, ("dp", "head")),
        P(None, ("dp", "head")),
        P(None, ("dp", "head")),
        P("head"),
        P("dp", "head"),
    )
    return jax.shard_map(
        functools.partial(shards, mesh.shape["dp"]),
        mesh=mesh,
        in_specs=placed,
        out_specs=(
            P("dp", "head"),
            P("dp", "head"),
            P(None, "head"),
            P(None, "head"),
            P(None, "head"),
            P("head", None),
            P(),
            P(),
            P(),
            P(),
            P(None, ("dp", "head")),
            P(None, ("dp", "head")),
            P(None, ("dp", "head")),
            P("head"),
        ),
        check_vma=False,
    )
```
